32 devices in a mesh: frames: 8 (over z, x), pos: 4 (over y, core).
Axes of the slice: x: 2, y: 2, z: 4, core: 2. Of those that a mesh axis runs over, the one named last changes fastest.
Arguments:
- inputs: bfloat16 [1024, 16, 1024], P('frames', None, 'pos'), may hold values from -6 to 6
- counts: int32 [1024], P('frames'), may hold values from 8 to 16, as said below
- gain_attn: float32 [1024], replicated, may hold values from 0.25 to 1.75
- weight_qkv: bfloat16 [1024, 3, 1024], P(None, None, 'pos'), may hold values from -0.1875 to 0.1875
- weight_out: bfloat16 [1024, 1024], replicated, may hold values from -0.375 to 0.375
- gain_ffn: float32 [16, 1024], P('pos'), may hold values from 0.25 to 1.75
- weight_ffn: bfloat16 [4096, 16, 3, 1024], P('frames', 'pos'), may hold values from -0.1875 to 0.1875
- cotangent: bfloat16 [1024, 16, 1024], P('frames', None, 'pos'), may hold values from -6 to 6
Outputs:
- block_out: bfloat16 [1024, 16, 1024], P('frames', None, 'pos')
- input_grad: bfloat16 [1024, 16, 1024], P('frames', None, 'pos')
- gain_attn_grad: float32 [1024], replicated
- qkv_grad: float32 [1024, 3, 1024], P('frames', None, 'pos')
- out_grad: float32 [1024, 1024], replicated
- gain_ffn_grad: float32 [16, 1024], P('pos', 'frames')
- ffn_grad: float32 [4096, 16, 3, 1024], P('frames', 'pos')
The draws below stay inside these ranges and needn't reach their ends.
Inputs may be any that keep to these rules, and one draw needn't show every extreme that they name: `counts`: each frame's count is 8 or 16; both occur in every draw.
All inputs are finite; a program needn't handle non-finite values.
Results may differ from the reference program's by a relative error of at most 0.017.
Values may be sent and summed in bfloat16 or wider, within the bound.
No kernel may reach another device: no remote copies, remote signals or barrier semaphores. Data moves between devices by JAX's collectives and lax.ppermute only.
A program may use at most 512 MiB of HBM per device.

```python
import math
import jax
import jax.numpy as jnp
from jax import lax

D = 1024
HEADS = 16
HEAD_DIM = 64
FF = 4096
DEPTH = 16
FRAMES = 1024


def draw_counts(key, part):
    key = jax.random.fold_in(key, 11)
    key_bits, key_first, key_second = jax.random.split(key, 3)
    halves = jax.random.randint(key_bits, (FRAMES,), 0, 2)
    first_full = jax.random.randint(key_first, (), 0, FRAMES)
    second_half = (first_full + 1 + jax.random.randint(key_second, (), 0, FRAMES - 1)) % FRAMES
    indices = jnp.arange(FRAMES)
    depths = DEPTH // 2 + DEPTH // 2 * halves
    depths = jnp.where(indices == first_full, DEPTH, depths)
    depths = jnp.where(indices == second_half, DEPTH // 2, depths)
    return depths.astype(jnp.int32)


def block_levels(stream_key, shape, cuts, low, top_value):
    level, own = 1.0, jax.random.fold_in(stream_key, 6)
    for dim, parts in cuts:
        draws = jnp.exp(jax.random.uniform(jax.random.fold_in(own, dim), (parts,), jnp.float32, low / len(cuts), top_value / len(cuts)))
        level = level * jnp.repeat(draws, shape[dim] // parts).reshape([-1 if axis == dim else 1 for axis in range(len(shape))])
    return level


def normal_values(rng, dims, scale, limit, cuts=(), kind=jnp.bfloat16):
    values = jax.random.normal(rng, dims, jnp.float32) * scale
    if len(cuts) > 0:
        values = block_levels(rng, dims, cuts, -0.22, 0.18) * values
    return jnp.clip(values, min=-limit, max=limit).astype(kind)


def setup_inputs(seed: int = 0) -> dict:
    splits = jax.random.split(jax.random.key(seed), 9)
    return {
        "inputs": normal_values(splits[0], (FRAMES, DEPTH, D), 1.0, 6.0, ((0, 8), (2, 4))),
        "counts": draw_counts(jax.random.fold_in(splits[8], 71), 0),
        "gain_attn": jnp.clip(1.0 + 0.15 * jax.random.normal(splits[2], (D,), jnp.float32), 0.25, 1.75),
        "weight_qkv": normal_values(splits[3], (D, 3, D), D ** -0.5, 0.1875, ((2, 4),)),
        "weight_out": normal_values(splits[4], (D, D), (D // 4) ** -0.5, 0.375),
        "gain_ffn": jnp.clip(1.0 + 0.15 * jax.random.normal(splits[5], (DEPTH, D), jnp.float32), 0.25, 1.75),
        "weight_ffn": normal_values(splits[6], (FF, DEPTH, 3, D), D ** -0.5, 0.1875, ((0, 8), (1, 4))),
        "cotangent": normal_values(splits[7], (FRAMES, DEPTH, D), 1.0, 6.0, ((0, 8), (2, 4))),
    }


epsilon = 1e-05
masked_score = -1e+30

@jax.custom_vjp
def low(v):
    return lax.optimization_barrier(v.astype(jnp.bfloat16)).astype(jnp.float32)

@jax.custom_vjp
def low_back(v):
    return v

def low_keep(v):
    return (low(v), None)

def low_pass(kept, grad):
    return (grad,)

def back_keep(v):
    return (v, None)

def back_low(kept, grad):
    return (low(grad),)
low.defvjp(low_keep, low_pass)
low_back.defvjp(back_keep, back_low)

def highest(form, left, right):
    return jnp.einsum(form, left, right, precision=lax.Precision.HIGHEST)

def layer(inputs, depths, gain_attn, weight_qkv, weight_out, gain_ffn, weight_ffn):
    frames_now = inputs.shape[0]
    positions = jnp.arange(DEPTH, dtype=jnp.int32)
    live_mask = (positions[None, :] < depths[:, None]).astype(jnp.float32)
    scale_attn = lax.rsqrt(lax.optimization_barrier(jnp.mean(inputs * inputs, axis=-1, keepdims=True)) + epsilon)
    normed = low(inputs * scale_attn * gain_attn)
    project = low(low_back(highest('fkd,dje->fkje', normed, weight_qkv)))
    shaped = project.reshape(frames_now, DEPTH, 3, HEADS, HEAD_DIM)
    query_heads = shaped[:, :, 0]
    key_heads = shaped[:, :, 1]
    value_heads = shaped[:, :, 2]
    scores = low_back(highest('fihe,fjhe->fhij', query_heads, key_heads) * HEAD_DIM ** (-0.5))
    allowed = (positions[None, None, :] <= positions[None, :, None]) & (positions[None, None, :] < depths[:, None, None])
    scores = jnp.where(allowed[:, None], scores, masked_score)
    attn_probs = low(jax.nn.softmax(scores, axis=-1))
    head_mixed = highest('fhij,fjhe->fihe', attn_probs, value_heads).reshape(frames_now, DEPTH, D)
    head_mixed = low(low_back(head_mixed))
    attended = highest('fkd,de->fke', head_mixed, weight_out)
    hidden = low_back(inputs + attended)
    scale_ffn = lax.rsqrt(lax.optimization_barrier(jnp.mean(hidden * hidden, axis=-1, keepdims=True)) + epsilon)
    hidden_norm = low(hidden * scale_ffn * gain_ffn[None])
    gate_up = low_back(highest('fkd,nkjd->fkjn', hidden_norm, weight_ffn[:, :, :2]))
    activated = low(jax.nn.silu(gate_up[:, :, 0]) * gate_up[:, :, 1])
    branch = highest('fkn,nkd->fkd', activated, weight_ffn[:, :, 2])
    return live_mask[:, :, None] * (hidden + branch)

def reference(inputs, counts, gain_attn, weight_qkv, weight_out, gain_ffn, weight_ffn, cotangent):
    block_size = math.gcd(FRAMES, 256)
    steps_count = FRAMES // block_size
    params = (gain_attn.astype(jnp.float32), weight_qkv.astype(jnp.float32), weight_out.astype(jnp.float32), gain_ffn.astype(jnp.float32), weight_ffn.astype(jnp.float32))
    input_blocks = inputs.astype(jnp.float32).reshape(steps_count, block_size, DEPTH, D)
    count_blocks = counts.reshape(steps_count, block_size)
    cot_blocks = cotangent.astype(jnp.float32).reshape(steps_count, block_size, DEPTH, D)

    def one_block(totals, pieces):
        part_in, part_count, part_cot = pieces

        def closed(values, gain_first, qkv_in, out_in, gain_second, ffn_in):
            return layer(values, part_count, gain_first, qkv_in, out_in, gain_second, ffn_in)
        result, pullback = jax.vjp(closed, part_in, *params)
        gradients = pullback(part_cot)
        totals = tuple((running + update for running, update in zip(totals, gradients[1:])))
        return (totals, (result.astype(jnp.bfloat16), gradients[0].astype(jnp.bfloat16)))
    zeros_start = tuple((jnp.zeros_like(entry) for entry in params))
    totals, (outputs, input_grads) = lax.scan(one_block, zeros_start, (input_blocks, count_blocks, cot_blocks))
    return (outputs.reshape(FRAMES, DEPTH, D), input_grads.reshape(FRAMES, DEPTH, D), totals[0], totals[1], totals[2], totals[3], totals[4])
```

```python
import jax
import jax.numpy as jnp
from jax import lax
from jax.sharding import PartitionSpec as P

HEAD_DIM = 64


epsilon = 1e-05
masked_score = -1e30


def body(inputs, counts, gain_attn, weight_qkv, weight_out, gain_ffn, weight_ffn, cotangent):
    pos_count = lax.axis_size("pos")
    pos_index = lax.axis_index("pos")
    frame_rows, depth_all, feature_part = inputs.shape
    feature_all = feature_part * pos_count
    per_device = depth_all // pos_count
    local_cols = weight_qkv.shape[2]
    local_heads = local_cols // HEAD_DIM
    positions = jnp.arange(depth_all, dtype=jnp.int32)
    live_mask = (positions[None, :] < counts[:, None]).astype(jnp.float32)
    gathered = lax.all_gather(inputs, "pos", axis=2, tiled=True)
    inputs_full = gathered.astype(jnp.float32)
    scale_attn = lax.rsqrt(jnp.mean(inputs_full * inputs_full, axis=-1, keepdims=True) + epsilon)
    normal_attn = inputs_full * scale_attn
    normed = (normal_attn * gain_attn).astype(jnp.bfloat16)
    project = jnp.einsum(
        "fkd,dje->fkje", normed, weight_qkv, preferred_element_type=jnp.float32
    ).astype(jnp.bfloat16)
    shaped = project.reshape(frame_rows, depth_all, 3, local_heads, HEAD_DIM)
    query_heads = shaped[:, :, 0]
    key_heads = shaped[:, :, 1]
    value_heads = shaped[:, :, 2]
    factor = HEAD_DIM ** (-0.5)
    scores = (
        jnp.einsum("fihe,fjhe->fhij", query_heads, key_heads, preferred_element_type=jnp.float32)
        * factor
    )
    allowed = (
        (positions[None, None, :] <= positions[None, :, None])
        & (positions[None, None, :] < counts[:, None, None])
    )[:, None]
    scores = jnp.where(allowed, scores, masked_score)
    top_score = jnp.max(scores, axis=-1, keepdims=True)
    exp_score = jnp.exp(scores - top_score)
    attn_probs = exp_score / jnp.sum(exp_score, axis=-1, keepdims=True)
    probs_low = attn_probs.astype(jnp.bfloat16)
    head_mixed = jnp.einsum(
        "fhij,fjhe->fihe", probs_low, value_heads, preferred_element_type=jnp.float32
    )
    head_mixed = head_mixed.astype(jnp.bfloat16).reshape(frame_rows, depth_all, local_cols)
    arrived = lax.all_to_all(head_mixed, "pos", split_axis=1, concat_axis=2, tiled=True)
    first_row = pos_index * per_device
    resid_rows = lax.dynamic_slice_in_dim(inputs_full, first_row, per_device, 1)
    live_rows = lax.dynamic_slice_in_dim(live_mask, first_row, per_device, 1)[:, :, None]
    attended = jnp.einsum("fkd,de->fke", arrived, weight_out, preferred_element_type=jnp.float32)
    hidden = resid_rows + attended
    scale_ffn = lax.rsqrt(jnp.mean(hidden * hidden, axis=-1, keepdims=True) + epsilon)
    normal_ffn = hidden * scale_ffn
    hidden_norm = (normal_ffn * gain_ffn[None]).astype(jnp.bfloat16)
    cot_rows = lax.all_to_all(cotangent, "pos", split_axis=1, concat_axis=2, tiled=True)
    branch_grad = cot_rows * live_rows.astype(jnp.bfloat16)
    grad_all = lax.all_gather(branch_grad, "frames", axis=0, tiled=True)
    norm_all = lax.all_gather(hidden_norm, "frames", axis=0, tiled=True)
    gate_up = jnp.einsum(
        "fkd,nkjd->fkjn", norm_all, weight_ffn[:, :, :2], preferred_element_type=jnp.float32
    )
    gate_val = gate_up[:, :, 0]
    up_val = gate_up[:, :, 1]
    sigmoid_val = jax.nn.sigmoid(gate_val)
    activated = (gate_val * sigmoid_val * up_val).astype(jnp.bfloat16)
    act_grad = jnp.einsum(
        "fkd,nkd->fkn", grad_all, weight_ffn[:, :, 2], preferred_element_type=jnp.float32
    )
    gate_grad = act_grad * up_val * sigmoid_val * (1.0 + gate_val * (1.0 - sigmoid_val))
    up_grad = act_grad * gate_val * sigmoid_val
    pair_grad = jnp.stack([gate_grad, up_grad], 2).astype(jnp.bfloat16)
    norm_sum = jnp.einsum(
        "fkjn,nkjd->fkd", pair_grad, weight_ffn[:, :, :2], preferred_element_type=jnp.float32
    ).astype(jnp.bfloat16)
    norm_part = lax.psum_scatter(norm_sum, "frames", scatter_dimension=0, tiled=True).astype(
        jnp.float32
    )
    branch_sum = jnp.einsum(
        "fkn,nkd->fkd", activated, weight_ffn[:, :, 2], preferred_element_type=jnp.float32
    ).astype(jnp.bfloat16)
    branch_out = lax.psum_scatter(branch_sum, "frames", scatter_dimension=0, tiled=True).astype(
        jnp.float32
    )
    block_rows = (live_rows * (hidden + branch_out)).astype(jnp.bfloat16)
    block_out = lax.all_to_all(block_rows, "pos", split_axis=2, concat_axis=1, tiled=True)
    gate_term = jnp.einsum(
        "fkjn,fkd->nkjd", pair_grad, norm_all, preferred_element_type=jnp.float32
    )
    down_term = jnp.einsum(
        "fkn,fkd->nkd", activated, grad_all, preferred_element_type=jnp.float32
    )
    ffn_grad = jnp.concatenate([gate_term, down_term[:, :, None]], 2)
    scaled_grad = gain_ffn[None] * norm_part
    row_mean = jnp.mean(normal_ffn * scaled_grad, axis=-1, keepdims=True)
    hidden_grad = live_rows * cot_rows.astype(jnp.float32) + scale_ffn * (
        scaled_grad - normal_ffn * row_mean
    )
    hidden_low = hidden_grad.astype(jnp.bfloat16)
    gain_ffn_part = jnp.sum(norm_part * normal_ffn, axis=0)
    out_weight_part = jnp.einsum(
        "fkd,fke->de", arrived, hidden_low, preferred_element_type=jnp.float32
    )
    mixed_grad = jnp.einsum(
        "fke,de->fkd", hidden_low, weight_out, preferred_element_type=jnp.float32
    ).astype(jnp.bfloat16)
    resid_back, mixed_back = (
        lax.all_to_all(hidden_low, "pos", split_axis=2, concat_axis=1, tiled=True),
        lax.all_to_all(mixed_grad, "pos", split_axis=2, concat_axis=1, tiled=True),
    )
    mixed_heads = mixed_back.reshape(frame_rows, depth_all, local_heads, HEAD_DIM)
    probs_grad = jnp.einsum(
        "fihe,fjhe->fhij", mixed_heads, value_heads, preferred_element_type=jnp.float32
    )
    value_grad = jnp.einsum(
        "fhij,fihe->fjhe", probs_low, mixed_heads, preferred_element_type=jnp.float32
    )
    score_grad = attn_probs * (
        probs_grad - jnp.sum(attn_probs * probs_grad, axis=-1, keepdims=True)
    )
    score_low = score_grad.astype(jnp.bfloat16)
    query_grad = (
        jnp.einsum("fhij,fjhe->fihe", score_low, key_heads, preferred_element_type=jnp.float32)
        * factor
    )
    key_grad = (
        jnp.einsum("fhij,fihe->fjhe", score_low, query_heads, preferred_element_type=jnp.float32)
        * factor
    )
    project_grad = jnp.stack([query_grad, key_grad, value_grad], 2)
    project_grad = project_grad.reshape(frame_rows, depth_all, 3, local_cols).astype(jnp.bfloat16)
    qkv_part = jnp.einsum("fkd,fkje->dje", normed, project_grad, preferred_element_type=jnp.float32)
    normed_grad = jnp.einsum(
        "fkje,dje->fkd", project_grad, weight_qkv, preferred_element_type=jnp.float32
    )
    gain_attn_part = jnp.sum(normed_grad * normal_attn, axis=(0, 1))
    scaled_attn = normed_grad * gain_attn
    row_partial = jnp.sum(normal_attn * scaled_attn, axis=-1)
    scaled_local = lax.psum_scatter(
        scaled_attn.astype(jnp.bfloat16), "pos", scatter_dimension=2, tiled=True
    ).astype(jnp.float32)
    row_total = lax.psum(row_partial, "pos")
    normal_local = lax.dynamic_slice_in_dim(normal_attn, pos_index * feature_part, feature_part, 2)
    input_grad = resid_back.astype(jnp.float32) + scale_attn * (
        scaled_local - normal_local * (row_total[:, :, None] / feature_all)
    )
    input_grad = input_grad.astype(jnp.bfloat16)
    shared = (
        lax.psum_scatter(
            qkv_part.astype(jnp.bfloat16), "frames", scatter_dimension=0, tiled=True
        ).astype(jnp.float32),
        lax.psum_scatter(
            gain_ffn_part.astype(jnp.bfloat16), "frames", scatter_dimension=1, tiled=True
        ).astype(jnp.float32),
    )
    out_low = lax.psum_scatter(
        out_weight_part.astype(jnp.bfloat16), ("frames", "pos"), scatter_dimension=0, tiled=True
    )
    out_grad = lax.all_gather(out_low, ("frames", "pos"), axis=0, tiled=True).astype(jnp.float32)
    gain_attn_grad = lax.psum(gain_attn_part, ("frames", "pos"))
    return (block_out, input_grad, gain_attn_grad, shared[0], out_grad, shared[1], ffn_grad)


def solution(mesh):
    placed = (
        P("frames", None, "pos"),
        P("frames"),
        P(),
        P(None, None, "pos"),
        P(),
        P("pos", None),
        P("frames", "pos", None, None),
        P("frames", None, "pos"),
    )
    return jax.shard_map(
        body,
        mesh=mesh,
        in_specs=placed,
        out_specs=(
            P("frames", None, "pos"),
            P("frames", None, "pos"),
            P(),
            P("frames", None, "pos"),
            P(),
            P("pos", "frames"),
            P("frames", "pos", None, None),
        ),
        check_vma=False,
    )
```

```python
import functools

import jax
import jax.numpy as jnp
from jax import lax
from jax.experimental import pallas as pl
from jax.experimental.pallas import tpu as pltpu
from jax.sharding import PartitionSpec as P

HEAD_DIM = 64
EPS = 1e-05
MASKED = -1e30
GROUP = 16
STEP = 32
EXTRA = 16
COST = 0.5
VMEM_LIMIT = 56 * 1024 * 1024

f32 = jnp.float32
bf16 = jnp.bfloat16


def dot(a, b, ca, cb):
    return lax.dot_general(a, b, (((ca,), (cb,)), ((), ())), preferred_element_type=f32)


def cost(us):
    us = us * COST
    return pl.CostEstimate(flops=int(us * 1.15e9), bytes_accessed=int(us * 1e6), transcendentals=0)


def params():
    return pltpu.CompilerParams(vmem_limit_bytes=VMEM_LIMIT)


def to_owners(me, rows, depth, local):
    r = lax.broadcasted_iota(jnp.int32, (rows, rows), 0)
    c = lax.broadcasted_iota(jnp.int32, (rows, rows), 1)
    frames = rows // depth
    k = r // frames
    source = (r % frames) * depth + ((k // local) ^ me) * local + k % local
    return jnp.where(c == source, 1.0, 0.0).astype(bf16)


def from_owners(me, rows, depth, local):
    r = lax.broadcasted_iota(jnp.int32, (rows, rows), 0)
    c = lax.broadcasted_iota(jnp.int32, (rows, rows), 1)
    frames = rows // depth
    k = r % depth
    source = (((k // local) ^ me) * local + k % local) * frames + r // depth
    return jnp.where(c == source, 1.0, 0.0).astype(bf16)


def pick(blocks, index):
    out = blocks[0]
    for b in range(1, len(blocks)):
        out = jnp.where(index == b, blocks[b], out)
    return out


def row_to_column(row):
    n = row.shape[1]
    r = lax.broadcasted_iota(jnp.int32, (n, n), 0)
    c = lax.broadcasted_iota(jnp.int32, (n, n), 1)
    return jnp.sum(jnp.where(r == c, row, 0.0), axis=1, keepdims=True)


def column_to_row(column):
    n = column.shape[0]
    r = lax.broadcasted_iota(jnp.int32, (n, n), 0)
    c = lax.broadcasted_iota(jnp.int32, (n, n), 1)
    return jnp.sum(jnp.where(r == c, column, 0.0), axis=0, keepdims=True)


def pair_mask(live_row, half, depth):
    n = live_row.shape[1] // 2
    live = row_to_column(live_row[:, half * n : (half + 1) * n])
    r = lax.broadcasted_iota(jnp.int32, (n, n), 0)
    c = lax.broadcasted_iota(jnp.int32, (n, n), 1)
    allowed = ((r // depth) == (c // depth)) & (r <= c) & (live > 0.5)
    return jnp.concatenate([allowed, allowed], 1)


def split_heads(block):
    lane = lax.broadcasted_iota(jnp.int32, block.shape, 1)
    zero = jnp.zeros_like(block)
    return jnp.concatenate(
        [jnp.where(lane < HEAD_DIM, block, zero), jnp.where(lane >= HEAD_DIM, block, zero)], 0
    )


def join_heads(pair):
    n = pair.shape[0] // 2
    lane = lax.broadcasted_iota(jnp.int32, (n, pair.shape[1]), 1)
    return jnp.where(lane < HEAD_DIM, pair[:n], pair[n:])


def pair_probs(q2, k2, allowed):
    scores = jnp.where(allowed, dot(k2, q2, 1, 1), MASKED)
    e = jnp.exp(scores - jnp.max(scores, axis=0, keepdims=True))
    return e * (1.0 / jnp.sum(e, axis=0, keepdims=True))


def per_step(frames, step):
    return min(step, frames)


def place(back, pieces, f):
    local, _, part = pieces[0].shape
    blocks = [p[:, f].reshape(local * GROUP, part) for p in pieces]
    return dot(back, jnp.concatenate(blocks, 0), 1, 0)


def row_scale(pieces):
    total = None
    for x in pieces:
        xf = x.astype(f32)
        term = jnp.sum(xf * xf, axis=-1, keepdims=True)
        total = term if total is None else total + term
    return lax.rsqrt(total / (pieces[0].shape[1] * len(pieces)) + EPS)


def cot_kernel(count, idx_ref, cot_ref, live_ref, *outs):
    step, depth, part = cot_ref.shape
    rows = GROUP * depth
    local = depth // count
    move = to_owners(idx_ref[0], rows, depth, local)
    for g in range(step // GROUP):
        f = slice(g * GROUP, (g + 1) * GROUP)
        live = row_to_column(live_ref[g])
        masked = (cot_ref[f].reshape(rows, part).astype(f32) * live).astype(bf16)
        moved = dot(move, masked, 1, 0).astype(bf16).reshape(count, local, GROUP, part)
        for j in range(count):
            outs[j][:, f] = moved[j]


def split_cot(idx, cot, live, count):
    frames, depth, part = cot.shape
    local = depth // count
    step = per_step(frames, 64)
    return pl.pallas_call(
        functools.partial(cot_kernel, count),
        grid_spec=pltpu.PrefetchScalarGridSpec(
            num_scalar_prefetch=1,
            grid=(frames // step,),
            in_specs=[
                pl.BlockSpec((step, depth, part), lambda i, s: (i, 0, 0)),
                pl.BlockSpec((step // GROUP, 1, GROUP * depth), lambda i, s: (i, 0, 0)),
            ],
            out_specs=[pl.BlockSpec((local, step, part), lambda i, s: (0, i, 0))] * count,
        ),
        out_shape=[jax.ShapeDtypeStruct((local, frames, part), bf16)] * count,
        compiler_params=params(),
        cost_estimate=cost(4),
    )(idx, cot, live)


def attn_kernel(count, idx_ref, *refs):
    xs = refs[:count]
    w_ref, gain_ref, live_ref = refs[count : count + 3]
    qkv_ref, resid_ref = refs[count + 3 : count + 5]
    outs = refs[count + 5 :]
    me = idx_ref[0]
    step, depth, part = xs[0].shape
    rows = GROUP * depth
    local = depth // count
    half_rows = rows // 2
    move = to_owners(me, rows, depth, local)
    own = move[: local * GROUP]
    for g in range(step // GROUP):
        f = slice(g * GROUP, (g + 1) * GROUP)
        r = slice(g * rows, (g + 1) * rows)
        pieces = [x[f].reshape(rows, part) for x in xs]
        rms = row_scale(pieces)
        acc = [None] * 3
        for j in range(count):
            normed = (pieces[j].astype(f32) * rms * gain_ref[me ^ j]).astype(bf16)
            for c in range(3):
                term = dot(normed, w_ref[c, me ^ j], 1, 0)
                acc[c] = term if acc[c] is None else acc[c] + term
            moved = dot(own, pieces[j], 1, 0).astype(bf16)
            resid_ref[me ^ j, :, f] = moved.reshape(local, GROUP, part)
        q, k, v = [a.astype(bf16) for a in acc]
        qkv_ref[0, r], qkv_ref[1, r], qkv_ref[2, r] = q, k, v
        q = q * (HEAD_DIM**-0.5)
        mixed = []
        for half in range(2):
            allowed = pair_mask(live_ref[g], half, depth)
            sl = slice(half * half_rows, (half + 1) * half_rows)
            cols = []
            for pair in range(part // 128):
                ln = slice(pair * 128, (pair + 1) * 128)
                probs = pair_probs(split_heads(q[sl, ln]), k[sl, ln], allowed).astype(bf16)
                cols.append(join_heads(dot(probs, v[sl, ln], 0, 0)).astype(bf16))
            mixed.append(jnp.concatenate(cols, 1) if len(cols) > 1 else cols[0])
        mixed = jnp.concatenate(mixed, 0)
        moved = dot(move, mixed, 1, 0).astype(bf16).reshape(count, local, GROUP, part)
        for j in range(count):
            outs[j][:, f] = moved[j]


def attention(idx, xs, w, gain, live, chunk, chunks):
    count = len(xs)
    frames, depth, part = xs[0].shape
    local = depth // count
    frames = frames // chunks
    step = per_step(frames, STEP)
    n = frames // step
    base = chunk * n
    rows = step * depth
    return pl.pallas_call(
        functools.partial(attn_kernel, count),
        grid_spec=pltpu.PrefetchScalarGridSpec(
            num_scalar_prefetch=1,
            grid=(n,),
            in_specs=[pl.BlockSpec((step, depth, part), lambda i, s: (i + base, 0, 0))] * count
            + [
                pl.BlockSpec(w.shape, lambda i, s: (0, 0, 0, 0)),
                pl.BlockSpec(gain.shape, lambda i, s: (0, 0, 0)),
                pl.BlockSpec((step // GROUP, 1, GROUP * depth), lambda i, s: (i + base, 0, 0)),
            ],
            out_specs=[
                pl.BlockSpec((3, rows, part), lambda i, s: (0, i, 0)),
                pl.BlockSpec((count, local, step, part), lambda i, s: (0, 0, i, 0)),
            ]
            + [pl.BlockSpec((local, step, part), lambda i, s: (0, i, 0))] * count,
        ),
        out_shape=[
            jax.ShapeDtypeStruct((3, frames * depth, part), bf16),
            jax.ShapeDtypeStruct((count, local, frames, part), bf16),
        ]
        + [jax.ShapeDtypeStruct((local, frames, part), bf16)] * count,
        compiler_params=params(),
        cost_estimate=cost(8),
    )(idx, *xs, w, gain, live)


def half_specs(local, frames, width):
    half = local // 2
    return [
        pl.BlockSpec((1, frames, width), lambda k, *s: (jnp.minimum(k, half - 1), 0, 0)),
        pl.BlockSpec((1, frames, width), lambda k, *s: (jnp.maximum(k - half, 0), 0, 0)),
    ]


def store_half(is_first, first_ref, second_ref, at, value):
    @pl.when(is_first)
    def _():
        first_ref[at] = value

    @pl.when(jnp.logical_not(is_first))
    def _():
        second_ref[at] = value


def load_half(is_first, first_ref, second_ref):
    return jnp.where(is_first, first_ref[0], second_ref[0])


def project_kernel(count, chunks, idx_ref, *refs):
    mixed = refs[: count * chunks]
    resids = refs[count * chunks : (count + 1) * chunks]
    w_ref, gain_ref, hidden_ref, first_ref, second_ref = refs[(count + 1) * chunks :]
    me = idx_ref[0]
    is_first = pl.program_id(0) < pl.num_programs(0) // 2
    size = mixed[0].shape[1]
    for c in range(chunks):
        f = slice(c * size, (c + 1) * size)
        hidden = jnp.concatenate([resids[c][b, 0] for b in range(count)], 1).astype(f32)
        for j in range(count):
            hidden = hidden + dot(mixed[c * count + j][0], w_ref[me ^ j], 1, 0)
        hidden_ref[0, f] = hidden
        rms = lax.rsqrt(jnp.mean(hidden * hidden, axis=-1, keepdims=True) + EPS)
        norm = (hidden * rms * gain_ref[0]).astype(bf16)
        store_half(is_first, first_ref, second_ref, (0, f), norm)


def project(idx, mixed, resids, w, gain):
    chunks, count = len(mixed), len(mixed[0])
    local, size, part = mixed[0][0].shape
    frames, width = size * chunks, part * count
    each = pl.BlockSpec((1, frames, width), lambda k, s: (k, 0, 0))
    return pl.pallas_call(
        functools.partial(project_kernel, count, chunks),
        grid_spec=pltpu.PrefetchScalarGridSpec(
            num_scalar_prefetch=1,
            grid=(local,),
            in_specs=[pl.BlockSpec((1, size, part), lambda k, s: (k, 0, 0))] * (count * chunks)
            + [pl.BlockSpec((count, 1, size, part), lambda k, s: (0, k, 0, 0))] * chunks
            + [
                pl.BlockSpec(w.shape, lambda k, s: (0, 0, 0)),
                pl.BlockSpec((1, 1, width), lambda k, s: (k, 0, 0)),
            ],
            out_specs=[each, *half_specs(local, frames, width)],
        ),
        out_shape=[
            jax.ShapeDtypeStruct((local, frames, width), f32),
            *[jax.ShapeDtypeStruct((local // 2, frames, width), bf16)] * 2,
        ],
        compiler_params=params(),
        cost_estimate=cost(6),
    )(idx, *[m for part_ in mixed for m in part_], *resids, w, gain)


def ffn_kernel(n, *refs):
    norms, grads, w_ref = refs[: 2 * n], refs[2 * n : 4 * n], refs[4 * n]
    dnorms, branches = refs[4 * n + 1 : 6 * n + 1], refs[6 * n + 1 : 8 * n + 1]
    act_ref = refs[-1]
    frames = norms[0].shape[1]
    is_first = pl.program_id(0) < pl.num_programs(0) // 2
    norm = jnp.concatenate([load_half(is_first, *norms[2 * i : 2 * i + 2]) for i in range(n)], 0)
    grad = jnp.concatenate([load_half(is_first, *grads[2 * i : 2 * i + 2]) for i in range(n)], 0)
    gate = dot(norm, w_ref[0, 0], 1, 1)
    up = dot(norm, w_ref[0, 1], 1, 1)
    dact = dot(grad, w_ref[0, 2], 1, 1)
    sig = jax.nn.sigmoid(gate)
    silu = gate * sig
    act = (silu * up).astype(bf16)
    dgate = (dact * up * sig * (1.0 + gate * (1.0 - sig))).astype(bf16)
    dup = (dact * silu).astype(bf16)
    act_ref[0, 0] = dgate
    act_ref[0, 1] = dup
    act_ref[0, 2] = act
    dnorm = (dot(dgate, w_ref[0, 0], 1, 0) + dot(dup, w_ref[0, 1], 1, 0)).astype(bf16)
    branch = dot(act, w_ref[0, 2], 1, 0).astype(bf16)
    for i in range(n):
        rows = slice(i * frames, (i + 1) * frames)
        store_half(is_first, *dnorms[2 * i : 2 * i + 2], 0, dnorm[rows])
        store_half(is_first, *branches[2 * i : 2 * i + 2], 0, branch[rows])


def ffn(norms, grads, w):
    n = len(norms)
    half, frames, width = norms[0][0].shape
    local, _, hidden, _ = w.shape
    specs = half_specs(local, frames, width)
    *out, act = pl.pallas_call(
        functools.partial(ffn_kernel, n),
        grid=(local,),
        in_specs=specs * (2 * n)
        + [pl.BlockSpec((1, 3, hidden, width), lambda k: (k, 0, 0, 0))],
        out_specs=specs * (2 * n)
        + [pl.BlockSpec((1, 3, n * frames, hidden), lambda k: (k, 0, 0, 0))],
        out_shape=[jax.ShapeDtypeStruct((half, frames, width), bf16)] * (4 * n)
        + [jax.ShapeDtypeStruct((local, 3, n * frames, hidden), bf16)],
        compiler_params=params(),
        cost_estimate=cost(3.5 + 5 * n),
    )(*[h for v in norms for h in v], *[h for v in grads for h in v], w)
    pairs = [out[i : i + 2] for i in range(0, 4 * n, 2)]
    return pairs[:n], pairs[n:], act


def weight_kernel(n, row, *refs):
    acts, others, out_ref = refs[:n], refs[n : -1], refs[-1]
    half, frames, _ = others[0].shape
    for k in range(acts[0].shape[0]):
        total, first = None, 0
        for a in acts:
            size = a.shape[2] // frames
            both = [others[2 * (first + i) + k // half][k % half] for i in range(size)]
            first += size
            both = jnp.concatenate(both, 0) if size > 1 else both[0]
            term = dot(a[k, 0], both, 0, 0)
            total = term if total is None else total + term
        out_ref[:, 0, k] = total


def weight_grad(acts, others, row, out):
    n = len(acts)
    half, frames, width = others[0][0].shape
    local, _, _, hidden = acts[0].shape
    chunk = min(128, hidden)
    whole = pl.BlockSpec(
        (half, frames, width), lambda c: (0, 0, 0), pipeline_mode=pl.Buffered(1)
    )
    others = [h for v in others for h in v]
    ins = list(acts) + others
    specs = [
        pl.BlockSpec((local, 1, a.shape[2], chunk), lambda c: (0, row, 0, c)) for a in acts
    ] + [whole] * len(others)
    aliases = {}
    kernel = functools.partial(weight_kernel, n, row)
    if out is not None:
        aliases = {len(ins): 0}
        ins.append(out)
        specs.append(pl.BlockSpec(memory_space=pl.ANY))
        kernel = lambda *refs: weight_kernel(n, row, *refs[:-2], refs[-1])
    return pl.pallas_call(
        kernel,
        grid=(hidden // chunk,),
        in_specs=specs,
        out_specs=pl.BlockSpec((chunk, 1, local, width), lambda c: (c, row, 0, 0)),
        out_shape=jax.ShapeDtypeStruct((hidden, 3, local, width), f32),
        input_output_aliases=aliases,
        compiler_params=params(),
        cost_estimate=cost(12),
    )(*ins)


def add_low(x, y):
    return (x.astype(f32) + y.astype(f32)).astype(bf16)


def merge(x, y, up, down):
    return add_low(x, up), add_low(y, down)


def sum_halves(refs):
    is_first = pl.program_id(0) < pl.num_programs(0) // 2
    total = None
    for i in range(0, len(refs), 2):
        term = load_half(is_first, *refs[i : i + 2]).astype(f32)
        total = term if total is None else total + term
    return total


def resid_kernel(count, idx_ref, *refs):
    hidden_ref, branch_ref, gain_ref, w_ref, low_ref, gsum_ref = refs[6:12]
    dms, dhs = refs[12 : 12 + count], refs[12 + count :]
    me = idx_ref[0]
    part = w_ref.shape[1]
    dnorm = sum_halves(refs[:6])
    hidden = hidden_ref[0]
    rms = lax.rsqrt(jnp.mean(hidden * hidden, axis=-1, keepdims=True) + EPS)
    xhat = hidden * rms
    gsum_ref[0] = jnp.sum(dnorm * xhat, axis=0, keepdims=True)
    u = dnorm * gain_ref[0]
    inner = jnp.mean(xhat * u, axis=-1, keepdims=True)
    low = (branch_ref[0].astype(f32) + rms * (u - xhat * inner)).astype(bf16)
    low_ref[0] = low
    blocks = [low[:, b * part : (b + 1) * part] for b in range(count)]
    for j in range(count):
        dhs[j][0] = pick(blocks, me ^ j)
        dms[j][0] = dot(low, w_ref[me ^ j], 1, 1).astype(bf16)


def resid_grad(idx, recv, own, hidden, branch, gain, w):
    count, part, width = w.shape
    local, frames, _ = hidden.shape
    each = pl.BlockSpec((1, frames, width), lambda k, s: (k, 0, 0))
    return pl.pallas_call(
        functools.partial(resid_kernel, count),
        grid_spec=pltpu.PrefetchScalarGridSpec(
            num_scalar_prefetch=1,
            grid=(local,),
            in_specs=half_specs(local, frames, width) * 3
            + [each] * 2
            + [
                pl.BlockSpec((1, 1, width), lambda k, s: (k, 0, 0)),
                pl.BlockSpec(w.shape, lambda k, s: (0, 0, 0)),
            ],
            out_specs=[each, pl.BlockSpec((1, 1, width), lambda k, s: (k, 0, 0))]
            + [pl.BlockSpec((1, frames, part), lambda k, s: (k, 0, 0))] * (2 * count),
        ),
        out_shape=[
            jax.ShapeDtypeStruct((local, frames, width), bf16),
            jax.ShapeDtypeStruct((local, 1, width), f32),
        ]
        + [jax.ShapeDtypeStruct((local, frames, part), bf16)] * (2 * count),
        compiler_params=params(),
        cost_estimate=cost(8),
    )(idx, *recv, *own, hidden, branch, gain, w)


def attn_back_kernel(count, idx_ref, *refs):
    xs = refs[:count]
    dms = refs[count : 2 * count]
    qkv_ref, w_ref, gain_ref, live_ref = refs[2 * count : 2 * count + 4]
    keep_ref, send_ref, wsum_ref, gsum_ref = refs[2 * count + 4 :]
    me = idx_ref[0]
    step, depth, part = xs[0].shape
    rows = GROUP * depth
    back = from_owners(me, rows, depth, depth // count)
    half_rows = rows // 2
    factor = HEAD_DIM**-0.5

    @pl.when(pl.program_id(0) == 0)
    def _():
        wsum_ref[...] = jnp.zeros_like(wsum_ref)
        gsum_ref[...] = jnp.zeros_like(gsum_ref)

    every, rmss = [[], [], []], []
    for g in range(step // GROUP):
        f = slice(g * GROUP, (g + 1) * GROUP)
        r = slice(g * rows, (g + 1) * rows)
        dmixed = place(back, dms, f).astype(bf16)
        q, k, v = qkv_ref[0, r] * factor, qkv_ref[1, r], qkv_ref[2, r]
        for half in range(2):
            allowed = pair_mask(live_ref[g], half, depth)
            sl = slice(half * half_rows, (half + 1) * half_rows)
            cols = [[], [], []]
            for pair in range(part // 128):
                ln = slice(pair * 128, (pair + 1) * 128)
                q2, k2, v2 = split_heads(q[sl, ln]), k[sl, ln], v[sl, ln]
                dm2 = split_heads(dmixed[sl, ln])
                probs = pair_probs(q2, k2, allowed)
                dprobs = dot(v2, dm2, 1, 1)
                inner = jnp.sum(probs * dprobs, axis=0, keepdims=True)
                ds = (probs * (dprobs - inner)).astype(bf16)
                cols[0].append((join_heads(dot(ds, k2, 0, 0)) * factor).astype(bf16))
                cols[1].append(dot(ds, q2, 1, 0).astype(bf16))
                cols[2].append(dot(probs.astype(bf16), dm2, 1, 0).astype(bf16))
            for c in range(3):
                every[c].append(jnp.concatenate(cols[c], 1) if len(cols[c]) > 1 else cols[c][0])
    dqkv = [jnp.concatenate(p, 0) for p in every]
    rows = step * depth
    pieces = [x[...].reshape(rows, part) for x in xs]
    rms = row_scale(pieces)
    inner = jnp.zeros((rows, 1), f32)
    for j in range(count):
        owner = me ^ j
        xhat = pieces[j].astype(f32) * rms
        scaled = xhat * gain_ref[owner]
        normed = scaled.astype(bf16)
        dn = jnp.zeros((rows, part), f32)
        for c in range(3):
            dn = dn + dot(dqkv[c], w_ref[c, owner], 1, 1)
            wsum_ref[c, owner] += dot(normed, dqkv[c], 0, 0)
        inner = inner + jnp.sum(scaled * dn, axis=-1, keepdims=True)
        gsum_ref[owner] += jnp.sum(dn * xhat, axis=0, keepdims=True)
        (send_ref if j & 1 else keep_ref)[j // 2, :rows] = dn.astype(bf16)
    size = GROUP * depth
    lines = [column_to_row(inner[g * size : (g + 1) * size]) for g in range(step // GROUP)]
    lines = [line[:, i : i + part] for line in lines for i in range(0, size, part)]
    lines.append(jnp.zeros((EXTRA - len(lines), part), f32))
    lines = jnp.concatenate(lines, 0).astype(bf16)
    for i in range(count // 2):
        send_ref[i, rows:] = lines
        keep_ref[i, rows:] = lines


def attention_back(idx, xs, dms, qkv, w, gain, live, chunk, chunks):
    count = len(xs)
    frames, depth, part = xs[0].shape
    local = dms[0].shape[0]
    frames = frames // chunks
    step = per_step(frames, STEP)
    n = frames // step
    base = chunk * n
    rows = step * depth
    lives = pl.BlockSpec((step // GROUP, 1, GROUP * depth), lambda i, s: (i + base, 0, 0))
    return pl.pallas_call(
        functools.partial(attn_back_kernel, count),
        grid_spec=pltpu.PrefetchScalarGridSpec(
            num_scalar_prefetch=1,
            grid=(n,),
            in_specs=[pl.BlockSpec((step, depth, part), lambda i, s: (i + base, 0, 0))] * count
            + [pl.BlockSpec((local, step, part), lambda i, s: (0, i + base, 0))] * count
            + [
                pl.BlockSpec((3, rows, part), lambda i, s: (0, i, 0)),
                pl.BlockSpec(w.shape, lambda i, s: (0, 0, 0, 0)),
                pl.BlockSpec(gain.shape, lambda i, s: (0, 0, 0)),
                lives,
            ],
            out_specs=[pl.BlockSpec((count // 2, rows + EXTRA, part), lambda i, s: (0, i, 0))] * 2
            + [
                pl.BlockSpec(w.shape, lambda i, s: (0, 0, 0, 0)),
                pl.BlockSpec((count, 1, part), lambda i, s: (0, 0, 0)),
            ],
        ),
        out_shape=[jax.ShapeDtypeStruct((count // 2, n * (rows + EXTRA), part), bf16)] * 2
        + [
            jax.ShapeDtypeStruct(w.shape, f32),
            jax.ShapeDtypeStruct((count, 1, part), f32),
        ],
        compiler_params=params(),
        cost_estimate=cost(14),
    )(idx, *xs, *dms, qkv, w, gain, live)


def input_kernel(count, terms_count, idx_ref, *refs):
    xs = refs[:count]
    dhs = refs[count : 2 * count]
    terms = refs[2 * count : 2 * count + terms_count]
    gain_ref, out_ref = refs[2 * count + terms_count :]
    me = idx_ref[0]
    step, depth, part = xs[0].shape
    rows = GROUP * depth
    back = from_owners(me, rows, depth, depth // count)
    sums = terms[0][0, step * depth :].astype(f32)
    for t in terms[1:]:
        sums = sums + t[0, step * depth :].astype(f32)
    lines = rows // part
    for g in range(step // GROUP):
        f = slice(g * GROUP, (g + 1) * GROUP)
        r = slice(g * rows, (g + 1) * rows)
        resid = place(back, dhs, f)
        pieces = [x[f].reshape(rows, part) for x in xs]
        rms = row_scale(pieces)
        xhat = pieces[0].astype(f32) * rms
        dn = terms[0][0, r].astype(f32)
        for t in terms[1:]:
            dn = dn + t[0, r].astype(f32)
        line = [sums[i : i + 1] for i in range(g * lines, (g + 1) * lines)]
        line = jnp.concatenate(line, 1) if lines > 1 else line[0]
        inner = row_to_column(line) / (part * count)
        out = resid + rms * (dn * gain_ref[me] - xhat * inner)
        out_ref[f] = out.astype(bf16).reshape(GROUP, depth, part)


def input_grad(idx, xs, dhs, terms, gain, chunk, chunks):
    count = len(xs)
    frames, depth, part = xs[0].shape
    local = dhs[0].shape[0]
    frames = frames // chunks
    step = per_step(frames, STEP)
    n = frames // step
    base = chunk * n
    rows = step * depth
    return pl.pallas_call(
        functools.partial(input_kernel, count, len(terms)),
        grid_spec=pltpu.PrefetchScalarGridSpec(
            num_scalar_prefetch=1,
            grid=(n,),
            in_specs=[pl.BlockSpec((step, depth, part), lambda i, s: (i + base, 0, 0))] * count
            + [pl.BlockSpec((local, step, part), lambda i, s: (0, i + base, 0))] * count
            + [pl.BlockSpec((1, rows + EXTRA, part), lambda i, s: (0, i, 0))] * len(terms)
            + [pl.BlockSpec(gain.shape, lambda i, s: (0, 0, 0))],
            out_specs=pl.BlockSpec((step, depth, part), lambda i, s: (i, 0, 0)),
        ),
        out_shape=jax.ShapeDtypeStruct((frames, depth, part), bf16),
        compiler_params=params(),
        cost_estimate=cost(4),
    )(idx, *xs, *dhs, *terms, gain)


def block_kernel(count, idx_ref, *refs):
    hidden_ref, live_ref, outs = refs[6], refs[7], refs[8:]
    me = idx_ref[0]
    part = outs[0].shape[2]
    branch = sum_halves(refs[:6])
    rows = ((hidden_ref[0] + branch) * row_to_column(live_ref[0])).astype(bf16)
    blocks = [rows[:, b * part : (b + 1) * part] for b in range(count)]
    for j in range(count):
        outs[j][0] = pick(blocks, me ^ j)


def block_rows(idx, recv, own, hidden, live, count):
    local, frames, width = hidden.shape
    part = width // count
    each = pl.BlockSpec((1, frames, width), lambda k, s: (k, 0, 0))
    return pl.pallas_call(
        functools.partial(block_kernel, count),
        grid_spec=pltpu.PrefetchScalarGridSpec(
            num_scalar_prefetch=1,
            grid=(local,),
            in_specs=half_specs(local, frames, width) * 3
            + [each, pl.BlockSpec((1, 1, frames), lambda k, s: (k, 0, 0))],
            out_specs=[pl.BlockSpec((1, frames, part), lambda k, s: (k, 0, 0))] * count,
        ),
        out_shape=[jax.ShapeDtypeStruct((local, frames, part), bf16)] * count,
        compiler_params=params(),
        cost_estimate=cost(4),
    )(idx, *recv, *own, hidden, live)


def gather_kernel(count, idx_ref, *refs):
    pieces, out_ref = refs[:count], refs[count]
    step, depth, part = out_ref.shape
    back = from_owners(idx_ref[0], GROUP * depth, depth, depth // count)
    for g in range(step // GROUP):
        f = slice(g * GROUP, (g + 1) * GROUP)
        out = place(back, pieces, f)
        out_ref[f] = out.astype(bf16).reshape(GROUP, depth, part)


def gather_block(idx, pieces):
    count = len(pieces)
    local, frames, part = pieces[0].shape
    depth = local * count
    step = per_step(frames, 64)
    return pl.pallas_call(
        functools.partial(gather_kernel, count),
        grid_spec=pltpu.PrefetchScalarGridSpec(
            num_scalar_prefetch=1,
            grid=(frames // step,),
            in_specs=[pl.BlockSpec((local, step, part), lambda i, s: (0, i, 0))] * count,
            out_specs=pl.BlockSpec((step, depth, part), lambda i, s: (i, 0, 0)),
        ),
        out_shape=jax.ShapeDtypeStruct((frames, depth, part), bf16),
        compiler_params=params(),
        cost_estimate=cost(4),
    )(idx, *pieces)


def swap(value, count, bits, axis="pos"):
    return lax.ppermute(value, axis, [(i, i ^ bits) for i in range(count)])


def exchange(pieces):
    count = len(pieces)
    return [pieces[0]] + [swap(pieces[j], count, j) for j in range(1, count)]


def gather_pos(value, count):
    pieces = {0: value}
    bit = count // 2
    while bit:
        for j in list(pieces):
            pieces[j ^ bit] = swap(pieces[j], count, bit)
        bit //= 2
    return [pieces[j] for j in range(count)]


def sum_axis(value, count, axis):
    bit = 1
    while bit < count:
        value = value + swap(value, count, bit, axis)
        bit *= 2
    return value


def after(value, *others):
    return lax.optimization_barrier((value, *others))[0]


def scatter_halves(blocks, bits, axis):
    count = blocks.shape[0]
    blocks = blocks.astype(f32)
    left = list(range(count))
    for bit in bits:
        keep = [i for i, j in enumerate(left) if not j & bit]
        send = [left.index(left[i] ^ bit) for i in keep]
        moved = swap(jnp.stack([blocks[i] for i in send]).astype(bf16), count, bit, axis)
        blocks = jnp.stack([blocks[i] for i in keep]) + moved.astype(f32)
        left = [left[i] for i in keep]
    return blocks[0]


def gather_doubles(value, count, bits, axis):
    blocks, have = value[None], [0]
    for bit in bits:
        blocks = jnp.concatenate([blocks, swap(blocks, count, bit, axis)], 0)
        have = have + [j ^ bit for j in have]
    inverse = jnp.array([have.index(j) for j in range(count)])
    order = jnp.take(inverse, lax.axis_index(axis) ^ jnp.arange(count), mode="clip")
    return jnp.take(blocks, order, axis=0, mode="clip")


def ring_steps(count):
    order = list(range(0, count, 2)) + list(range(count - 1, 0, -2))
    forward = [(order[i], order[(i + 1) % count]) for i in range(count)]
    return forward, [(b, a) for a, b in forward]


def ring_gather(value, steps, count, beside=None):
    forward, back = steps
    far = count // 2
    blocks = [[None, None] for _ in range(count)]
    blocks[0] = list(value)
    x_up, x_down = value
    y_up, y_down = value[1], value[0]
    tie = []
    for s in range(1, far + 1):
        if tie:
            x_up, x_down = after(x_up, *tie), after(x_down, *tie)
            y_up, y_down = after(y_up, *tie), after(y_down, *tie)
        tie = beside(s - 1, blocks) if beside else []
        x_up = blocks[s][0] = lax.ppermute(x_up, "frames", forward)
        x_down = blocks[count - s][1] = lax.ppermute(x_down, "frames", back)
        if s < far:
            y_up = blocks[s][1] = lax.ppermute(y_up, "frames", forward)
            y_down = blocks[count - s][0] = lax.ppermute(y_down, "frames", back)
    if beside:
        beside(far, blocks)
    return blocks


def ring_sum(blocks, steps, count, beside):
    forward, back = steps
    far = count // 2
    y_up = lax.ppermute(blocks[count - far + 1][1], "frames", forward)
    y_down = lax.ppermute(blocks[far - 1][0], "frames", back)
    x_up = lax.ppermute(blocks[far][0], "frames", forward)
    x_down = lax.ppermute(blocks[far][1], "frames", back)
    tie = beside(0, blocks[far])
    for h in range(far - 1, 0, -1):
        ready = []
        if h < far - 1:
            x, y = merge(after(blocks[count - h][1], *tie), blocks[h][0], y_up, y_down)
            y_up = lax.ppermute(x, "frames", forward)
            y_down = lax.ppermute(y, "frames", back)
            ready = [x, y]
        x, y = merge(after(blocks[count - h][0], *tie), blocks[h][1], x_up, x_down)
        x_up = lax.ppermute(x, "frames", forward)
        x_down = lax.ppermute(y, "frames", back)
        tie = beside(far - h, ready + [x, y])
    return [x_up, y_up, y_down, x_down], tie


CHUNKS = 2


def body(inputs, counts, gain_attn, weight_qkv, weight_out, gain_ffn, weight_ffn, cotangent):
    count = lax.axis_size("pos")
    ring = lax.axis_size("frames")
    me = lax.axis_index("pos")
    idx = me.astype(jnp.int32).reshape(1)
    frames, depth, part = inputs.shape
    width = part * count
    local = depth // count
    steps = ring_steps(ring)

    positions = jnp.arange(depth, dtype=jnp.int32)
    live = (positions[None, :] < counts[:, None]).astype(f32)
    live_rows = live.reshape(frames // GROUP, 1, GROUP * depth)
    live_own = lax.dynamic_slice_in_dim(live, me * local, local, 1).T.reshape(local, 1, frames)
    w_qkv = weight_qkv.transpose(1, 0, 2).reshape(3, count, part, part)
    w_out = weight_out.reshape(count, part, width)
    gain1 = gain_attn.reshape(count, 1, part)
    gain2 = gain_ffn.reshape(local, 1, width)

    cot_pieces = split_cot(idx, cotangent, live_rows, count)
    w_ffn = after(weight_ffn, cot_pieces[0]).transpose(1, 2, 0, 3)
    cot_pieces = exchange(cot_pieces)

    order = me ^ jnp.arange(count)
    branch = jnp.take(jnp.stack(cot_pieces), order, axis=0, mode="clip").transpose(1, 2, 0, 3)
    branch = branch.reshape(local, frames, width)
    half = local // 2
    xs = gather_pos(after(inputs, branch, w_ffn), count)

    parts = []

    def beside_grads(step, blocks):
        if 1 <= step <= CHUNKS:
            first = after(xs[0], *blocks[step], *blocks[ring - step])
            parts.append(
                attention(idx, [first] + xs[1:], w_qkv, gain1, live_rows, step - 1, CHUNKS)
            )
        return []

    grads = ring_gather([branch[:half], branch[half:]], steps, ring, beside_grads)
    qkvs = [p[0] for p in parts]
    resids = [p[1] for p in parts]
    mixeds = [exchange(p[2:]) for p in parts]
    hidden, *norm = project(idx, mixeds, resids, w_out, gain2)

    far = ring // 2
    groups = [[0]] + [[s, ring - s] for s in range(1, far)] + [[far]]
    dnorms, branches, acts = [None] * ring, [None] * ring, []

    def beside_norms(step, blocks):
        group = groups[step]
        norms = [list(blocks[d]) for d in group]
        if step:
            norms[0][0] = after(norms[0][0], acts[-1])
        down, forth, act = ffn(norms, [grads[d] for d in group], w_ffn)
        for i, d in enumerate(group):
            dnorms[d], branches[d] = down[i], forth[i]
        acts.append(act)
        return [act]

    norms = ring_gather(norm, steps, ring, beside_norms)

    totals, sets = [], [range(q, min(q + 6, far + 1)) for q in range(0, far + 1, 6)]

    def weights(row, ready):
        for i, chosen in enumerate(sets):
            if row == 0:
                totals.append(None)
            others = [(grads if row == 2 else norms)[d] for q in chosen for d in groups[q]]
            mine = [acts[q] for q in chosen]
            mine[0] = after(mine[0], *ready)
            totals[i] = weight_grad(mine, others, row, totals[i])
        return totals

    def beside_low(step, ready):
        return weights(step - 1, ready) if 1 <= step <= 3 else []

    recv, tie = ring_sum(dnorms, steps, ring, beside_low)
    for d in (far, far - 1, far + 1):
        branches[d] = [after(b, recv[1], recv[2]) for b in branches[d]]
    recv[0] = after(recv[0], *tie)
    low, gsum, *rest = resid_grad(idx, recv, dnorms[0], hidden, branch, gain2, w_out)
    dms = exchange(rest[:count])
    dhs = exchange([rest[count]] + [after(v, *dms) for v in rest[count + 1 :]])

    backs = []

    def beside_block(step, ready):
        if 1 <= step <= CHUNKS:
            c = step - 1
            first = after(dms[0], *ready)
            backs.append(
                attention_back(
                    idx, xs, [first] + dms[1:], qkvs[c], w_qkv, gain1, live_rows, c, CHUNKS
                )
            )
            return backs[-1][:1]
        return []

    recv, _ = ring_sum(branches, steps, ring, beside_block)
    rows = block_rows(idx, recv, branches[0], hidden, live_own, count)
    block_out = gather_block(idx, exchange(rows))

    grad_in, qkv_part, gain_part = [], 0.0, 0.0
    for c in range(CHUNKS):
        keep, send, qkv_c, gain_c = backs[c]
        qkv_part = qkv_part + qkv_c
        gain_part = gain_part + gain_c
        terms = [keep, swap(send, count, 1)]
        bit = 1
        while bit < count // 2:
            total = sum(t.astype(f32) for t in terms).astype(bf16)
            index = [i for i in range(total.shape[0]) if i & 1]
            going = jnp.stack([total[i] for i in index])
            stay = [i for i in range(total.shape[0]) if not i & 1]
            terms = [jnp.stack([t[i] for i in stay]) for t in terms]
            terms.append(swap(going, count, 2 * bit))
            bit *= 2
        grad_in.append(input_grad(idx, xs, dhs, terms, gain1, c, CHUNKS))
    grad_in = jnp.concatenate(grad_in, 0)

    ffn_grad = totals[0]
    for term in totals[1:]:
        ffn_grad = ffn_grad + term
    ffn_grad = ffn_grad.transpose(0, 2, 1, 3)

    mixed_all = [jnp.concatenate([m[j] for m in mixeds], 1) for j in range(count)]
    out_part = jnp.stack(
        [
            jnp.einsum("kfd,kfe->de", m, low, preferred_element_type=f32).astype(bf16)
            for m in mixed_all
        ]
    )
    out_part = after(out_part, *dms)
    bits = [1 << i for i in range((count - 1).bit_length())]
    ring_bits = [1 << i for i in range((ring - 1).bit_length())]
    out_low = scatter_halves(out_part, bits, "pos")
    ring_order = lax.axis_index("frames") ^ jnp.arange(ring)
    out_low = out_low.astype(bf16).reshape(ring, part // ring, width)
    out_low = jnp.take(out_low, ring_order, axis=0, mode="clip")
    out_low = scatter_halves(out_low, ring_bits, "frames")
    out_grad = gather_doubles(out_low.astype(bf16), ring, ring_bits, "frames")
    out_grad = gather_doubles(out_grad, count, bits[::-1], "pos")
    out_grad = out_grad.reshape(width, width).astype(f32)
    rows = width // ring
    qkv_rows = qkv_part.reshape(3, ring, rows, part).transpose(1, 0, 2, 3)
    packed = [
        qkv_rows.reshape(ring, 3 * rows, part),
        jnp.broadcast_to(gain_part.reshape(1, count, part), (ring, count, part)),
    ]
    columns = gsum.reshape(local, ring, rows).transpose(1, 0, 2).reshape(ring, local * rows)
    lines = -(-local * rows // part)
    columns = jnp.pad(columns, ((0, 0), (0, lines * part - local * rows)))
    packed.append(columns.reshape(ring, lines, part))
    packed = jnp.concatenate([p.astype(bf16) for p in packed], 1)
    moved = lax.all_to_all(packed, "frames", 0, 0, tiled=True)
    moved = jnp.sum(moved.astype(f32), axis=0)
    qkv_grad = moved[: 3 * rows].reshape(3, rows, part)
    gain_attn_grad = sum_axis(moved[3 * rows : 3 * rows + count], count, "pos").reshape(width)
    gain_ffn_grad = moved[3 * rows + count :].reshape(-1)[: local * rows].reshape(local, rows)
    return (
        block_out,
        grad_in,
        gain_attn_grad,
        qkv_grad.transpose(1, 0, 2),
        out_grad,
        gain_ffn_grad,
        ffn_grad,
    )


def solution(mesh):
    placed = (
        P("frames", None, "pos"),
        P("frames"),
        P(),
        P(None, None, "pos"),
        P(),
        P("pos", None),
        P("frames", "pos", None, None),
        P("frames", None, "pos"),
    )
    return jax.shard_map(
        body,
        mesh=mesh,
        in_specs=placed,
        out_specs=(
            P("frames", None, "pos"),
            P("frames", None, "pos"),
            P(),
            P("frames", None, "pos"),
            P(),
            P("pos", "frames"),
            P("frames", "pos", None, None),
        ),
        check_vma=False,
    )
```

```python
import functools

import jax
import jax.numpy as jnp
from jax import lax
from jax.experimental import pallas as pl
from jax.experimental.pallas import tpu as pltpu
from jax.sharding import PartitionSpec as P

HEAD_DIM = 64
EPS = 1e-05
MASKED = -1e30
GROUP = 16
STEP = 32
EXTRA = 16
COST = 0.0001
VMEM_LIMIT = 56 * 1024 * 1024

f32 = jnp.float32
bf16 = jnp.bfloat16


def dot(a, b, ca, cb):
    return lax.dot_general(a, b, (((ca,), (cb,)), ((), ())), preferred_element_type=f32)


def cost(us):
    us = us * COST
    return pl.CostEstimate(flops=int(us * 1.15e9), bytes_accessed=int(us * 1e6), transcendentals=0)


def params():
    return pltpu.CompilerParams(vmem_limit_bytes=VMEM_LIMIT)


def to_owners(me, rows, depth, local):
    r = lax.broadcasted_iota(jnp.int32, (rows, rows), 0)
    c = lax.broadcasted_iota(jnp.int32, (rows, rows), 1)
    frames = rows // depth
    k = r // frames
    source = (r % frames) * depth + ((k // local) ^ me) * local + k % local
    return jnp.where(c == source, 1.0, 0.0).astype(bf16)


def from_owners(me, rows, depth, local):
    r = lax.broadcasted_iota(jnp.int32, (rows, rows), 0)
    c = lax.broadcasted_iota(jnp.int32, (rows, rows), 1)
    frames = rows // depth
    k = r % depth
    source = (((k // local) ^ me) * local + k % local) * frames + r // depth
    return jnp.where(c == source, 1.0, 0.0).astype(bf16)


def pick(blocks, index):
    out = blocks[0]
    for b in range(1, len(blocks)):
        out = jnp.where(index == b, blocks[b], out)
    return out


def row_to_column(row):
    n = row.shape[1]
    r = lax.broadcasted_iota(jnp.int32, (n, n), 0)
    c = lax.broadcasted_iota(jnp.int32, (n, n), 1)
    return jnp.sum(jnp.where(r == c, row, 0.0), axis=1, keepdims=True)


def column_to_row(column):
    n = column.shape[0]
    r = lax.broadcasted_iota(jnp.int32, (n, n), 0)
    c = lax.broadcasted_iota(jnp.int32, (n, n), 1)
    return jnp.sum(jnp.where(r == c, column, 0.0), axis=0, keepdims=True)


def pair_mask(live_row, half, depth):
    n = live_row.shape[1] // 2
    live = row_to_column(live_row[:, half * n : (half + 1) * n])
    r = lax.broadcasted_iota(jnp.int32, (n, n), 0)
    c = lax.broadcasted_iota(jnp.int32, (n, n), 1)
    allowed = ((r // depth) == (c // depth)) & (r <= c) & (live > 0.5)
    return jnp.concatenate([allowed, allowed], 1)


def split_heads(block):
    lane = lax.broadcasted_iota(jnp.int32, block.shape, 1)
    zero = jnp.zeros_like(block)
    return jnp.concatenate(
        [jnp.where(lane < HEAD_DIM, block, zero), jnp.where(lane >= HEAD_DIM, block, zero)], 0
    )


def join_heads(pair):
    n = pair.shape[0] // 2
    lane = lax.broadcasted_iota(jnp.int32, (n, pair.shape[1]), 1)
    return jnp.where(lane < HEAD_DIM, pair[:n], pair[n:])


def pair_probs(q2, k2, allowed):
    scores = jnp.where(allowed, dot(k2, q2, 1, 1), MASKED)
    e = jnp.exp(scores - jnp.max(scores, axis=0, keepdims=True))
    return e * (1.0 / jnp.sum(e, axis=0, keepdims=True))


def per_step(frames, step):
    return min(step, frames)


def place(back, pieces, f):
    local, _, part = pieces[0].shape
    blocks = [p[:, f].reshape(local * GROUP, part) for p in pieces]
    return dot(back, jnp.concatenate(blocks, 0), 1, 0)


def row_scale(pieces):
    total = None
    for x in pieces:
        xf = x.astype(f32)
        term = jnp.sum(xf * xf, axis=-1, keepdims=True)
        total = term if total is None else total + term
    return lax.rsqrt(total / (pieces[0].shape[1] * len(pieces)) + EPS)


def cot_kernel(count, idx_ref, cot_ref, live_ref, *outs):
    step, depth, part = cot_ref.shape
    rows = GROUP * depth
    local = depth // count
    move = to_owners(idx_ref[0], rows, depth, local)
    for g in range(step // GROUP):
        f = slice(g * GROUP, (g + 1) * GROUP)
        live = row_to_column(live_ref[g])
        masked = (cot_ref[f].reshape(rows, part).astype(f32) * live).astype(bf16)
        moved = dot(move, masked, 1, 0).astype(bf16).reshape(count, local, GROUP, part)
        for j in range(count):
            outs[j][:, f] = moved[j]


def split_cot(idx, cot, live, count):
    frames, depth, part = cot.shape
    local = depth // count
    step = per_step(frames, 64)
    return pl.pallas_call(
        functools.partial(cot_kernel, count),
        grid_spec=pltpu.PrefetchScalarGridSpec(
            num_scalar_prefetch=1,
            grid=(frames // step,),
            in_specs=[
                pl.BlockSpec((step, depth, part), lambda i, s: (i, 0, 0)),
                pl.BlockSpec((step // GROUP, 1, GROUP * depth), lambda i, s: (i, 0, 0)),
            ],
            out_specs=[pl.BlockSpec((local, step, part), lambda i, s: (0, i, 0))] * count,
        ),
        out_shape=[jax.ShapeDtypeStruct((local, frames, part), bf16)] * count,
        compiler_params=params(),
        cost_estimate=cost(4),
    )(idx, cot, live)


def attn_kernel(count, idx_ref, *refs):
    xs = refs[:count]
    w_ref, gain_ref, live_ref = refs[count : count + 3]
    qkv_ref, resid_ref = refs[count + 3 : count + 5]
    outs = refs[count + 5 :]
    me = idx_ref[0]
    step, depth, part = xs[0].shape
    rows = GROUP * depth
    local = depth // count
    half_rows = rows // 2
    move = to_owners(me, rows, depth, local)
    own = move[: local * GROUP]
    for g in range(step // GROUP):
        f = slice(g * GROUP, (g + 1) * GROUP)
        r = slice(g * rows, (g + 1) * rows)
        pieces = [x[f].reshape(rows, part) for x in xs]
        rms = row_scale(pieces)
        acc = [None] * 3
        for j in range(count):
            normed = (pieces[j].astype(f32) * rms * gain_ref[me ^ j]).astype(bf16)
            for c in range(3):
                term = dot(normed, w_ref[c, me ^ j], 1, 0)
                acc[c] = term if acc[c] is None else acc[c] + term
            moved = dot(own, pieces[j], 1, 0).astype(bf16)
            resid_ref[me ^ j, :, f] = moved.reshape(local, GROUP, part)
        q, k, v = [a.astype(bf16) for a in acc]
        qkv_ref[0, r], qkv_ref[1, r], qkv_ref[2, r] = q, k, v
        q = q * (HEAD_DIM**-0.5)
        mixed = []
        for half in range(2):
            allowed = pair_mask(live_ref[g], half, depth)
            sl = slice(half * half_rows, (half + 1) * half_rows)
            cols = []
            for pair in range(part // 128):
                ln = slice(pair * 128, (pair + 1) * 128)
                probs = pair_probs(split_heads(q[sl, ln]), k[sl, ln], allowed).astype(bf16)
                cols.append(join_heads(dot(probs, v[sl, ln], 0, 0)).astype(bf16))
            mixed.append(jnp.concatenate(cols, 1) if len(cols) > 1 else cols[0])
        mixed = jnp.concatenate(mixed, 0)
        moved = dot(move, mixed, 1, 0).astype(bf16).reshape(count, local, GROUP, part)
        for j in range(count):
            outs[j][:, f] = moved[j]


def attention(idx, xs, w, gain, live, chunk, chunks):
    count = len(xs)
    frames, depth, part = xs[0].shape
    local = depth // count
    frames = frames // chunks
    step = per_step(frames, STEP)
    n = frames // step
    base = chunk * n
    rows = step * depth
    return pl.pallas_call(
        functools.partial(attn_kernel, count),
        grid_spec=pltpu.PrefetchScalarGridSpec(
            num_scalar_prefetch=1,
            grid=(n,),
            in_specs=[pl.BlockSpec((step, depth, part), lambda i, s: (i + base, 0, 0))] * count
            + [
                pl.BlockSpec(w.shape, lambda i, s: (0, 0, 0, 0)),
                pl.BlockSpec(gain.shape, lambda i, s: (0, 0, 0)),
                pl.BlockSpec((step // GROUP, 1, GROUP * depth), lambda i, s: (i + base, 0, 0)),
            ],
            out_specs=[
                pl.BlockSpec((3, rows, part), lambda i, s: (0, i, 0)),
                pl.BlockSpec((count, local, step, part), lambda i, s: (0, 0, i, 0)),
            ]
            + [pl.BlockSpec((local, step, part), lambda i, s: (0, i, 0))] * count,
        ),
        out_shape=[
            jax.ShapeDtypeStruct((3, frames * depth, part), bf16),
            jax.ShapeDtypeStruct((count, local, frames, part), bf16),
        ]
        + [jax.ShapeDtypeStruct((local, frames, part), bf16)] * count,
        compiler_params=params(),
        cost_estimate=cost(8),
    )(idx, *xs, w, gain, live)


def half_specs(local, frames, width):
    half = local // 2
    return [
        pl.BlockSpec((1, frames, width), lambda k, *s: (jnp.minimum(k, half - 1), 0, 0)),
        pl.BlockSpec((1, frames, width), lambda k, *s: (jnp.maximum(k - half, 0), 0, 0)),
    ]


def store_half(is_first, first_ref, second_ref, at, value):
    @pl.when(is_first)
    def _():
        first_ref[at] = value

    @pl.when(jnp.logical_not(is_first))
    def _():
        second_ref[at] = value


def load_half(is_first, first_ref, second_ref):
    return jnp.where(is_first, first_ref[0], second_ref[0])


def project_kernel(count, chunks, idx_ref, *refs):
    mixed = refs[: count * chunks]
    resids = refs[count * chunks : (count + 1) * chunks]
    w_ref, gain_ref, hidden_ref, norm_ref = refs[(count + 1) * chunks :]
    me = idx_ref[0]
    size = mixed[0].shape[1]
    for c in range(chunks):
        f = slice(c * size, (c + 1) * size)
        hidden = jnp.concatenate([resids[c][b, 0] for b in range(count)], 1).astype(f32)
        for j in range(count):
            hidden = hidden + dot(mixed[c * count + j][0], w_ref[me ^ j], 1, 0)
        hidden_ref[0, f] = hidden
        rms = lax.rsqrt(jnp.mean(hidden * hidden, axis=-1, keepdims=True) + EPS)
        norm_ref[0, f] = (hidden * rms * gain_ref[0]).astype(bf16)


def project(idx, mixed, resids, w, gain):
    chunks, count = len(mixed), len(mixed[0])
    local, size, part = mixed[0][0].shape
    frames, width = size * chunks, part * count
    each = pl.BlockSpec((1, frames, width), lambda k, s: (k, 0, 0))
    return pl.pallas_call(
        functools.partial(project_kernel, count, chunks),
        grid_spec=pltpu.PrefetchScalarGridSpec(
            num_scalar_prefetch=1,
            grid=(local,),
            in_specs=[pl.BlockSpec((1, size, part), lambda k, s: (k, 0, 0))] * (count * chunks)
            + [pl.BlockSpec((count, 1, size, part), lambda k, s: (0, k, 0, 0))] * chunks
            + [
                pl.BlockSpec(w.shape, lambda k, s: (0, 0, 0)),
                pl.BlockSpec((1, 1, width), lambda k, s: (k, 0, 0)),
            ],
            out_specs=[each, each],
        ),
        out_shape=[
            jax.ShapeDtypeStruct((local, frames, width), f32),
            jax.ShapeDtypeStruct((local, frames, width), bf16),
        ],
        compiler_params=params(),
        cost_estimate=cost(6),
    )(idx, *[m for part_ in mixed for m in part_], *resids, w, gain)


def load_block(is_first, refs):
    return refs[0][0] if len(refs) == 1 else load_half(is_first, *refs)


def block_parts(block):
    return list(block) if isinstance(block, tuple) else [block]


def ffn_kernel(sizes, idx_ref, *refs):
    n = len(sizes) // 2
    ins = sum(sizes)
    w_ref = refs[ins]
    dnorms, branches = refs[ins + 1 : ins + 1 + 2 * n], refs[ins + 1 + 2 * n : ins + 1 + 3 * n]
    act_ref = refs[-1]
    is_first = pl.program_id(0) < pl.num_programs(0) // 2
    blocks, at = [], 0
    for size in sizes:
        blocks.append(load_block(is_first, refs[at : at + size]))
        at += size
    frames = blocks[0].shape[0]
    norm = jnp.concatenate(blocks[:n], 0)
    grad = jnp.concatenate(blocks[n:], 0)
    gate = dot(norm, w_ref[0, 0], 1, 1)
    up = dot(norm, w_ref[0, 1], 1, 1)
    dact = dot(grad, w_ref[0, 2], 1, 1)
    sig = jax.nn.sigmoid(gate)
    silu = gate * sig
    act = (silu * up).astype(bf16)
    dgate = (dact * up * sig * (1.0 + gate * (1.0 - sig))).astype(bf16)
    dup = (dact * silu).astype(bf16)
    act_ref[0, 0] = dgate
    act_ref[0, 1] = dup
    act_ref[0, 2] = act
    dnorm = (dot(dgate, w_ref[0, 0], 1, 0) + dot(dup, w_ref[0, 1], 1, 0)).astype(bf16)
    branch = dot(act, w_ref[0, 2], 1, 0).astype(bf16)
    for i in range(n):
        rows = slice(i * frames, (i + 1) * frames)
        store_half(is_first, *dnorms[2 * i : 2 * i + 2], 0, dnorm[rows])
        branches[i][0] = branch[rows]


def ffn(idx, norms, grads, w):
    n = len(norms)
    blocks = [block_parts(v) for v in (*norms, *grads)]
    local, _, hidden, width = w.shape
    frames = blocks[0][0].shape[1]
    halves = half_specs(local, frames, width)
    whole = [pl.BlockSpec((1, frames, width), lambda k, s: (k, 0, 0))]
    *out, act = pl.pallas_call(
        functools.partial(ffn_kernel, [len(v) for v in blocks]),
        grid_spec=pltpu.PrefetchScalarGridSpec(
            num_scalar_prefetch=1,
            grid=(local,),
            in_specs=[x for v in blocks for x in (whole if len(v) == 1 else halves)]
            + [pl.BlockSpec((1, 3, hidden, width), lambda k, s: (k, 0, 0, 0))],
            out_specs=halves * n
            + whole * n
            + [pl.BlockSpec((1, 3, n * frames, hidden), lambda k, s: (k, 0, 0, 0))],
        ),
        out_shape=[jax.ShapeDtypeStruct((local // 2, frames, width), bf16)] * (2 * n)
        + [jax.ShapeDtypeStruct((local, frames, width), bf16)] * n
        + [jax.ShapeDtypeStruct((local, 3, n * frames, hidden), bf16)],
        compiler_params=params(),
        cost_estimate=cost(3.5 + 5 * n),
    )(idx, *[x for v in blocks for x in v], w)
    pairs = [out[i : i + 2] for i in range(0, 2 * n, 2)]
    return pairs, out[2 * n :], act


def weight_kernel(n, row, sizes, idx_ref, *refs):
    acts, out_ref = refs[:n], refs[-1]
    local = acts[0].shape[0]
    others, at = [], n
    for size in sizes:
        others.append(refs[at : at + size])
        at += size
    frames = others[0][0].shape[1]

    def entry(block, k):
        return block[k // block[0].shape[0]][k % block[0].shape[0]]

    for k in range(local):
        total, first = None, 0
        for a in acts:
            size = a.shape[2] // frames
            both = [entry(others[first + i], k) for i in range(size)]
            first += size
            both = jnp.concatenate(both, 0) if size > 1 else both[0]
            term = dot(a[k, 0], both, 0, 0)
            total = term if total is None else total + term
        out_ref[:, 0, k] = total


def weight_grad(idx, acts, others, row, out):
    n = len(acts)
    local, _, _, hidden = acts[0].shape
    chunk = min(128, hidden)
    others = [block_parts(v) for v in others]
    width = others[0][0].shape[2]
    ins = list(acts) + [x for v in others for x in v]
    specs = [
        pl.BlockSpec((local, 1, a.shape[2], chunk), lambda c, s: (0, row, 0, c)) for a in acts
    ] + [
        pl.BlockSpec(x.shape, lambda c, s: (0, 0, 0), pipeline_mode=pl.Buffered(1))
        for v in others
        for x in v
    ]
    aliases = {}
    kernel = functools.partial(weight_kernel, n, row, [len(v) for v in others])
    if out is not None:
        aliases = {1 + len(ins): 0}
        ins.append(out)
        specs.append(pl.BlockSpec(memory_space=pl.ANY))
    return pl.pallas_call(
        kernel,
        grid_spec=pltpu.PrefetchScalarGridSpec(
            num_scalar_prefetch=1,
            grid=(hidden // chunk,),
            in_specs=specs,
            out_specs=pl.BlockSpec((chunk, 1, local, width), lambda c, s: (c, row, 0, 0)),
        ),
        out_shape=jax.ShapeDtypeStruct((hidden, 3, local, width), f32),
        input_output_aliases=aliases,
        compiler_params=params(),
        cost_estimate=cost(12),
    )(idx, *ins)


def add_low(x, y):
    return (x.astype(f32) + y.astype(f32)).astype(bf16)


def merge_kernel(n, idx_ref, *refs):
    for i in range(n):
        refs[2 * n + i][...] = add_low(refs[i][...], refs[n + i][...])


def merge(idx, mine, moved):
    n = len(mine)
    half, frames, width = mine[0].shape
    each = pl.BlockSpec((1, frames, width), lambda k, s: (k, 0, 0))
    return pl.pallas_call(
        functools.partial(merge_kernel, n),
        grid_spec=pltpu.PrefetchScalarGridSpec(
            num_scalar_prefetch=1,
            grid=(half,),
            in_specs=[each] * (2 * n),
            out_specs=[each] * n,
        ),
        out_shape=[jax.ShapeDtypeStruct(mine[0].shape, bf16)] * n,
        compiler_params=params(),
        cost_estimate=cost(1.2 * n),
    )(idx, *mine, *moved)


def whole_kernel(half, idx_ref, f_ref, b_ref, up_ref, down_ref, fo_ref, bo_ref):
    if half is None:
        fo_ref[...] = add_low(f_ref[...], up_ref[...])
        bo_ref[...] = add_low(b_ref[...], down_ref[...])
        return
    is_first = pl.program_id(0) < half
    fo_ref[...] = jnp.where(is_first, add_low(f_ref[...], up_ref[...]), f_ref[...])
    bo_ref[...] = jnp.where(is_first, b_ref[...], add_low(b_ref[...], down_ref[...]))


def merge_whole(idx, f, b, up, down):
    local, frames, width = f.shape
    half = None if up.shape == f.shape else local // 2
    each = pl.BlockSpec((1, frames, width), lambda k, s: (k, 0, 0))
    moved = half_specs(local, frames, width) if half else [each] * 2
    return pl.pallas_call(
        functools.partial(whole_kernel, half),
        grid_spec=pltpu.PrefetchScalarGridSpec(
            num_scalar_prefetch=1,
            grid=(local,),
            in_specs=[each, each, *moved],
            out_specs=[each, each],
        ),
        out_shape=[jax.ShapeDtypeStruct(f.shape, bf16)] * 2,
        compiler_params=params(),
        cost_estimate=cost(4),
    )(idx, f, b, up, down)


def sum_halves(refs):
    is_first = pl.program_id(0) < pl.num_programs(0) // 2
    total = None
    for i in range(0, len(refs), 2):
        term = load_half(is_first, *refs[i : i + 2]).astype(f32)
        total = term if total is None else total + term
    return total


def resid_kernel(count, idx_ref, *refs):
    hidden_ref, branch_ref, gain_ref, w_ref, low_ref, gsum_ref = refs[6:12]
    dms, dhs = refs[12 : 12 + count], refs[12 + count :]
    me = idx_ref[0]
    part = w_ref.shape[1]
    dnorm = sum_halves(refs[:6])
    hidden = hidden_ref[0]
    rms = lax.rsqrt(jnp.mean(hidden * hidden, axis=-1, keepdims=True) + EPS)
    xhat = hidden * rms
    gsum_ref[0] = jnp.sum(dnorm * xhat, axis=0, keepdims=True)
    u = dnorm * gain_ref[0]
    inner = jnp.mean(xhat * u, axis=-1, keepdims=True)
    low = (branch_ref[0].astype(f32) + rms * (u - xhat * inner)).astype(bf16)
    low_ref[0] = low
    blocks = [low[:, b * part : (b + 1) * part] for b in range(count)]
    for j in range(count):
        dhs[j][0] = pick(blocks, me ^ j)
        dms[j][0] = dot(low, w_ref[me ^ j], 1, 1).astype(bf16)


def resid_grad(idx, recv, own, hidden, branch, gain, w):
    count, part, width = w.shape
    local, frames, _ = hidden.shape
    each = pl.BlockSpec((1, frames, width), lambda k, s: (k, 0, 0))
    return pl.pallas_call(
        functools.partial(resid_kernel, count),
        grid_spec=pltpu.PrefetchScalarGridSpec(
            num_scalar_prefetch=1,
            grid=(local,),
            in_specs=half_specs(local, frames, width) * 3
            + [each] * 2
            + [
                pl.BlockSpec((1, 1, width), lambda k, s: (k, 0, 0)),
                pl.BlockSpec(w.shape, lambda k, s: (0, 0, 0)),
            ],
            out_specs=[each, pl.BlockSpec((1, 1, width), lambda k, s: (k, 0, 0))]
            + [pl.BlockSpec((1, frames, part), lambda k, s: (k, 0, 0))] * (2 * count),
        ),
        out_shape=[
            jax.ShapeDtypeStruct((local, frames, width), bf16),
            jax.ShapeDtypeStruct((local, 1, width), f32),
        ]
        + [jax.ShapeDtypeStruct((local, frames, part), bf16)] * (2 * count),
        compiler_params=params(),
        cost_estimate=cost(8),
    )(idx, *recv, *own, hidden, branch, gain, w)


def attn_back_kernel(count, ring, idx_ref, *refs):
    xs = refs[:count]
    dms = refs[count : 2 * count]
    qkv_ref, w_ref, gain_ref, live_ref = refs[2 * count : 2 * count + 4]
    keep_ref, send_ref, wlow_ref, gsum_ref, wsum_ref = refs[2 * count + 4 :]
    me = idx_ref[0]
    step, depth, part = xs[0].shape
    rows = GROUP * depth
    back = from_owners(me, rows, depth, depth // count)
    half_rows = rows // 2
    factor = HEAD_DIM**-0.5

    @pl.when(pl.program_id(0) == 0)
    def _():
        wsum_ref[...] = jnp.zeros_like(wsum_ref)
        gsum_ref[...] = jnp.zeros_like(gsum_ref)

    every, rmss = [[], [], []], []
    for g in range(step // GROUP):
        f = slice(g * GROUP, (g + 1) * GROUP)
        r = slice(g * rows, (g + 1) * rows)
        dmixed = place(back, dms, f).astype(bf16)
        q, k, v = qkv_ref[0, r] * factor, qkv_ref[1, r], qkv_ref[2, r]
        for half in range(2):
            allowed = pair_mask(live_ref[g], half, depth)
            sl = slice(half * half_rows, (half + 1) * half_rows)
            cols = [[], [], []]
            for pair in range(part // 128):
                ln = slice(pair * 128, (pair + 1) * 128)
                q2, k2, v2 = split_heads(q[sl, ln]), k[sl, ln], v[sl, ln]
                dm2 = split_heads(dmixed[sl, ln])
                probs = pair_probs(q2, k2, allowed)
                dprobs = dot(v2, dm2, 1, 1)
                inner = jnp.sum(probs * dprobs, axis=0, keepdims=True)
                ds = (probs * (dprobs - inner)).astype(bf16)
                cols[0].append((join_heads(dot(ds, k2, 0, 0)) * factor).astype(bf16))
                cols[1].append(dot(ds, q2, 1, 0).astype(bf16))
                cols[2].append(dot(probs.astype(bf16), dm2, 1, 0).astype(bf16))
            for c in range(3):
                every[c].append(jnp.concatenate(cols[c], 1) if len(cols[c]) > 1 else cols[c][0])
    dqkv = [jnp.concatenate(p, 0) for p in every]
    rows = step * depth
    pieces = [x[...].reshape(rows, part) for x in xs]
    rms = row_scale(pieces)
    inner = jnp.zeros((rows, 1), f32)
    for j in range(count):
        owner = me ^ j
        xhat = pieces[j].astype(f32) * rms
        scaled = xhat * gain_ref[owner]
        normed = scaled.astype(bf16)
        dn = jnp.zeros((rows, part), f32)
        for c in range(3):
            dn = dn + dot(dqkv[c], w_ref[c, owner], 1, 1)
            wsum_ref[c, owner] += dot(normed, dqkv[c], 0, 0)
        inner = inner + jnp.sum(scaled * dn, axis=-1, keepdims=True)
        gsum_ref[owner] += jnp.sum(dn * xhat, axis=0, keepdims=True)
        (send_ref if j & 1 else keep_ref)[j // 2, :rows] = dn.astype(bf16)
    size = GROUP * depth
    lines = [column_to_row(inner[g * size : (g + 1) * size]) for g in range(step // GROUP)]
    lines = [line[:, i : i + part] for line in lines for i in range(0, size, part)]
    lines.append(jnp.zeros((EXTRA - len(lines), part), f32))
    lines = jnp.concatenate(lines, 0).astype(bf16)
    for i in range(count // 2):
        send_ref[i, rows:] = lines
        keep_ref[i, rows:] = lines

    @pl.when(pl.program_id(0) == pl.num_programs(0) - 1)
    def _():
        size = part * count // ring
        for i in range(ring):
            block, line = i * size // part, i * size % part
            for c in range(3):
                wlow_ref[i, c * size : (c + 1) * size] = wsum_ref[
                    c, block, line : line + size
                ].astype(bf16)


def attention_back(idx, xs, dms, qkv, w, gain, live, ring):
    count = len(xs)
    frames, depth, part = xs[0].shape
    local = dms[0].shape[0]
    step = per_step(frames, STEP)
    n = frames // step
    rows = step * depth
    low_shape = (ring, 3 * part * count // ring, part)
    lives = pl.BlockSpec((step // GROUP, 1, GROUP * depth), lambda i, s: (i, 0, 0))
    return pl.pallas_call(
        functools.partial(attn_back_kernel, count, ring),
        grid_spec=pltpu.PrefetchScalarGridSpec(
            num_scalar_prefetch=1,
            grid=(n,),
            in_specs=[pl.BlockSpec((step, depth, part), lambda i, s: (i, 0, 0))] * count
            + [pl.BlockSpec((local, step, part), lambda i, s: (0, i, 0))] * count
            + [
                pl.BlockSpec((3, rows, part), lambda i, s: (0, i, 0)),
                pl.BlockSpec(w.shape, lambda i, s: (0, 0, 0, 0)),
                pl.BlockSpec(gain.shape, lambda i, s: (0, 0, 0)),
                lives,
            ],
            out_specs=[pl.BlockSpec((count // 2, rows + EXTRA, part), lambda i, s: (0, i, 0))] * 2
            + [
                pl.BlockSpec(low_shape, lambda i, s: (0, 0, 0)),
                pl.BlockSpec((count, 1, part), lambda i, s: (0, 0, 0)),
            ],
            scratch_shapes=[pltpu.VMEM(w.shape, f32)],
        ),
        out_shape=[jax.ShapeDtypeStruct((count // 2, n * (rows + EXTRA), part), bf16)] * 2
        + [
            jax.ShapeDtypeStruct(low_shape, bf16),
            jax.ShapeDtypeStruct((count, 1, part), f32),
        ],
        compiler_params=params(),
        cost_estimate=cost(26),
    )(idx, *xs, *dms, qkv, w, gain, live)


def fold_kernel(n, idx_ref, *refs):
    total = refs[0][...].astype(f32)
    for r in refs[1:n]:
        total = total + r[...].astype(f32)
    refs[n][...] = total.astype(bf16)


def fold(idx, terms, bit):
    n = len(terms)
    _, rows, part = terms[0].shape
    hop = bit // 2

    def spec(i):
        step = 1 if i < 2 else 1 << (i - 1)
        return pl.BlockSpec((1, rows, part), lambda g, s: (hop * (2 * g + 1) // step, 0, 0))

    return pl.pallas_call(
        functools.partial(fold_kernel, n),
        grid_spec=pltpu.PrefetchScalarGridSpec(
            num_scalar_prefetch=1,
            grid=(terms[0].shape[0] // bit,),
            in_specs=[spec(i) for i in range(n)],
            out_specs=pl.BlockSpec((1, rows, part), lambda g, s: (g, 0, 0)),
        ),
        out_shape=jax.ShapeDtypeStruct((terms[0].shape[0] // bit, rows, part), bf16),
        compiler_params=params(),
        cost_estimate=cost(2),
    )(idx, *terms)


def out_kernel(count, chunks, idx_ref, *refs):
    low_ref, outs = refs[count * chunks], refs[count * chunks + 1 :]
    local, size, _ = refs[0].shape
    width = low_ref.shape[2]
    lows = []
    for c in range(chunks):
        part_ = low_ref[:, c * size : (c + 1) * size]
        lows.append(part_.reshape(local * size, width))
    low = jnp.concatenate(lows, 0)
    for j in range(count):
        mine = [refs[c * count + j][...].reshape(local * size, -1) for c in range(chunks)]
        out = dot(jnp.concatenate(mine, 0), low, 0, 0).astype(bf16)
        if j & 1:
            outs[-1][j // 2] = out
        else:
            outs[j // 2][...] = out


def out_terms(idx, mixeds, low):
    chunks, count = len(mixeds), len(mixeds[0])
    part, width = mixeds[0][0].shape[2], low.shape[2]
    return pl.pallas_call(
        functools.partial(out_kernel, count, chunks),
        grid_spec=pltpu.PrefetchScalarGridSpec(
            num_scalar_prefetch=1,
            grid=(1,),
            in_specs=[pl.BlockSpec(m.shape, lambda i, s: (0, 0, 0)) for p in mixeds for m in p]
            + [pl.BlockSpec(low.shape, lambda i, s: (0, 0, 0))],
            out_specs=[pl.BlockSpec((part, width), lambda i, s: (0, 0))] * (count // 2)
            + [pl.BlockSpec((count // 2, part, width), lambda i, s: (0, 0, 0))],
        ),
        out_shape=[jax.ShapeDtypeStruct((part, width), bf16)] * (count // 2)
        + [jax.ShapeDtypeStruct((count // 2, part, width), bf16)],
        compiler_params=params(),
        cost_estimate=cost(6),
    )(idx, *[m for p in mixeds for m in p], low)


def input_kernel(count, terms_count, idx_ref, *refs):
    xs = refs[:count]
    dhs = refs[count : 2 * count]
    terms = refs[2 * count : 2 * count + terms_count]
    gain_ref, out_ref = refs[2 * count + terms_count :]
    me = idx_ref[0]
    step, depth, part = xs[0].shape
    rows = GROUP * depth
    back = from_owners(me, rows, depth, depth // count)
    sums = terms[0][0, step * depth :].astype(f32)
    for t in terms[1:]:
        sums = sums + t[0, step * depth :].astype(f32)
    lines = rows // part
    for g in range(step // GROUP):
        f = slice(g * GROUP, (g + 1) * GROUP)
        r = slice(g * rows, (g + 1) * rows)
        resid = place(back, dhs, f)
        pieces = [x[f].reshape(rows, part) for x in xs]
        rms = row_scale(pieces)
        xhat = pieces[0].astype(f32) * rms
        dn = terms[0][0, r].astype(f32)
        for t in terms[1:]:
            dn = dn + t[0, r].astype(f32)
        line = [sums[i : i + 1] for i in range(g * lines, (g + 1) * lines)]
        line = jnp.concatenate(line, 1) if lines > 1 else line[0]
        inner = row_to_column(line) / (part * count)
        out = resid + rms * (dn * gain_ref[me] - xhat * inner)
        out_ref[f] = out.astype(bf16).reshape(GROUP, depth, part)


def input_grad(idx, xs, dhs, terms, gain, chunk, chunks):
    count = len(xs)
    frames, depth, part = xs[0].shape
    local = dhs[0].shape[0]
    frames = frames // chunks
    step = per_step(frames, STEP)
    n = frames // step
    base = chunk * n
    rows = step * depth
    return pl.pallas_call(
        functools.partial(input_kernel, count, len(terms)),
        grid_spec=pltpu.PrefetchScalarGridSpec(
            num_scalar_prefetch=1,
            grid=(n,),
            in_specs=[pl.BlockSpec((step, depth, part), lambda i, s: (i + base, 0, 0))] * count
            + [pl.BlockSpec((local, step, part), lambda i, s: (0, i + base, 0))] * count
            + [pl.BlockSpec((1, rows + EXTRA, part), lambda i, s: (0, i, 0))] * len(terms)
            + [pl.BlockSpec(gain.shape, lambda i, s: (0, 0, 0))],
            out_specs=pl.BlockSpec((step, depth, part), lambda i, s: (i, 0, 0)),
        ),
        out_shape=jax.ShapeDtypeStruct((frames, depth, part), bf16),
        compiler_params=params(),
        cost_estimate=cost(4),
    )(idx, *xs, *dhs, *terms, gain)


def block_kernel(count, idx_ref, *refs):
    up, down, own, hidden_ref, live_ref = refs[:5]
    outs = refs[5:]
    me = idx_ref[0]
    part = outs[0].shape[2]
    branch = up[0].astype(f32) + down[0].astype(f32) + own[0].astype(f32)
    rows = ((hidden_ref[0] + branch) * row_to_column(live_ref[0])).astype(bf16)
    blocks = [rows[:, b * part : (b + 1) * part] for b in range(count)]
    for j in range(count):
        outs[j][0] = pick(blocks, me ^ j)


def block_rows(idx, recv, own, hidden, live, count):
    local, frames, width = hidden.shape
    part = width // count
    each = pl.BlockSpec((1, frames, width), lambda k, s: (k, 0, 0))
    return pl.pallas_call(
        functools.partial(block_kernel, count),
        grid_spec=pltpu.PrefetchScalarGridSpec(
            num_scalar_prefetch=1,
            grid=(local,),
            in_specs=[each] * 4 + [pl.BlockSpec((1, 1, frames), lambda k, s: (k, 0, 0))],
            out_specs=[pl.BlockSpec((1, frames, part), lambda k, s: (k, 0, 0))] * count,
        ),
        out_shape=[jax.ShapeDtypeStruct((local, frames, part), bf16)] * count,
        compiler_params=params(),
        cost_estimate=cost(4),
    )(idx, *recv, own, hidden, live)


def gather_kernel(count, idx_ref, *refs):
    pieces, out_ref = refs[:count], refs[count]
    step, depth, part = out_ref.shape
    back = from_owners(idx_ref[0], GROUP * depth, depth, depth // count)
    for g in range(step // GROUP):
        f = slice(g * GROUP, (g + 1) * GROUP)
        out = place(back, pieces, f)
        out_ref[f] = out.astype(bf16).reshape(GROUP, depth, part)


def gather_block(idx, pieces):
    count = len(pieces)
    local, frames, part = pieces[0].shape
    depth = local * count
    step = per_step(frames, 64)
    return pl.pallas_call(
        functools.partial(gather_kernel, count),
        grid_spec=pltpu.PrefetchScalarGridSpec(
            num_scalar_prefetch=1,
            grid=(frames // step,),
            in_specs=[pl.BlockSpec((local, step, part), lambda i, s: (0, i, 0))] * count,
            out_specs=pl.BlockSpec((step, depth, part), lambda i, s: (i, 0, 0)),
        ),
        out_shape=jax.ShapeDtypeStruct((frames, depth, part), bf16),
        compiler_params=params(),
        cost_estimate=cost(4),
    )(idx, *pieces)


class Order:
    def __init__(self):
        self.last = []

    def tie(self, *values, after=()):
        flat, tree = jax.tree.flatten(values)
        held = [*self.last, *jax.tree.leaves(after)]
        if held:
            flat = lax.optimization_barrier((*flat, *held))[: len(flat)]
        values = jax.tree.unflatten(tree, flat)
        return values[0] if len(values) == 1 else values

    def run(self, kernel, first, *args, after=()):
        out = kernel(self.tie(first, after=after), *args)
        self.last = [min(jax.tree.leaves(out), key=lambda v: v.size)]
        return out

    def fuse(self, step, *args, after=()):
        args = self.tie(*args, after=after)
        out = step(*args) if isinstance(args, tuple) else step(args)
        self.last = jax.tree.leaves(out)
        return out

    def send(self, value, axis, pairs):
        return lax.ppermute(self.tie(value), axis, pairs)

    def swap(self, value, bits, axis="pos"):
        count = lax.axis_size(axis)
        return self.send(value, axis, [(i, i ^ bits) for i in range(count)])

    def exchange(self, pieces):
        back = {j: self.swap(pieces[j], j) for j in range(len(pieces) - 1, 0, -1)}
        return [pieces[0]] + [back[j] for j in range(1, len(pieces))]


def ring_steps(count):
    order = list(range(0, count, 2)) + list(range(count - 1, 0, -2))
    forward = [(order[i], order[(i + 1) % count]) for i in range(count)]
    return forward, [(b, a) for a, b in forward]


class RingGather:
    def __init__(self, order, count, value):
        self.order, self.count = order, count
        self.forward, self.back = ring_steps(count)
        self.blocks = [value] + [None] * (count - 1)

    def step(self, s):
        count, blocks = self.count, self.blocks
        up, down = blocks[s - 1], blocks[(count - s + 1) % count]
        if s == count // 2:
            half = up.shape[0] // 2
            up, down = up[:half], down[half:]
        up = self.order.send(up, "frames", self.forward)
        down = self.order.send(down, "frames", self.back)
        if s < count // 2:
            blocks[s], blocks[count - s] = up, down
        else:
            blocks[s] = (up, down)

    def received(self, s):
        return [self.blocks[s], self.blocks[self.count - s]]


class RingSumWhole:
    def __init__(self, order, count, blocks, idx):
        self.order, self.count, self.blocks, self.idx = order, count, blocks, idx
        self.forward, self.back = ring_steps(count)

    def step(self, s, after=()):
        count, far = self.count, self.count // 2
        if s == 1:
            block = self.blocks[far]
            half = block.shape[0] // 2
            f, b = block[:half], block[half:]
        else:
            h = far - s + 1
            f, b = self.order.run(
                merge_whole, self.idx, self.blocks[count - h], self.blocks[h], *self.parts, after=after
            )
        self.parts = [
            self.order.send(f, "frames", self.forward),
            self.order.send(b, "frames", self.back),
        ]


class RingSum:
    def __init__(self, order, count, blocks, idx):
        self.order, self.count, self.blocks, self.idx = order, count, blocks, idx
        self.forward, self.back = ring_steps(count)
        self.parts = {}

    def step(self, chains, s, after=()):
        count, far = self.count, self.count // 2
        mine = []
        for chain in chains:
            h = far - s + 1 if chain == "x" else far - s
            first, second = (0, 1) if chain == "x" else (1, 0)
            mine += [self.blocks[(count - h) % count][first], self.blocks[h][second]]
        if s > 1:
            moved = [p for chain in chains for p in self.parts[chain]]
            mine = self.order.run(merge, self.idx, mine, moved, after=after)
        for i, chain in enumerate(chains):
            self.parts[chain] = [
                self.order.send(mine[2 * i], "frames", self.forward),
                self.order.send(mine[2 * i + 1], "frames", self.back),
            ]

    def received(self):
        return [self.parts["x"][0], self.parts["y"][0], self.parts["y"][1], self.parts["x"][1]]


CHUNKS = 1


def body(inputs, counts, gain_attn, weight_qkv, weight_out, gain_ffn, weight_ffn, cotangent):
    count = lax.axis_size("pos")
    ring = lax.axis_size("frames")
    far = ring // 2
    me = lax.axis_index("pos")
    idx = me.astype(jnp.int32).reshape(1)
    frames, depth, part = inputs.shape
    width = part * count
    local = depth // count
    half = local // 2
    order = Order()

    positions = jnp.arange(depth, dtype=jnp.int32)
    live = (positions[None, :] < counts[:, None]).astype(f32)
    live_rows = live.reshape(frames // GROUP, 1, GROUP * depth)
    live_own = lax.dynamic_slice_in_dim(live, me * local, local, 1).T.reshape(local, 1, frames)
    w_qkv = weight_qkv.transpose(1, 0, 2).reshape(3, count, part, part)
    w_out = weight_out.reshape(count, part, width)
    gain1 = gain_attn.reshape(count, 1, part)
    gain2 = gain_ffn.reshape(local, 1, width)
    distance = me ^ jnp.arange(count)

    def in_order(blocks):
        return jnp.take(blocks, distance, axis=0, mode="clip")

    cots = order.exchange(order.run(split_cot, idx, cotangent, live_rows, count))
    w_ffn = order.fuse(lambda w: w.transpose(1, 2, 0, 3), weight_ffn)

    def assemble(first, *rest):
        rows = in_order(jnp.stack([first, *rest])).transpose(1, 2, 0, 3)
        return rows.reshape(local, frames, width)

    branch = order.fuse(assemble, *cots)
    grads = RingGather(order, ring, branch)
    grads.step(1)

    xs = {0: inputs}
    bit = count // 2
    while bit:
        for j in list(xs):
            xs[j ^ bit] = order.swap(xs[j], bit)
        bit //= 2
    xs = [xs[j] for j in range(count)]
    grads.step(2)
    qkv, resid, *mixed = order.run(
        attention, idx, xs, w_qkv, gain1, live_rows, 0, 1, after=grads.received(1)
    )
    mixed = order.exchange(mixed)
    grads.step(3)
    hidden, norm = order.run(
        project, idx, [mixed], [resid], w_out, gain2, after=grads.received(2)
    )
    norms = RingGather(order, ring, norm)
    norms.step(1)

    groups = [[0]] + [[s, ring - s] for s in range(1, far)] + [[far]]
    dnorms, branches, acts = [None] * ring, [None] * ring, []

    def feed(s, after=()):
        group = groups[s]
        down, forth, act = order.run(
            ffn,
            idx,
            [norms.blocks[d] for d in group],
            [grads.blocks[d] for d in group],
            w_ffn,
            after=after,
        )
        for i, d in enumerate(group):
            dnorms[d], branches[d] = down[i], forth[i]
        acts.append(act)

    feed(0, after=grads.received(3))
    for s in range(4, far + 1):
        grads.step(s)
    for s in range(2, far + 1):
        norms.step(s)
        feed(s - 1)

    totals = {}

    def weights(row):
        for q in range(0, far + 1, 6):
            chosen = range(q, min(q + 6, far + 1))
            source = (grads if row == 2 else norms).blocks
            totals[q] = order.run(
                weight_grad,
                idx,
                [acts[i] for i in chosen],
                [source[d] for i in chosen for d in groups[i]],
                row,
                totals.get(q),
            )

    dnorm = RingSum(order, ring, dnorms, idx)
    forth = RingSumWhole(order, ring, branches, idx)
    dnorm.step("y", 1)
    feed(far)
    dnorm.step("x", 1)
    for s in range(2, far):
        dnorm.step("y", s)
        dnorm.step("x", s)
    dnorm.step("x", far)
    forth.step(1)

    low, gsum, *rest = order.run(
        resid_grad, idx, dnorm.received(), dnorms[0], hidden, branch, gain2, w_out
    )
    bits = [1 << i for i in range((count - 1).bit_length())]

    dms = order.exchange(rest[:count])
    *stay, going = order.run(out_terms, idx, [mixed], low)
    weights(0)

    def out_sum(stay, moved):
        shape = (2, part // 2, width)
        mine = [v.reshape(shape) for v in stay]
        moved = [moved[i].reshape(shape) for i in range(len(stay))]
        return [v.reshape(part, width) for v in order.run(merge, idx, mine, moved)]

    rows = width // ring

    def pack(out, gsum):
        columns = gsum.reshape(local, ring, rows).transpose(1, 0, 2).reshape(ring, 1, local * rows)
        columns = jnp.pad(columns, ((0, 0), (0, 0), (0, -(local * rows) % width)))
        pieces = [out.reshape(ring, part // ring, width), columns.reshape(ring, -1, width)]
        return jnp.concatenate([p.astype(bf16) for p in pieces], 1)

    forth.step(2, after=dms)
    dhs = order.exchange(rest[count:])
    keep, send, qkv_low, gain_sum = order.run(
        attention_back, idx, xs, dms, qkv, w_qkv, gain1, live_rows, ring
    )
    forth.step(3, after=dhs)
    out_moved = order.swap(going, 1)
    sums = [keep, order.swap(send, 1)]
    outs = out_sum(stay, out_moved)
    for bit in bits[1:]:
        out_moved = order.swap(jnp.stack(outs[1::2]), bit)
        if bit == 2:
            weights(1)
        sums.append(order.swap(order.run(fold, idx, sums, bit), bit))
        outs = out_sum(outs[0::2], out_moved)
    packed = order.fuse(pack, outs[0], gsum)
    packed = lax.all_to_all(packed, "frames", 0, 0, tiled=True)
    for s in range(4, far + 1):
        forth.step(s)
    weights(2)
    block = order.run(block_rows, idx, forth.parts, branches[0], hidden, live_own, count)
    block = order.exchange(block)
    packed = order.fuse(lambda m: jnp.sum(m.astype(f32), axis=0), packed)
    out_low = packed[: part // ring].astype(bf16)
    gain_ffn_grad = packed[part // ring :].reshape(-1)[: local * rows]

    def both(a, b):
        return jnp.concatenate([a, b], 0)

    def unmix(blocks, axis, bits):
        have = [0]
        for bit in bits:
            have = have + [j ^ bit for j in have]
        inverse = jnp.array([have.index(j) for j in range(len(have))])
        places = jnp.take(inverse, lax.axis_index(axis) ^ jnp.arange(len(have)), mode="clip")
        return jnp.take(blocks, places, axis=0, mode="clip")

    def join(a, b, c, d):
        return both(a, c), b + d

    def both_ways(out, gain, axis, bit):
        nearby = order.swap(out, bit, axis), order.swap(gain, bit, axis)
        return order.fuse(join, out, gain, *nearby)

    ring_bits = [1 << i for i in range((ring - 1).bit_length())]
    out_low = out_low[None]
    for i, bit in enumerate(ring_bits):
        nearby = order.swap(out_low, bit, "frames"), order.swap(gain_sum, bit, "frames")
        if i == 0:
            grad_in = order.run(input_grad, idx, xs, dhs, sums, gain1, 0, 1)
        if i == 1:
            block_out = order.run(gather_block, idx, block)
        out_low, gain_sum = order.fuse(join, out_low, gain_sum, *nearby)
    moved = lax.all_to_all(order.tie(qkv_low), "frames", 0, 0, tiled=True)
    out_low = unmix(out_low, "frames", ring_bits)[None]
    for bit in bits[::-1]:
        out_low, gain_sum = both_ways(out_low, gain_sum, "pos", bit)
    qkv_grad = order.fuse(lambda m: jnp.sum(m.astype(f32), axis=0), moved).reshape(3, rows, part)
    out_grad = unmix(out_low, "pos", bits[::-1]).reshape(width, width).astype(f32)
    gain_attn_grad = gain_sum

    ffn_grad = None
    for term in totals.values():
        ffn_grad = term if ffn_grad is None else ffn_grad + term
    return (
        block_out,
        grad_in,
        gain_attn_grad.reshape(width),
        qkv_grad.transpose(1, 0, 2),
        out_grad,
        gain_ffn_grad.reshape(local, rows),
        ffn_grad.transpose(0, 2, 1, 3),
    )


def solution(mesh):
    placed = (
        P("frames", None, "pos"),
        P("frames"),
        P(),
        P(None, None, "pos"),
        P(),
        P("pos", None),
        P("frames", "pos", None, None),
        P("frames", None, "pos"),
    )
    return jax.shard_map(
        body,
        mesh=mesh,
        in_specs=placed,
        out_specs=(
            P("frames", None, "pos"),
            P("frames", None, "pos"),
            P(),
            P("frames", None, "pos"),
            P(),
            P("pos", "frames"),
            P("frames", "pos", None, None),
        ),
        check_vma=False,
    )
```

```python
import functools

import jax
import jax.numpy as jnp
from jax import lax
from jax.experimental import pallas as pl
from jax.experimental.pallas import tpu as pltpu
from jax.sharding import PartitionSpec as P

HEAD_DIM = 64
EPS = 1e-05
MASKED = -1e30
GROUP = 16
STEP = 32
EXTRA = 16
COST = 0.0001
VMEM_LIMIT = 56 * 1024 * 1024

f32 = jnp.float32
bf16 = jnp.bfloat16


def dot(a, b, ca, cb):
    return lax.dot_general(a, b, (((ca,), (cb,)), ((), ())), preferred_element_type=f32)


def cost(us):
    us = us * COST
    return pl.CostEstimate(flops=int(us * 1.15e9), bytes_accessed=int(us * 1e6), transcendentals=0)


def params():
    return pltpu.CompilerParams(vmem_limit_bytes=VMEM_LIMIT)


def to_owners(me, rows, depth, local):
    r = lax.broadcasted_iota(jnp.int32, (rows, rows), 0)
    c = lax.broadcasted_iota(jnp.int32, (rows, rows), 1)
    frames = rows // depth
    k = r // frames
    source = (r % frames) * depth + ((k // local) ^ me) * local + k % local
    return jnp.where(c == source, 1.0, 0.0).astype(bf16)


def from_owners(me, rows, depth, local):
    r = lax.broadcasted_iota(jnp.int32, (rows, rows), 0)
    c = lax.broadcasted_iota(jnp.int32, (rows, rows), 1)
    frames = rows // depth
    k = r % depth
    source = (((k // local) ^ me) * local + k % local) * frames + r // depth
    return jnp.where(c == source, 1.0, 0.0).astype(bf16)


def pick(blocks, index):
    out = blocks[0]
    for b in range(1, len(blocks)):
        out = jnp.where(index == b, blocks[b], out)
    return out


def row_to_column(row):
    n = row.shape[1]
    r = lax.broadcasted_iota(jnp.int32, (n, n), 0)
    c = lax.broadcasted_iota(jnp.int32, (n, n), 1)
    return jnp.sum(jnp.where(r == c, row, 0.0), axis=1, keepdims=True)


def column_to_row(column):
    n = column.shape[0]
    r = lax.broadcasted_iota(jnp.int32, (n, n), 0)
    c = lax.broadcasted_iota(jnp.int32, (n, n), 1)
    return jnp.sum(jnp.where(r == c, column, 0.0), axis=0, keepdims=True)


def pair_mask(live_row, half, depth):
    n = live_row.shape[1] // 2
    live = row_to_column(live_row[:, half * n : (half + 1) * n])
    r = lax.broadcasted_iota(jnp.int32, (n, n), 0)
    c = lax.broadcasted_iota(jnp.int32, (n, n), 1)
    allowed = ((r // depth) == (c // depth)) & (r <= c) & (live > 0.5)
    return jnp.concatenate([allowed, allowed], 1)


def split_heads(block):
    lane = lax.broadcasted_iota(jnp.int32, block.shape, 1)
    zero = jnp.zeros_like(block)
    return jnp.concatenate(
        [jnp.where(lane < HEAD_DIM, block, zero), jnp.where(lane >= HEAD_DIM, block, zero)], 0
    )


def join_heads(pair):
    n = pair.shape[0] // 2
    lane = lax.broadcasted_iota(jnp.int32, (n, pair.shape[1]), 1)
    return jnp.where(lane < HEAD_DIM, pair[:n], pair[n:])


def pair_probs(q2, k2, allowed):
    scores = jnp.where(allowed, dot(k2, q2, 1, 1), MASKED)
    e = jnp.exp(scores - jnp.max(scores, axis=0, keepdims=True))
    return e * (1.0 / jnp.sum(e, axis=0, keepdims=True))


def per_step(frames, step):
    return min(step, frames)


def place(back, pieces, f):
    local, _, part = pieces[0].shape
    blocks = [p[:, f].reshape(local * GROUP, part) for p in pieces]
    return dot(back, jnp.concatenate(blocks, 0), 1, 0)


def row_scale(pieces):
    total = None
    for x in pieces:
        xf = x.astype(f32)
        term = jnp.sum(xf * xf, axis=-1, keepdims=True)
        total = term if total is None else total + term
    return lax.rsqrt(total / (pieces[0].shape[1] * len(pieces)) + EPS)


def cot_kernel(count, idx_ref, cot_ref, live_ref, *outs):
    step, depth, part = cot_ref.shape
    rows = GROUP * depth
    local = depth // count
    move = to_owners(idx_ref[0], rows, depth, local)
    for g in range(step // GROUP):
        f = slice(g * GROUP, (g + 1) * GROUP)
        live = row_to_column(live_ref[g])
        masked = (cot_ref[f].reshape(rows, part).astype(f32) * live).astype(bf16)
        moved = dot(move, masked, 1, 0).astype(bf16).reshape(count, local, GROUP, part)
        for j in range(count):
            outs[j][:, f] = moved[j]


def split_cot(idx, cot, live, count):
    frames, depth, part = cot.shape
    local = depth // count
    step = per_step(frames, 64)
    return pl.pallas_call(
        functools.partial(cot_kernel, count),
        grid_spec=pltpu.PrefetchScalarGridSpec(
            num_scalar_prefetch=1,
            grid=(frames // step,),
            in_specs=[
                pl.BlockSpec((step, depth, part), lambda i, s: (i, 0, 0)),
                pl.BlockSpec((step // GROUP, 1, GROUP * depth), lambda i, s: (i, 0, 0)),
            ],
            out_specs=[pl.BlockSpec((local, step, part), lambda i, s: (0, i, 0))] * count,
        ),
        out_shape=[jax.ShapeDtypeStruct((local, frames, part), bf16)] * count,
        compiler_params=params(),
        cost_estimate=cost(4),
    )(idx, cot, live)


def attn_kernel(count, idx_ref, *refs):
    xs = refs[:count]
    w_ref, gain_ref, live_ref = refs[count : count + 3]
    qkv_ref, resid_ref = refs[count + 3 : count + 5]
    outs = refs[count + 5 :]
    me = idx_ref[0]
    step, depth, part = xs[0].shape
    rows = GROUP * depth
    local = depth // count
    half_rows = rows // 2
    move = to_owners(me, rows, depth, local)
    own = move[: local * GROUP]
    for g in range(step // GROUP):
        f = slice(g * GROUP, (g + 1) * GROUP)
        r = slice(g * rows, (g + 1) * rows)
        pieces = [x[f].reshape(rows, part) for x in xs]
        rms = row_scale(pieces)
        acc = [None] * 3
        for j in range(count):
            normed = (pieces[j].astype(f32) * rms * gain_ref[me ^ j]).astype(bf16)
            for c in range(3):
                term = dot(normed, w_ref[c, me ^ j], 1, 0)
                acc[c] = term if acc[c] is None else acc[c] + term
            moved = dot(own, pieces[j], 1, 0).astype(bf16)
            resid_ref[me ^ j, :, f] = moved.reshape(local, GROUP, part)
        q, k, v = [a.astype(bf16) for a in acc]
        qkv_ref[0, r], qkv_ref[1, r], qkv_ref[2, r] = q, k, v
        q = q * (HEAD_DIM**-0.5)
        mixed = []
        for half in range(2):
            allowed = pair_mask(live_ref[g], half, depth)
            sl = slice(half * half_rows, (half + 1) * half_rows)
            cols = []
            for pair in range(part // 128):
                ln = slice(pair * 128, (pair + 1) * 128)
                probs = pair_probs(split_heads(q[sl, ln]), k[sl, ln], allowed).astype(bf16)
                cols.append(join_heads(dot(probs, v[sl, ln], 0, 0)).astype(bf16))
            mixed.append(jnp.concatenate(cols, 1) if len(cols) > 1 else cols[0])
        mixed = jnp.concatenate(mixed, 0)
        moved = dot(move, mixed, 1, 0).astype(bf16).reshape(count, local, GROUP, part)
        for j in range(count):
            outs[j][:, f] = moved[j]


def attention(idx, xs, w, gain, live, chunk, chunks):
    count = len(xs)
    frames, depth, part = xs[0].shape
    local = depth // count
    frames = frames // chunks
    step = per_step(frames, STEP)
    n = frames // step
    base = chunk * n
    rows = step * depth
    return pl.pallas_call(
        functools.partial(attn_kernel, count),
        grid_spec=pltpu.PrefetchScalarGridSpec(
            num_scalar_prefetch=1,
            grid=(n,),
            in_specs=[pl.BlockSpec((step, depth, part), lambda i, s: (i + base, 0, 0))] * count
            + [
                pl.BlockSpec(w.shape, lambda i, s: (0, 0, 0, 0)),
                pl.BlockSpec(gain.shape, lambda i, s: (0, 0, 0)),
                pl.BlockSpec((step // GROUP, 1, GROUP * depth), lambda i, s: (i + base, 0, 0)),
            ],
            out_specs=[
                pl.BlockSpec((3, rows, part), lambda i, s: (0, i, 0)),
                pl.BlockSpec((count, local, step, part), lambda i, s: (0, 0, i, 0)),
            ]
            + [pl.BlockSpec((local, step, part), lambda i, s: (0, i, 0))] * count,
        ),
        out_shape=[
            jax.ShapeDtypeStruct((3, frames * depth, part), bf16),
            jax.ShapeDtypeStruct((count, local, frames, part), bf16),
        ]
        + [jax.ShapeDtypeStruct((local, frames, part), bf16)] * count,
        compiler_params=params(),
        cost_estimate=cost(8),
    )(idx, *xs, w, gain, live)


def half_specs(local, frames, width):
    half = local // 2
    return [
        pl.BlockSpec((1, frames, width), lambda k, *s: (jnp.minimum(k, half - 1), 0, 0)),
        pl.BlockSpec((1, frames, width), lambda k, *s: (jnp.maximum(k - half, 0), 0, 0)),
    ]


def store_half(is_first, first_ref, second_ref, at, value):
    @pl.when(is_first)
    def _():
        first_ref[at] = value

    @pl.when(jnp.logical_not(is_first))
    def _():
        second_ref[at] = value


def load_half(is_first, first_ref, second_ref):
    return jnp.where(is_first, first_ref[0], second_ref[0])


def project_kernel(count, chunks, idx_ref, *refs):
    mixed = refs[: count * chunks]
    resids = refs[count * chunks : (count + 1) * chunks]
    w_ref, gain_ref, hidden_ref, norm_ref = refs[(count + 1) * chunks :]
    me = idx_ref[0]
    size = mixed[0].shape[1]
    for c in range(chunks):
        f = slice(c * size, (c + 1) * size)
        hidden = jnp.concatenate([resids[c][b, 0] for b in range(count)], 1).astype(f32)
        for j in range(count):
            hidden = hidden + dot(mixed[c * count + j][0], w_ref[me ^ j], 1, 0)
        hidden_ref[0, f] = hidden
        rms = lax.rsqrt(jnp.mean(hidden * hidden, axis=-1, keepdims=True) + EPS)
        norm_ref[0, f] = (hidden * rms * gain_ref[0]).astype(bf16)


def project(idx, mixed, resids, w, gain):
    chunks, count = len(mixed), len(mixed[0])
    local, size, part = mixed[0][0].shape
    frames, width = size * chunks, part * count
    each = pl.BlockSpec((1, frames, width), lambda k, s: (k, 0, 0))
    return pl.pallas_call(
        functools.partial(project_kernel, count, chunks),
        grid_spec=pltpu.PrefetchScalarGridSpec(
            num_scalar_prefetch=1,
            grid=(local,),
            in_specs=[pl.BlockSpec((1, size, part), lambda k, s: (k, 0, 0))] * (count * chunks)
            + [pl.BlockSpec((count, 1, size, part), lambda k, s: (0, k, 0, 0))] * chunks
            + [
                pl.BlockSpec(w.shape, lambda k, s: (0, 0, 0)),
                pl.BlockSpec((1, 1, width), lambda k, s: (k, 0, 0)),
            ],
            out_specs=[each, each],
        ),
        out_shape=[
            jax.ShapeDtypeStruct((local, frames, width), f32),
            jax.ShapeDtypeStruct((local, frames, width), bf16),
        ],
        compiler_params=params(),
        cost_estimate=cost(6),
    )(idx, *[m for part_ in mixed for m in part_], *resids, w, gain)


def load_block(is_first, refs):
    return refs[0][0] if len(refs) == 1 else load_half(is_first, *refs)


def block_parts(block):
    return list(block) if isinstance(block, tuple) else [block]


def ffn_kernel(sizes, idx_ref, *refs):
    n = len(sizes) // 2
    ins = sum(sizes)
    w_ref = refs[ins]
    dnorms, branches = refs[ins + 1 : ins + 1 + 2 * n], refs[ins + 1 + 2 * n : ins + 1 + 3 * n]
    act_ref = refs[-1]
    is_first = pl.program_id(0) < pl.num_programs(0) // 2
    blocks, at = [], 0
    for size in sizes:
        blocks.append(load_block(is_first, refs[at : at + size]))
        at += size
    frames = blocks[0].shape[0]
    norm = jnp.concatenate(blocks[:n], 0)
    grad = jnp.concatenate(blocks[n:], 0)
    gate = dot(norm, w_ref[0, 0], 1, 1)
    up = dot(norm, w_ref[0, 1], 1, 1)
    dact = dot(grad, w_ref[0, 2], 1, 1)
    sig = jax.nn.sigmoid(gate)
    silu = gate * sig
    act = (silu * up).astype(bf16)
    dgate = (dact * up * sig * (1.0 + gate * (1.0 - sig))).astype(bf16)
    dup = (dact * silu).astype(bf16)
    act_ref[0, 0] = dgate
    act_ref[0, 1] = dup
    act_ref[0, 2] = act
    dnorm = (dot(dgate, w_ref[0, 0], 1, 0) + dot(dup, w_ref[0, 1], 1, 0)).astype(bf16)
    branch = dot(act, w_ref[0, 2], 1, 0).astype(bf16)
    for i in range(n):
        rows = slice(i * frames, (i + 1) * frames)
        store_half(is_first, *dnorms[2 * i : 2 * i + 2], 0, dnorm[rows])
        branches[i][0] = branch[rows]


def ffn(idx, norms, grads, w):
    n = len(norms)
    blocks = [block_parts(v) for v in (*norms, *grads)]
    local, _, hidden, width = w.shape
    frames = blocks[0][0].shape[1]
    halves = half_specs(local, frames, width)
    whole = [pl.BlockSpec((1, frames, width), lambda k, s: (k, 0, 0))]
    *out, act = pl.pallas_call(
        functools.partial(ffn_kernel, [len(v) for v in blocks]),
        grid_spec=pltpu.PrefetchScalarGridSpec(
            num_scalar_prefetch=1,
            grid=(local,),
            in_specs=[x for v in blocks for x in (whole if len(v) == 1 else halves)]
            + [pl.BlockSpec((1, 3, hidden, width), lambda k, s: (k, 0, 0, 0))],
            out_specs=halves * n
            + whole * n
            + [pl.BlockSpec((1, 3, n * frames, hidden), lambda k, s: (k, 0, 0, 0))],
        ),
        out_shape=[jax.ShapeDtypeStruct((local // 2, frames, width), bf16)] * (2 * n)
        + [jax.ShapeDtypeStruct((local, frames, width), bf16)] * n
        + [jax.ShapeDtypeStruct((local, 3, n * frames, hidden), bf16)],
        compiler_params=params(),
        cost_estimate=cost(3.5 + 5 * n),
    )(idx, *[x for v in blocks for x in v], w)
    pairs = [out[i : i + 2] for i in range(0, 2 * n, 2)]
    return pairs, out[2 * n :], act


def weight_kernel(n, row, sizes, idx_ref, *refs):
    acts, out_ref = refs[:n], refs[-1]
    local = acts[0].shape[0]
    others, at = [], n
    for size in sizes:
        others.append(refs[at : at + size])
        at += size
    frames = others[0][0].shape[1]

    def entry(block, k):
        return block[k // block[0].shape[0]][k % block[0].shape[0]]

    for k in range(local):
        total, first = None, 0
        for a in acts:
            size = a.shape[2] // frames
            both = [entry(others[first + i], k) for i in range(size)]
            first += size
            both = jnp.concatenate(both, 0) if size > 1 else both[0]
            term = dot(a[k, 0], both, 0, 0)
            total = term if total is None else total + term
        out_ref[:, 0, k] = total


def weight_grad(idx, acts, others, row, out):
    n = len(acts)
    local, _, _, hidden = acts[0].shape
    chunk = min(128, hidden)
    others = [block_parts(v) for v in others]
    width = others[0][0].shape[2]
    ins = list(acts) + [x for v in others for x in v]
    specs = [
        pl.BlockSpec((local, 1, a.shape[2], chunk), lambda c, s: (0, row, 0, c)) for a in acts
    ] + [
        pl.BlockSpec(x.shape, lambda c, s: (0, 0, 0), pipeline_mode=pl.Buffered(1))
        for v in others
        for x in v
    ]
    aliases = {}
    kernel = functools.partial(weight_kernel, n, row, [len(v) for v in others])
    if out is not None:
        aliases = {1 + len(ins): 0}
        ins.append(out)
        specs.append(pl.BlockSpec(memory_space=pl.ANY))
    return pl.pallas_call(
        kernel,
        grid_spec=pltpu.PrefetchScalarGridSpec(
            num_scalar_prefetch=1,
            grid=(hidden // chunk,),
            in_specs=specs,
            out_specs=pl.BlockSpec((chunk, 1, local, width), lambda c, s: (c, row, 0, 0)),
        ),
        out_shape=jax.ShapeDtypeStruct((hidden, 3, local, width), f32),
        input_output_aliases=aliases,
        compiler_params=params(),
        cost_estimate=cost(12),
    )(idx, *ins)


def add_low(x, y):
    return (x.astype(f32) + y.astype(f32)).astype(bf16)


def merge_kernel(n, idx_ref, *refs):
    for i in range(n):
        refs[2 * n + i][...] = add_low(refs[i][...], refs[n + i][...])


def merge(idx, mine, moved):
    n = len(mine)
    half, frames, width = mine[0].shape
    each = pl.BlockSpec((1, frames, width), lambda k, s: (k, 0, 0))
    return pl.pallas_call(
        functools.partial(merge_kernel, n),
        grid_spec=pltpu.PrefetchScalarGridSpec(
            num_scalar_prefetch=1,
            grid=(half,),
            in_specs=[each] * (2 * n),
            out_specs=[each] * n,
        ),
        out_shape=[jax.ShapeDtypeStruct(mine[0].shape, bf16)] * n,
        compiler_params=params(),
        cost_estimate=cost(1.2 * n),
    )(idx, *mine, *moved)


def whole_kernel(half, idx_ref, f_ref, b_ref, up_ref, down_ref, fo_ref, bo_ref):
    if half is None:
        fo_ref[...] = add_low(f_ref[...], up_ref[...])
        bo_ref[...] = add_low(b_ref[...], down_ref[...])
        return
    is_first = pl.program_id(0) < half
    fo_ref[...] = jnp.where(is_first, add_low(f_ref[...], up_ref[...]), f_ref[...])
    bo_ref[...] = jnp.where(is_first, b_ref[...], add_low(b_ref[...], down_ref[...]))


def merge_whole(idx, f, b, up, down):
    local, frames, width = f.shape
    half = None if up.shape == f.shape else local // 2
    each = pl.BlockSpec((1, frames, width), lambda k, s: (k, 0, 0))
    moved = half_specs(local, frames, width) if half else [each] * 2
    return pl.pallas_call(
        functools.partial(whole_kernel, half),
        grid_spec=pltpu.PrefetchScalarGridSpec(
            num_scalar_prefetch=1,
            grid=(local,),
            in_specs=[each, each, *moved],
            out_specs=[each, each],
        ),
        out_shape=[jax.ShapeDtypeStruct(f.shape, bf16)] * 2,
        compiler_params=params(),
        cost_estimate=cost(4),
    )(idx, f, b, up, down)


def sum_halves(refs):
    is_first = pl.program_id(0) < pl.num_programs(0) // 2
    total = None
    for i in range(0, len(refs), 2):
        term = load_half(is_first, *refs[i : i + 2]).astype(f32)
        total = term if total is None else total + term
    return total


def resid_kernel(count, idx_ref, *refs):
    hidden_ref, branch_ref, gain_ref, w_ref, low_ref, gsum_ref = refs[6:12]
    dms, dhs = refs[12 : 12 + count], refs[12 + count :]
    me = idx_ref[0]
    part = w_ref.shape[1]
    dnorm = sum_halves(refs[:6])
    hidden = hidden_ref[0]
    rms = lax.rsqrt(jnp.mean(hidden * hidden, axis=-1, keepdims=True) + EPS)
    xhat = hidden * rms
    gsum_ref[0] = jnp.sum(dnorm * xhat, axis=0, keepdims=True)
    u = dnorm * gain_ref[0]
    inner = jnp.mean(xhat * u, axis=-1, keepdims=True)
    low = (branch_ref[0].astype(f32) + rms * (u - xhat * inner)).astype(bf16)
    low_ref[0] = low
    blocks = [low[:, b * part : (b + 1) * part] for b in range(count)]
    for j in range(count):
        dhs[j][0] = pick(blocks, me ^ j)
        dms[j][0] = dot(low, w_ref[me ^ j], 1, 1).astype(bf16)


def resid_grad(idx, recv, own, hidden, branch, gain, w):
    count, part, width = w.shape
    local, frames, _ = hidden.shape
    each = pl.BlockSpec((1, frames, width), lambda k, s: (k, 0, 0))
    return pl.pallas_call(
        functools.partial(resid_kernel, count),
        grid_spec=pltpu.PrefetchScalarGridSpec(
            num_scalar_prefetch=1,
            grid=(local,),
            in_specs=half_specs(local, frames, width) * 3
            + [each] * 2
            + [
                pl.BlockSpec((1, 1, width), lambda k, s: (k, 0, 0)),
                pl.BlockSpec(w.shape, lambda k, s: (0, 0, 0)),
            ],
            out_specs=[each, pl.BlockSpec((1, 1, width), lambda k, s: (k, 0, 0))]
            + [pl.BlockSpec((1, frames, part), lambda k, s: (k, 0, 0))] * (2 * count),
        ),
        out_shape=[
            jax.ShapeDtypeStruct((local, frames, width), bf16),
            jax.ShapeDtypeStruct((local, 1, width), f32),
        ]
        + [jax.ShapeDtypeStruct((local, frames, part), bf16)] * (2 * count),
        compiler_params=params(),
        cost_estimate=cost(8),
    )(idx, *recv, *own, hidden, branch, gain, w)


def attn_back_kernel(count, ring, idx_ref, *refs):
    xs = refs[:count]
    dms = refs[count : 2 * count]
    qkv_ref, w_ref, gain_ref, live_ref = refs[2 * count : 2 * count + 4]
    keep_ref, send_ref, wlow_ref, gsum_ref, wsum_ref = refs[2 * count + 4 :]
    me = idx_ref[0]
    step, depth, part = xs[0].shape
    rows = GROUP * depth
    back = from_owners(me, rows, depth, depth // count)
    half_rows = rows // 2
    factor = HEAD_DIM**-0.5

    @pl.when(pl.program_id(0) == 0)
    def _():
        wsum_ref[...] = jnp.zeros_like(wsum_ref)
        gsum_ref[...] = jnp.zeros_like(gsum_ref)

    every, rmss = [[], [], []], []
    for g in range(step // GROUP):
        f = slice(g * GROUP, (g + 1) * GROUP)
        r = slice(g * rows, (g + 1) * rows)
        dmixed = place(back, dms, f).astype(bf16)
        q, k, v = qkv_ref[0, r] * factor, qkv_ref[1, r], qkv_ref[2, r]
        for half in range(2):
            allowed = pair_mask(live_ref[g], half, depth)
            sl = slice(half * half_rows, (half + 1) * half_rows)
            cols = [[], [], []]
            for pair in range(part // 128):
                ln = slice(pair * 128, (pair + 1) * 128)
                q2, k2, v2 = split_heads(q[sl, ln]), k[sl, ln], v[sl, ln]
                dm2 = split_heads(dmixed[sl, ln])
                probs = pair_probs(q2, k2, allowed)
                dprobs = dot(v2, dm2, 1, 1)
                inner = jnp.sum(probs * dprobs, axis=0, keepdims=True)
                ds = (probs * (dprobs - inner)).astype(bf16)
                cols[0].append((join_heads(dot(ds, k2, 0, 0)) * factor).astype(bf16))
                cols[1].append(dot(ds, q2, 1, 0).astype(bf16))
                cols[2].append(dot(probs.astype(bf16), dm2, 1, 0).astype(bf16))
            for c in range(3):
                every[c].append(jnp.concatenate(cols[c], 1) if len(cols[c]) > 1 else cols[c][0])
    dqkv = [jnp.concatenate(p, 0) for p in every]
    rows = step * depth
    pieces = [x[...].reshape(rows, part) for x in xs]
    rms = row_scale(pieces)
    inner = jnp.zeros((rows, 1), f32)
    for j in range(count):
        owner = me ^ j
        xhat = pieces[j].astype(f32) * rms
        scaled = xhat * gain_ref[owner]
        normed = scaled.astype(bf16)
        dn = jnp.zeros((rows, part), f32)
        for c in range(3):
            dn = dn + dot(dqkv[c], w_ref[c, owner], 1, 1)
            wsum_ref[c, owner] += dot(normed, dqkv[c], 0, 0)
        inner = inner + jnp.sum(scaled * dn, axis=-1, keepdims=True)
        gsum_ref[owner] += jnp.sum(dn * xhat, axis=0, keepdims=True)
        (send_ref if j & 1 else keep_ref)[j // 2, :rows] = dn.astype(bf16)
    size = GROUP * depth
    lines = [column_to_row(inner[g * size : (g + 1) * size]) for g in range(step // GROUP)]
    lines = [line[:, i : i + part] for line in lines for i in range(0, size, part)]
    lines.append(jnp.zeros((EXTRA - len(lines), part), f32))
    lines = jnp.concatenate(lines, 0).astype(bf16)
    for i in range(count // 2):
        send_ref[i, rows:] = lines
        keep_ref[i, rows:] = lines

    @pl.when(pl.program_id(0) == pl.num_programs(0) - 1)
    def _():
        size = part * count // ring
        for i in range(ring):
            block, line = i * size // part, i * size % part
            for c in range(3):
                wlow_ref[i, c * size : (c + 1) * size] = wsum_ref[
                    c, block, line : line + size
                ].astype(bf16)


def attention_back(idx, xs, dms, qkv, w, gain, live, ring):
    count = len(xs)
    frames, depth, part = xs[0].shape
    local = dms[0].shape[0]
    step = per_step(frames, STEP)
    n = frames // step
    rows = step * depth
    low_shape = (ring, 3 * part * count // ring, part)
    lives = pl.BlockSpec((step // GROUP, 1, GROUP * depth), lambda i, s: (i, 0, 0))
    return pl.pallas_call(
        functools.partial(attn_back_kernel, count, ring),
        grid_spec=pltpu.PrefetchScalarGridSpec(
            num_scalar_prefetch=1,
            grid=(n,),
            in_specs=[pl.BlockSpec((step, depth, part), lambda i, s: (i, 0, 0))] * count
            + [pl.BlockSpec((local, step, part), lambda i, s: (0, i, 0))] * count
            + [
                pl.BlockSpec((3, rows, part), lambda i, s: (0, i, 0)),
                pl.BlockSpec(w.shape, lambda i, s: (0, 0, 0, 0)),
                pl.BlockSpec(gain.shape, lambda i, s: (0, 0, 0)),
                lives,
            ],
            out_specs=[pl.BlockSpec((count // 2, rows + EXTRA, part), lambda i, s: (0, i, 0))] * 2
            + [
                pl.BlockSpec(low_shape, lambda i, s: (0, 0, 0)),
                pl.BlockSpec((count, 1, part), lambda i, s: (0, 0, 0)),
            ],
            scratch_shapes=[pltpu.VMEM(w.shape, f32)],
        ),
        out_shape=[jax.ShapeDtypeStruct((count // 2, n * (rows + EXTRA), part), bf16)] * 2
        + [
            jax.ShapeDtypeStruct(low_shape, bf16),
            jax.ShapeDtypeStruct((count, 1, part), f32),
        ],
        compiler_params=params(),
        cost_estimate=cost(26),
    )(idx, *xs, *dms, qkv, w, gain, live)


def fold_kernel(n, idx_ref, *refs):
    total = refs[0][...].astype(f32)
    for r in refs[1:n]:
        total = total + r[...].astype(f32)
    refs[n][...] = total.astype(bf16)


def fold(idx, terms, bit):
    n = len(terms)
    _, rows, part = terms[0].shape
    hop = bit // 2

    def spec(i):
        step = 1 if i < 2 else 1 << (i - 1)
        return pl.BlockSpec((1, rows, part), lambda g, s: (hop * (2 * g + 1) // step, 0, 0))

    return pl.pallas_call(
        functools.partial(fold_kernel, n),
        grid_spec=pltpu.PrefetchScalarGridSpec(
            num_scalar_prefetch=1,
            grid=(terms[0].shape[0] // bit,),
            in_specs=[spec(i) for i in range(n)],
            out_specs=pl.BlockSpec((1, rows, part), lambda g, s: (g, 0, 0)),
        ),
        out_shape=jax.ShapeDtypeStruct((terms[0].shape[0] // bit, rows, part), bf16),
        compiler_params=params(),
        cost_estimate=cost(2),
    )(idx, *terms)


def out_kernel(count, chunks, idx_ref, *refs):
    low_ref, outs = refs[count * chunks], refs[count * chunks + 1 :]
    local, size, _ = refs[0].shape
    width = low_ref.shape[2]
    lows = []
    for c in range(chunks):
        part_ = low_ref[:, c * size : (c + 1) * size]
        lows.append(part_.reshape(local * size, width))
    low = jnp.concatenate(lows, 0)
    for j in range(count):
        mine = [refs[c * count + j][...].reshape(local * size, -1) for c in range(chunks)]
        out = dot(jnp.concatenate(mine, 0), low, 0, 0).astype(bf16)
        if j & 1:
            outs[-1][j // 2] = out
        else:
            outs[j // 2][...] = out


def out_terms(idx, mixeds, low):
    chunks, count = len(mixeds), len(mixeds[0])
    part, width = mixeds[0][0].shape[2], low.shape[2]
    return pl.pallas_call(
        functools.partial(out_kernel, count, chunks),
        grid_spec=pltpu.PrefetchScalarGridSpec(
            num_scalar_prefetch=1,
            grid=(1,),
            in_specs=[pl.BlockSpec(m.shape, lambda i, s: (0, 0, 0)) for p in mixeds for m in p]
            + [pl.BlockSpec(low.shape, lambda i, s: (0, 0, 0))],
            out_specs=[pl.BlockSpec((part, width), lambda i, s: (0, 0))] * (count // 2)
            + [pl.BlockSpec((count // 2, part, width), lambda i, s: (0, 0, 0))],
        ),
        out_shape=[jax.ShapeDtypeStruct((part, width), bf16)] * (count // 2)
        + [jax.ShapeDtypeStruct((count // 2, part, width), bf16)],
        compiler_params=params(),
        cost_estimate=cost(6),
    )(idx, *[m for p in mixeds for m in p], low)


def input_kernel(count, terms_count, idx_ref, *refs):
    xs = refs[:count]
    dhs = refs[count : 2 * count]
    terms = refs[2 * count : 2 * count + terms_count]
    gain_ref, out_ref = refs[2 * count + terms_count :]
    me = idx_ref[0]
    step, depth, part = xs[0].shape
    rows = GROUP * depth
    back = from_owners(me, rows, depth, depth // count)
    sums = terms[0][0, step * depth :].astype(f32)
    for t in terms[1:]:
        sums = sums + t[0, step * depth :].astype(f32)
    lines = rows // part
    for g in range(step // GROUP):
        f = slice(g * GROUP, (g + 1) * GROUP)
        r = slice(g * rows, (g + 1) * rows)
        resid = place(back, dhs, f)
        pieces = [x[f].reshape(rows, part) for x in xs]
        rms = row_scale(pieces)
        xhat = pieces[0].astype(f32) * rms
        dn = terms[0][0, r].astype(f32)
        for t in terms[1:]:
            dn = dn + t[0, r].astype(f32)
        line = [sums[i : i + 1] for i in range(g * lines, (g + 1) * lines)]
        line = jnp.concatenate(line, 1) if lines > 1 else line[0]
        inner = row_to_column(line) / (part * count)
        out = resid + rms * (dn * gain_ref[me] - xhat * inner)
        out_ref[f] = out.astype(bf16).reshape(GROUP, depth, part)


def input_grad(idx, xs, dhs, terms, gain, chunk, chunks):
    count = len(xs)
    frames, depth, part = xs[0].shape
    local = dhs[0].shape[0]
    frames = frames // chunks
    step = per_step(frames, STEP)
    n = frames // step
    base = chunk * n
    rows = step * depth
    return pl.pallas_call(
        functools.partial(input_kernel, count, len(terms)),
        grid_spec=pltpu.PrefetchScalarGridSpec(
            num_scalar_prefetch=1,
            grid=(n,),
            in_specs=[pl.BlockSpec((step, depth, part), lambda i, s: (i + base, 0, 0))] * count
            + [pl.BlockSpec((local, step, part), lambda i, s: (0, i + base, 0))] * count
            + [pl.BlockSpec((1, rows + EXTRA, part), lambda i, s: (0, i, 0))] * len(terms)
            + [pl.BlockSpec(gain.shape, lambda i, s: (0, 0, 0))],
            out_specs=pl.BlockSpec((step, depth, part), lambda i, s: (i, 0, 0)),
        ),
        out_shape=jax.ShapeDtypeStruct((frames, depth, part), bf16),
        compiler_params=params(),
        cost_estimate=cost(4),
    )(idx, *xs, *dhs, *terms, gain)


def block_kernel(count, idx_ref, *refs):
    up, down, own, hidden_ref, live_ref = refs[:5]
    outs = refs[5:]
    me = idx_ref[0]
    part = outs[0].shape[2]
    branch = up[0].astype(f32) + down[0].astype(f32) + own[0].astype(f32)
    rows = ((hidden_ref[0] + branch) * row_to_column(live_ref[0])).astype(bf16)
    blocks = [rows[:, b * part : (b + 1) * part] for b in range(count)]
    for j in range(count):
        outs[j][0] = pick(blocks, me ^ j)


def block_rows(idx, recv, own, hidden, live, count):
    local, frames, width = hidden.shape
    part = width // count
    each = pl.BlockSpec((1, frames, width), lambda k, s: (k, 0, 0))
    return pl.pallas_call(
        functools.partial(block_kernel, count),
        grid_spec=pltpu.PrefetchScalarGridSpec(
            num_scalar_prefetch=1,
            grid=(local,),
            in_specs=[each] * 4 + [pl.BlockSpec((1, 1, frames), lambda k, s: (k, 0, 0))],
            out_specs=[pl.BlockSpec((1, frames, part), lambda k, s: (k, 0, 0))] * count,
        ),
        out_shape=[jax.ShapeDtypeStruct((local, frames, part), bf16)] * count,
        compiler_params=params(),
        cost_estimate=cost(4),
    )(idx, *recv, own, hidden, live)


def gather_kernel(count, idx_ref, *refs):
    pieces, out_ref = refs[:count], refs[count]
    step, depth, part = out_ref.shape
    back = from_owners(idx_ref[0], GROUP * depth, depth, depth // count)
    for g in range(step // GROUP):
        f = slice(g * GROUP, (g + 1) * GROUP)
        out = place(back, pieces, f)
        out_ref[f] = out.astype(bf16).reshape(GROUP, depth, part)


def gather_block(idx, pieces):
    count = len(pieces)
    local, frames, part = pieces[0].shape
    depth = local * count
    step = per_step(frames, 64)
    return pl.pallas_call(
        functools.partial(gather_kernel, count),
        grid_spec=pltpu.PrefetchScalarGridSpec(
            num_scalar_prefetch=1,
            grid=(frames // step,),
            in_specs=[pl.BlockSpec((local, step, part), lambda i, s: (0, i, 0))] * count,
            out_specs=pl.BlockSpec((step, depth, part), lambda i, s: (i, 0, 0)),
        ),
        out_shape=jax.ShapeDtypeStruct((frames, depth, part), bf16),
        compiler_params=params(),
        cost_estimate=cost(4),
    )(idx, *pieces)


class Order:
    def __init__(self):
        self.last = []

    def tie(self, *values, after=()):
        flat, tree = jax.tree.flatten(values)
        held = [*self.last, *jax.tree.leaves(after)]
        if held:
            flat = lax.optimization_barrier((*flat, *held))[: len(flat)]
        values = jax.tree.unflatten(tree, flat)
        return values[0] if len(values) == 1 else values

    def run(self, kernel, first, *args, after=()):
        out = kernel(self.tie(first, after=after), *args)
        self.last = [min(jax.tree.leaves(out), key=lambda v: v.size)]
        return out

    def fuse(self, step, *args, after=()):
        args = self.tie(*args, after=after)
        out = step(*args) if isinstance(args, tuple) else step(args)
        self.last = jax.tree.leaves(out)
        return out

    def send(self, value, axis, pairs):
        return lax.ppermute(self.tie(value), axis, pairs)

    def swap(self, value, bits, axis="pos"):
        count = lax.axis_size(axis)
        return self.send(value, axis, [(i, i ^ bits) for i in range(count)])

    def exchange(self, pieces):
        back = {j: self.swap(pieces[j], j) for j in range(len(pieces) - 1, 0, -1)}
        return [pieces[0]] + [back[j] for j in range(1, len(pieces))]


def ring_steps(count):
    order = list(range(0, count, 2)) + list(range(count - 1, 0, -2))
    forward = [(order[i], order[(i + 1) % count]) for i in range(count)]
    return forward, [(b, a) for a, b in forward]


class RingGather:
    def __init__(self, order, count, value):
        self.order, self.count = order, count
        self.forward, self.back = ring_steps(count)
        self.blocks = [value] + [None] * (count - 1)

    def step(self, s):
        count, blocks = self.count, self.blocks
        up, down = blocks[s - 1], blocks[(count - s + 1) % count]
        if s == count // 2:
            half = up.shape[0] // 2
            up, down = up[:half], down[half:]
        up = self.order.send(up, "frames", self.forward)
        down = self.order.send(down, "frames", self.back)
        if s < count // 2:
            blocks[s], blocks[count - s] = up, down
        else:
            blocks[s] = (up, down)

    def received(self, s):
        return [self.blocks[s], self.blocks[self.count - s]]


class RingSumWhole:
    def __init__(self, order, count, blocks, idx):
        self.order, self.count, self.blocks, self.idx = order, count, blocks, idx
        self.forward, self.back = ring_steps(count)

    def step(self, s, after=()):
        count, far = self.count, self.count // 2
        if s == 1:
            block = self.blocks[far]
            half = block.shape[0] // 2
            f, b = block[:half], block[half:]
        else:
            h = far - s + 1
            f, b = self.order.run(
                merge_whole, self.idx, self.blocks[count - h], self.blocks[h], *self.parts, after=after
            )
        self.parts = [
            self.order.send(f, "frames", self.forward),
            self.order.send(b, "frames", self.back),
        ]


class RingSum:
    def __init__(self, order, count, blocks, idx):
        self.order, self.count, self.blocks, self.idx = order, count, blocks, idx
        self.forward, self.back = ring_steps(count)
        self.parts = {}

    def step(self, chains, s, after=()):
        count, far = self.count, self.count // 2
        mine = []
        for chain in chains:
            h = far - s + 1 if chain == "x" else far - s
            first, second = (0, 1) if chain == "x" else (1, 0)
            mine += [self.blocks[(count - h) % count][first], self.blocks[h][second]]
        if s > 1:
            moved = [p for chain in chains for p in self.parts[chain]]
            mine = self.order.run(merge, self.idx, mine, moved, after=after)
        for i, chain in enumerate(chains):
            self.parts[chain] = [
                self.order.send(mine[2 * i], "frames", self.forward),
                self.order.send(mine[2 * i + 1], "frames", self.back),
            ]

    def received(self):
        return [self.parts["x"][0], self.parts["y"][0], self.parts["y"][1], self.parts["x"][1]]


CHUNKS = 1


def body(inputs, counts, gain_attn, weight_qkv, weight_out, gain_ffn, weight_ffn, cotangent):
    count = lax.axis_size("pos")
    ring = lax.axis_size("frames")
    far = ring // 2
    me = lax.axis_index("pos")
    idx = me.astype(jnp.int32).reshape(1)
    frames, depth, part = inputs.shape
    width = part * count
    local = depth // count
    half = local // 2
    order = Order()

    positions = jnp.arange(depth, dtype=jnp.int32)
    live = (positions[None, :] < counts[:, None]).astype(f32)
    live_rows = live.reshape(frames // GROUP, 1, GROUP * depth)
    live_own = lax.dynamic_slice_in_dim(live, me * local, local, 1).T.reshape(local, 1, frames)
    w_qkv = weight_qkv.transpose(1, 0, 2).reshape(3, count, part, part)
    w_out = weight_out.reshape(count, part, width)
    gain1 = gain_attn.reshape(count, 1, part)
    gain2 = gain_ffn.reshape(local, 1, width)
    distance = me ^ jnp.arange(count)

    def in_order(blocks):
        return jnp.take(blocks, distance, axis=0, mode="clip")

    cots = order.exchange(order.run(split_cot, idx, cotangent, live_rows, count))
    w_ffn = order.fuse(lambda w: w.transpose(1, 2, 0, 3), weight_ffn)

    def assemble(first, *rest):
        rows = in_order(jnp.stack([first, *rest])).transpose(1, 2, 0, 3)
        return rows.reshape(local, frames, width)

    branch = order.fuse(assemble, *cots)
    grads = RingGather(order, ring, branch)
    grads.step(1)

    xs = {0: inputs}
    bit = count // 2
    while bit:
        for j in list(xs):
            xs[j ^ bit] = order.swap(xs[j], bit)
        bit //= 2
    xs = [xs[j] for j in range(count)]
    grads.step(2)
    qkv, resid, *mixed = order.run(
        attention, idx, xs, w_qkv, gain1, live_rows, 0, 1, after=grads.received(1)
    )
    mixed = order.exchange(mixed)
    grads.step(3)
    hidden, norm = order.run(
        project, idx, [mixed], [resid], w_out, gain2, after=grads.received(2)
    )
    norms = RingGather(order, ring, norm)
    norms.step(1)

    groups = [[0]] + [[s, ring - s] for s in range(1, far)] + [[far]]
    dnorms, branches, acts = [None] * ring, [None] * ring, []

    def feed(s, after=()):
        group = groups[s]
        down, forth, act = order.run(
            ffn,
            idx,
            [norms.blocks[d] for d in group],
            [grads.blocks[d] for d in group],
            w_ffn,
            after=after,
        )
        for i, d in enumerate(group):
            dnorms[d], branches[d] = down[i], forth[i]
        acts.append(act)

    feed(0, after=grads.received(3))
    for s in range(4, far + 1):
        grads.step(s)
    for s in range(2, far + 1):
        norms.step(s)
        feed(s - 1)

    totals = {}

    def weights(row):
        for q in range(0, far + 1, 6):
            chosen = range(q, min(q + 6, far + 1))
            source = (grads if row == 2 else norms).blocks
            totals[q] = order.run(
                weight_grad,
                idx,
                [acts[i] for i in chosen],
                [source[d] for i in chosen for d in groups[i]],
                row,
                totals.get(q),
            )

    dnorm = RingSum(order, ring, dnorms, idx)
    forth = RingSumWhole(order, ring, branches, idx)
    dnorm.step("y", 1)
    feed(far)
    dnorm.step("x", 1)
    for s in range(2, far):
        dnorm.step("y", s)
        dnorm.step("x", s)
    dnorm.step("x", far)
    forth.step(1)

    low, gsum, *rest = order.run(
        resid_grad, idx, dnorm.received(), dnorms[0], hidden, branch, gain2, w_out
    )
    bits = [1 << i for i in range((count - 1).bit_length())]

    dms = order.exchange(rest[:count])
    *stay, going = order.run(out_terms, idx, [mixed], low)
    weights(0)

    def out_sum(stay, moved):
        shape = (2, part // 2, width)
        mine = [v.reshape(shape) for v in stay]
        moved = [moved[i].reshape(shape) for i in range(len(stay))]
        return [v.reshape(part, width) for v in order.run(merge, idx, mine, moved)]

    rows = width // ring

    def pack(out, gsum):
        columns = gsum.reshape(local, ring, rows).transpose(1, 0, 2).reshape(ring, 1, local * rows)
        columns = jnp.pad(columns, ((0, 0), (0, 0), (0, -(local * rows) % width)))
        pieces = [out.reshape(ring, part // ring, width), columns.reshape(ring, -1, width)]
        return jnp.concatenate([p.astype(bf16) for p in pieces], 1)

    forth.step(2, after=dms)
    dhs = order.exchange(rest[count:])
    keep, send, qkv_low, gain_sum = order.run(
        attention_back, idx, xs, dms, qkv, w_qkv, gain1, live_rows, ring
    )
    forth.step(3, after=dhs)
    out_moved = order.swap(going, 1)
    sums = [keep, order.swap(send, 1)]
    outs = out_sum(stay, out_moved)
    for bit in bits[1:]:
        out_moved = order.swap(jnp.stack(outs[1::2]), bit)
        sums.append(order.swap(order.run(fold, idx, sums, bit), bit))
        outs = out_sum(outs[0::2], out_moved)
    packed = order.fuse(pack, outs[0], gsum)
    packed = lax.all_to_all(packed, "frames", 0, 0, tiled=True)
    weights(1)
    for s in range(4, far + 1):
        forth.step(s)
    weights(2)
    packed = order.fuse(lambda m: jnp.sum(m.astype(f32), axis=0), packed)
    out_low = packed[: part // ring].astype(bf16)
    gain_ffn_grad = packed[part // ring :].reshape(-1)[: local * rows]

    def both(a, b):
        return jnp.concatenate([a, b], 0)

    def unmix(blocks, axis, bits):
        have = [0]
        for bit in bits:
            have = have + [j ^ bit for j in have]
        inverse = jnp.array([have.index(j) for j in range(len(have))])
        places = jnp.take(inverse, lax.axis_index(axis) ^ jnp.arange(len(have)), mode="clip")
        return jnp.take(blocks, places, axis=0, mode="clip")

    def join(a, b, c, d):
        return both(a, c), b + d

    def both_ways(out, gain, axis, bit):
        nearby = order.swap(out, bit, axis), order.swap(gain, bit, axis)
        return order.fuse(join, out, gain, *nearby)

    ring_bits = [1 << i for i in range((ring - 1).bit_length())][::-1]
    out_low = out_low[None]
    for i, bit in enumerate(ring_bits):
        nearby = order.swap(out_low, bit, "frames"), order.swap(gain_sum, bit, "frames")
        if i == 0:
            block = order.run(
                block_rows, idx, forth.parts, branches[0], hidden, live_own, count
            )
            block = order.exchange(block)
        if i == 1:
            grad_in = order.run(input_grad, idx, xs, dhs, sums, gain1, 0, 1)
        out_low, gain_sum = order.fuse(join, out_low, gain_sum, *nearby)
    moved = lax.all_to_all(order.tie(qkv_low), "frames", 0, 0, tiled=True)
    block_out = order.run(gather_block, idx, block)
    out_low = unmix(out_low, "frames", ring_bits)[None]
    for bit in bits[::-1]:
        out_low, gain_sum = both_ways(out_low, gain_sum, "pos", bit)
    qkv_grad = order.fuse(lambda m: jnp.sum(m.astype(f32), axis=0), moved).reshape(3, rows, part)
    out_grad = unmix(out_low, "pos", bits[::-1]).reshape(width, width).astype(f32)
    gain_attn_grad = gain_sum

    ffn_grad = None
    for term in totals.values():
        ffn_grad = term if ffn_grad is None else ffn_grad + term
    return (
        block_out,
        grad_in,
        gain_attn_grad.reshape(width),
        qkv_grad.transpose(1, 0, 2),
        out_grad,
        gain_ffn_grad.reshape(local, rows),
        ffn_grad.transpose(0, 2, 1, 3),
    )


def solution(mesh):
    placed = (
        P("frames", None, "pos"),
        P("frames"),
        P(),
        P(None, None, "pos"),
        P(),
        P("pos", None),
        P("frames", "pos", None, None),
        P("frames", None, "pos"),
    )
    return jax.shard_map(
        body,
        mesh=mesh,
        in_specs=placed,
        out_specs=(
            P("frames", None, "pos"),
            P("frames", None, "pos"),
            P(),
            P("frames", None, "pos"),
            P(),
            P("pos", "frames"),
            P("frames", "pos", None, None),
        ),
        check_vma=False,
    )
```

```python
import functools

import jax
import jax.numpy as jnp
from jax import lax
from jax.experimental import pallas as pl
from jax.experimental.pallas import tpu as pltpu
from jax.sharding import PartitionSpec as P

HEAD_DIM = 64
EPS = 1e-05
MASKED = -1e30
GROUP = 16
STEP = 32
EXTRA = 16
COST = 0.0001
VMEM_LIMIT = 56 * 1024 * 1024

f32 = jnp.float32
bf16 = jnp.bfloat16


def dot(a, b, ca, cb):
    return lax.dot_general(a, b, (((ca,), (cb,)), ((), ())), preferred_element_type=f32)


def cost(us):
    us = us * COST
    return pl.CostEstimate(flops=int(us * 1.15e9), bytes_accessed=int(us * 1e6), transcendentals=0)


def params():
    return pltpu.CompilerParams(vmem_limit_bytes=VMEM_LIMIT)


def to_owners(me, rows, depth, local):
    r = lax.broadcasted_iota(jnp.int32, (rows, rows), 0)
    c = lax.broadcasted_iota(jnp.int32, (rows, rows), 1)
    frames = rows // depth
    k = r // frames
    source = (r % frames) * depth + ((k // local) ^ me) * local + k % local
    return jnp.where(c == source, 1.0, 0.0).astype(bf16)


def from_owners(me, rows, depth, local):
    r = lax.broadcasted_iota(jnp.int32, (rows, rows), 0)
    c = lax.broadcasted_iota(jnp.int32, (rows, rows), 1)
    frames = rows // depth
    k = r % depth
    source = (((k // local) ^ me) * local + k % local) * frames + r // depth
    return jnp.where(c == source, 1.0, 0.0).astype(bf16)


def pick(blocks, index):
    out = blocks[0]
    for b in range(1, len(blocks)):
        out = jnp.where(index == b, blocks[b], out)
    return out


def row_to_column(row):
    n = row.shape[1]
    r = lax.broadcasted_iota(jnp.int32, (n, n), 0)
    c = lax.broadcasted_iota(jnp.int32, (n, n), 1)
    return jnp.sum(jnp.where(r == c, row, 0.0), axis=1, keepdims=True)


def column_to_row(column):
    n = column.shape[0]
    r = lax.broadcasted_iota(jnp.int32, (n, n), 0)
    c = lax.broadcasted_iota(jnp.int32, (n, n), 1)
    return jnp.sum(jnp.where(r == c, column, 0.0), axis=0, keepdims=True)


def pair_mask(live_row, half, depth):
    n = live_row.shape[1] // 2
    live = row_to_column(live_row[:, half * n : (half + 1) * n])
    r = lax.broadcasted_iota(jnp.int32, (n, n), 0)
    c = lax.broadcasted_iota(jnp.int32, (n, n), 1)
    allowed = ((r // depth) == (c // depth)) & (r <= c) & (live > 0.5)
    return jnp.concatenate([allowed, allowed], 1)


def split_heads(block):
    lane = lax.broadcasted_iota(jnp.int32, block.shape, 1)
    zero = jnp.zeros_like(block)
    return jnp.concatenate(
        [jnp.where(lane < HEAD_DIM, block, zero), jnp.where(lane >= HEAD_DIM, block, zero)], 0
    )


def join_heads(pair):
    n = pair.shape[0] // 2
    lane = lax.broadcasted_iota(jnp.int32, (n, pair.shape[1]), 1)
    return jnp.where(lane < HEAD_DIM, pair[:n], pair[n:])


def pair_probs(q2, k2, allowed):
    scores = jnp.where(allowed, dot(k2, q2, 1, 1), MASKED)
    e = jnp.exp(scores - jnp.max(scores, axis=0, keepdims=True))
    return e * (1.0 / jnp.sum(e, axis=0, keepdims=True))


def per_step(frames, step):
    return min(step, frames)


def place(back, pieces, f):
    local, _, part = pieces[0].shape
    blocks = [p[:, f].reshape(local * GROUP, part) for p in pieces]
    return dot(back, jnp.concatenate(blocks, 0), 1, 0)


def row_scale(pieces):
    total = None
    for x in pieces:
        xf = x.astype(f32)
        term = jnp.sum(xf * xf, axis=-1, keepdims=True)
        total = term if total is None else total + term
    return lax.rsqrt(total / (pieces[0].shape[1] * len(pieces)) + EPS)


def cot_kernel(count, idx_ref, cot_ref, live_ref, *outs):
    step, depth, part = cot_ref.shape
    rows = GROUP * depth
    local = depth // count
    move = to_owners(idx_ref[0], rows, depth, local)
    for g in range(step // GROUP):
        f = slice(g * GROUP, (g + 1) * GROUP)
        live = row_to_column(live_ref[g])
        masked = (cot_ref[f].reshape(rows, part).astype(f32) * live).astype(bf16)
        moved = dot(move, masked, 1, 0).astype(bf16).reshape(count, local, GROUP, part)
        for j in range(count):
            outs[j][:, f] = moved[j]


def split_cot(idx, cot, live, count):
    frames, depth, part = cot.shape
    local = depth // count
    step = per_step(frames, 64)
    return pl.pallas_call(
        functools.partial(cot_kernel, count),
        grid_spec=pltpu.PrefetchScalarGridSpec(
            num_scalar_prefetch=1,
            grid=(frames // step,),
            in_specs=[
                pl.BlockSpec((step, depth, part), lambda i, s: (i, 0, 0)),
                pl.BlockSpec((step // GROUP, 1, GROUP * depth), lambda i, s: (i, 0, 0)),
            ],
            out_specs=[pl.BlockSpec((local, step, part), lambda i, s: (0, i, 0))] * count,
        ),
        out_shape=[jax.ShapeDtypeStruct((local, frames, part), bf16)] * count,
        compiler_params=params(),
        cost_estimate=cost(4),
    )(idx, cot, live)


def attn_kernel(count, idx_ref, *refs):
    xs = refs[:count]
    w_ref, gain_ref, live_ref = refs[count : count + 3]
    qkv_ref, resid_ref = refs[count + 3 : count + 5]
    outs = refs[count + 5 :]
    me = idx_ref[0]
    step, depth, part = xs[0].shape
    rows = GROUP * depth
    local = depth // count
    half_rows = rows // 2
    move = to_owners(me, rows, depth, local)
    own = move[: local * GROUP]
    for g in range(step // GROUP):
        f = slice(g * GROUP, (g + 1) * GROUP)
        r = slice(g * rows, (g + 1) * rows)
        pieces = [x[f].reshape(rows, part) for x in xs]
        rms = row_scale(pieces)
        acc = [None] * 3
        for j in range(count):
            normed = (pieces[j].astype(f32) * rms * gain_ref[me ^ j]).astype(bf16)
            for c in range(3):
                term = dot(normed, w_ref[c, me ^ j], 1, 0)
                acc[c] = term if acc[c] is None else acc[c] + term
            moved = dot(own, pieces[j], 1, 0).astype(bf16)
            resid_ref[me ^ j, :, f] = moved.reshape(local, GROUP, part)
        q, k, v = [a.astype(bf16) for a in acc]
        qkv_ref[0, r], qkv_ref[1, r], qkv_ref[2, r] = q, k, v
        q = q * (HEAD_DIM**-0.5)
        mixed = []
        for half in range(2):
            allowed = pair_mask(live_ref[g], half, depth)
            sl = slice(half * half_rows, (half + 1) * half_rows)
            cols = []
            for pair in range(part // 128):
                ln = slice(pair * 128, (pair + 1) * 128)
                probs = pair_probs(split_heads(q[sl, ln]), k[sl, ln], allowed).astype(bf16)
                cols.append(join_heads(dot(probs, v[sl, ln], 0, 0)).astype(bf16))
            mixed.append(jnp.concatenate(cols, 1) if len(cols) > 1 else cols[0])
        mixed = jnp.concatenate(mixed, 0)
        moved = dot(move, mixed, 1, 0).astype(bf16).reshape(count, local, GROUP, part)
        for j in range(count):
            outs[j][:, f] = moved[j]


def attention(idx, xs, w, gain, live, chunk, chunks):
    count = len(xs)
    frames, depth, part = xs[0].shape
    local = depth // count
    frames = frames // chunks
    step = per_step(frames, STEP)
    n = frames // step
    base = chunk * n
    rows = step * depth
    return pl.pallas_call(
        functools.partial(attn_kernel, count),
        grid_spec=pltpu.PrefetchScalarGridSpec(
            num_scalar_prefetch=1,
            grid=(n,),
            in_specs=[pl.BlockSpec((step, depth, part), lambda i, s: (i + base, 0, 0))] * count
            + [
                pl.BlockSpec(w.shape, lambda i, s: (0, 0, 0, 0)),
                pl.BlockSpec(gain.shape, lambda i, s: (0, 0, 0)),
                pl.BlockSpec((step // GROUP, 1, GROUP * depth), lambda i, s: (i + base, 0, 0)),
            ],
            out_specs=[
                pl.BlockSpec((3, rows, part), lambda i, s: (0, i, 0)),
                pl.BlockSpec((count, local, step, part), lambda i, s: (0, 0, i, 0)),
            ]
            + [pl.BlockSpec((local, step, part), lambda i, s: (0, i, 0))] * count,
        ),
        out_shape=[
            jax.ShapeDtypeStruct((3, frames * depth, part), bf16),
            jax.ShapeDtypeStruct((count, local, frames, part), bf16),
        ]
        + [jax.ShapeDtypeStruct((local, frames, part), bf16)] * count,
        compiler_params=params(),
        cost_estimate=cost(8),
    )(idx, *xs, w, gain, live)


def half_specs(local, frames, width):
    half = local // 2
    return [
        pl.BlockSpec((1, frames, width), lambda k, *s: (jnp.minimum(k, half - 1), 0, 0)),
        pl.BlockSpec((1, frames, width), lambda k, *s: (jnp.maximum(k - half, 0), 0, 0)),
    ]


def store_half(is_first, first_ref, second_ref, at, value):
    @pl.when(is_first)
    def _():
        first_ref[at] = value

    @pl.when(jnp.logical_not(is_first))
    def _():
        second_ref[at] = value


def load_half(is_first, first_ref, second_ref):
    return jnp.where(is_first, first_ref[0], second_ref[0])


def project_kernel(count, chunks, idx_ref, *refs):
    mixed = refs[: count * chunks]
    resids = refs[count * chunks : (count + 1) * chunks]
    w_ref, gain_ref, hidden_ref, norm_ref = refs[(count + 1) * chunks :]
    me = idx_ref[0]
    size = mixed[0].shape[1]
    for c in range(chunks):
        f = slice(c * size, (c + 1) * size)
        hidden = jnp.concatenate([resids[c][b, 0] for b in range(count)], 1).astype(f32)
        for j in range(count):
            hidden = hidden + dot(mixed[c * count + j][0], w_ref[me ^ j], 1, 0)
        hidden_ref[0, f] = hidden
        rms = lax.rsqrt(jnp.mean(hidden * hidden, axis=-1, keepdims=True) + EPS)
        norm_ref[0, f] = (hidden * rms * gain_ref[0]).astype(bf16)


def project(idx, mixed, resids, w, gain):
    chunks, count = len(mixed), len(mixed[0])
    local, size, part = mixed[0][0].shape
    frames, width = size * chunks, part * count
    each = pl.BlockSpec((1, frames, width), lambda k, s: (k, 0, 0))
    return pl.pallas_call(
        functools.partial(project_kernel, count, chunks),
        grid_spec=pltpu.PrefetchScalarGridSpec(
            num_scalar_prefetch=1,
            grid=(local,),
            in_specs=[pl.BlockSpec((1, size, part), lambda k, s: (k, 0, 0))] * (count * chunks)
            + [pl.BlockSpec((count, 1, size, part), lambda k, s: (0, k, 0, 0))] * chunks
            + [
                pl.BlockSpec(w.shape, lambda k, s: (0, 0, 0)),
                pl.BlockSpec((1, 1, width), lambda k, s: (k, 0, 0)),
            ],
            out_specs=[each, each],
        ),
        out_shape=[
            jax.ShapeDtypeStruct((local, frames, width), f32),
            jax.ShapeDtypeStruct((local, frames, width), bf16),
        ],
        compiler_params=params(),
        cost_estimate=cost(6),
    )(idx, *[m for part_ in mixed for m in part_], *resids, w, gain)


def load_block(is_first, refs):
    return refs[0][0] if len(refs) == 1 else load_half(is_first, *refs)


def block_parts(block):
    return list(block) if isinstance(block, tuple) else [block]


def ffn_kernel(sizes, idx_ref, *refs):
    n = len(sizes) // 2
    ins = sum(sizes)
    w_ref = refs[ins]
    dnorms, branches = refs[ins + 1 : ins + 1 + 2 * n], refs[ins + 1 + 2 * n : ins + 1 + 3 * n]
    act_ref = refs[-1]
    is_first = pl.program_id(0) < pl.num_programs(0) // 2
    blocks, at = [], 0
    for size in sizes:
        blocks.append(load_block(is_first, refs[at : at + size]))
        at += size
    frames = blocks[0].shape[0]
    norm = jnp.concatenate(blocks[:n], 0)
    grad = jnp.concatenate(blocks[n:], 0)
    gate = dot(norm, w_ref[0, 0], 1, 1)
    up = dot(norm, w_ref[0, 1], 1, 1)
    dact = dot(grad, w_ref[0, 2], 1, 1)
    sig = jax.nn.sigmoid(gate)
    silu = gate * sig
    act = (silu * up).astype(bf16)
    dgate = (dact * up * sig * (1.0 + gate * (1.0 - sig))).astype(bf16)
    dup = (dact * silu).astype(bf16)
    act_ref[0, 0] = dgate
    act_ref[0, 1] = dup
    act_ref[0, 2] = act
    dnorm = (dot(dgate, w_ref[0, 0], 1, 0) + dot(dup, w_ref[0, 1], 1, 0)).astype(bf16)
    branch = dot(act, w_ref[0, 2], 1, 0).astype(bf16)
    for i in range(n):
        rows = slice(i * frames, (i + 1) * frames)
        store_half(is_first, *dnorms[2 * i : 2 * i + 2], 0, dnorm[rows])
        branches[i][0] = branch[rows]


def ffn(idx, norms, grads, w):
    n = len(norms)
    blocks = [block_parts(v) for v in (*norms, *grads)]
    local, _, hidden, width = w.shape
    frames = blocks[0][0].shape[1]
    halves = half_specs(local, frames, width)
    whole = [pl.BlockSpec((1, frames, width), lambda k, s: (k, 0, 0))]
    *out, act = pl.pallas_call(
        functools.partial(ffn_kernel, [len(v) for v in blocks]),
        grid_spec=pltpu.PrefetchScalarGridSpec(
            num_scalar_prefetch=1,
            grid=(local,),
            in_specs=[x for v in blocks for x in (whole if len(v) == 1 else halves)]
            + [pl.BlockSpec((1, 3, hidden, width), lambda k, s: (k, 0, 0, 0))],
            out_specs=halves * n
            + whole * n
            + [pl.BlockSpec((1, 3, n * frames, hidden), lambda k, s: (k, 0, 0, 0))],
        ),
        out_shape=[jax.ShapeDtypeStruct((local // 2, frames, width), bf16)] * (2 * n)
        + [jax.ShapeDtypeStruct((local, frames, width), bf16)] * n
        + [jax.ShapeDtypeStruct((local, 3, n * frames, hidden), bf16)],
        compiler_params=params(),
        cost_estimate=cost(3.5 + 5 * n),
    )(idx, *[x for v in blocks for x in v], w)
    pairs = [out[i : i + 2] for i in range(0, 2 * n, 2)]
    return pairs, out[2 * n :], act


def weight_kernel(n, row, sizes, idx_ref, *refs):
    acts, out_ref = refs[:n], refs[-1]
    local = acts[0].shape[0]
    others, at = [], n
    for size in sizes:
        others.append(refs[at : at + size])
        at += size
    frames = others[0][0].shape[1]

    def entry(block, k):
        return block[k // block[0].shape[0]][k % block[0].shape[0]]

    for k in range(local):
        total, first = None, 0
        for a in acts:
            size = a.shape[2] // frames
            both = [entry(others[first + i], k) for i in range(size)]
            first += size
            both = jnp.concatenate(both, 0) if size > 1 else both[0]
            term = dot(a[k, 0], both, 0, 0)
            total = term if total is None else total + term
        out_ref[:, 0, k] = total


def weight_grad(idx, acts, others, row, out):
    n = len(acts)
    local, _, _, hidden = acts[0].shape
    chunk = min(128, hidden)
    others = [block_parts(v) for v in others]
    width = others[0][0].shape[2]
    ins = list(acts) + [x for v in others for x in v]
    specs = [
        pl.BlockSpec((local, 1, a.shape[2], chunk), lambda c, s: (0, row, 0, c)) for a in acts
    ] + [
        pl.BlockSpec(x.shape, lambda c, s: (0, 0, 0), pipeline_mode=pl.Buffered(1))
        for v in others
        for x in v
    ]
    aliases = {}
    kernel = functools.partial(weight_kernel, n, row, [len(v) for v in others])
    if out is not None:
        aliases = {1 + len(ins): 0}
        ins.append(out)
        specs.append(pl.BlockSpec(memory_space=pl.ANY))
    return pl.pallas_call(
        kernel,
        grid_spec=pltpu.PrefetchScalarGridSpec(
            num_scalar_prefetch=1,
            grid=(hidden // chunk,),
            in_specs=specs,
            out_specs=pl.BlockSpec((chunk, 1, local, width), lambda c, s: (c, row, 0, 0)),
        ),
        out_shape=jax.ShapeDtypeStruct((hidden, 3, local, width), f32),
        input_output_aliases=aliases,
        compiler_params=params(),
        cost_estimate=cost(12),
    )(idx, *ins)


def add_low(x, y):
    return (x.astype(f32) + y.astype(f32)).astype(bf16)


def merge_kernel(n, idx_ref, *refs):
    for i in range(n):
        refs[2 * n + i][...] = add_low(refs[i][...], refs[n + i][...])


def merge(idx, mine, moved):
    n = len(mine)
    half, frames, width = mine[0].shape
    each = pl.BlockSpec((1, frames, width), lambda k, s: (k, 0, 0))
    return pl.pallas_call(
        functools.partial(merge_kernel, n),
        grid_spec=pltpu.PrefetchScalarGridSpec(
            num_scalar_prefetch=1,
            grid=(half,),
            in_specs=[each] * (2 * n),
            out_specs=[each] * n,
        ),
        out_shape=[jax.ShapeDtypeStruct(mine[0].shape, bf16)] * n,
        compiler_params=params(),
        cost_estimate=cost(1.2 * n),
    )(idx, *mine, *moved)


def whole_kernel(half, idx_ref, f_ref, b_ref, up_ref, down_ref, fo_ref, bo_ref):
    if half is None:
        fo_ref[...] = add_low(f_ref[...], up_ref[...])
        bo_ref[...] = add_low(b_ref[...], down_ref[...])
        return
    is_first = pl.program_id(0) < half
    fo_ref[...] = jnp.where(is_first, add_low(f_ref[...], up_ref[...]), f_ref[...])
    bo_ref[...] = jnp.where(is_first, b_ref[...], add_low(b_ref[...], down_ref[...]))


def merge_whole(idx, f, b, up, down):
    local, frames, width = f.shape
    half = None if up.shape == f.shape else local // 2
    each = pl.BlockSpec((1, frames, width), lambda k, s: (k, 0, 0))
    moved = half_specs(local, frames, width) if half else [each] * 2
    return pl.pallas_call(
        functools.partial(whole_kernel, half),
        grid_spec=pltpu.PrefetchScalarGridSpec(
            num_scalar_prefetch=1,
            grid=(local,),
            in_specs=[each, each, *moved],
            out_specs=[each, each],
        ),
        out_shape=[jax.ShapeDtypeStruct(f.shape, bf16)] * 2,
        compiler_params=params(),
        cost_estimate=cost(4),
    )(idx, f, b, up, down)


def sum_halves(refs):
    is_first = pl.program_id(0) < pl.num_programs(0) // 2
    total = None
    for i in range(0, len(refs), 2):
        term = load_half(is_first, *refs[i : i + 2]).astype(f32)
        total = term if total is None else total + term
    return total


def resid_kernel(count, idx_ref, *refs):
    hidden_ref, branch_ref, gain_ref, w_ref, low_ref, gsum_ref = refs[6:12]
    dms, dhs = refs[12 : 12 + count], refs[12 + count :]
    me = idx_ref[0]
    part = w_ref.shape[1]
    dnorm = sum_halves(refs[:6])
    hidden = hidden_ref[0]
    rms = lax.rsqrt(jnp.mean(hidden * hidden, axis=-1, keepdims=True) + EPS)
    xhat = hidden * rms
    gsum_ref[0] = jnp.sum(dnorm * xhat, axis=0, keepdims=True)
    u = dnorm * gain_ref[0]
    inner = jnp.mean(xhat * u, axis=-1, keepdims=True)
    low = (branch_ref[0].astype(f32) + rms * (u - xhat * inner)).astype(bf16)
    low_ref[0] = low
    blocks = [low[:, b * part : (b + 1) * part] for b in range(count)]
    for j in range(count):
        dhs[j][0] = pick(blocks, me ^ j)
        dms[j][0] = dot(low, w_ref[me ^ j], 1, 1).astype(bf16)


def resid_grad(idx, recv, own, hidden, branch, gain, w):
    count, part, width = w.shape
    local, frames, _ = hidden.shape
    each = pl.BlockSpec((1, frames, width), lambda k, s: (k, 0, 0))
    return pl.pallas_call(
        functools.partial(resid_kernel, count),
        grid_spec=pltpu.PrefetchScalarGridSpec(
            num_scalar_prefetch=1,
            grid=(local,),
            in_specs=half_specs(local, frames, width) * 3
            + [each] * 2
            + [
                pl.BlockSpec((1, 1, width), lambda k, s: (k, 0, 0)),
                pl.BlockSpec(w.shape, lambda k, s: (0, 0, 0)),
            ],
            out_specs=[each, pl.BlockSpec((1, 1, width), lambda k, s: (k, 0, 0))]
            + [pl.BlockSpec((1, frames, part), lambda k, s: (k, 0, 0))] * (2 * count),
        ),
        out_shape=[
            jax.ShapeDtypeStruct((local, frames, width), bf16),
            jax.ShapeDtypeStruct((local, 1, width), f32),
        ]
        + [jax.ShapeDtypeStruct((local, frames, part), bf16)] * (2 * count),
        compiler_params=params(),
        cost_estimate=cost(8),
    )(idx, *recv, *own, hidden, branch, gain, w)


def attn_back_kernel(count, ring, idx_ref, *refs):
    xs = refs[:count]
    dms = refs[count : 2 * count]
    qkv_ref, w_ref, gain_ref, live_ref = refs[2 * count : 2 * count + 4]
    keep_ref, send_ref, wlow_ref, gsum_ref, wsum_ref = refs[2 * count + 4 :]
    me = idx_ref[0]
    step, depth, part = xs[0].shape
    rows = GROUP * depth
    back = from_owners(me, rows, depth, depth // count)
    half_rows = rows // 2
    factor = HEAD_DIM**-0.5

    @pl.when(pl.program_id(0) == 0)
    def _():
        wsum_ref[...] = jnp.zeros_like(wsum_ref)
        gsum_ref[...] = jnp.zeros_like(gsum_ref)

    every, rmss = [[], [], []], []
    for g in range(step // GROUP):
        f = slice(g * GROUP, (g + 1) * GROUP)
        r = slice(g * rows, (g + 1) * rows)
        dmixed = place(back, dms, f).astype(bf16)
        q, k, v = qkv_ref[0, r] * factor, qkv_ref[1, r], qkv_ref[2, r]
        for half in range(2):
            allowed = pair_mask(live_ref[g], half, depth)
            sl = slice(half * half_rows, (half + 1) * half_rows)
            cols = [[], [], []]
            for pair in range(part // 128):
                ln = slice(pair * 128, (pair + 1) * 128)
                q2, k2, v2 = split_heads(q[sl, ln]), k[sl, ln], v[sl, ln]
                dm2 = split_heads(dmixed[sl, ln])
                probs = pair_probs(q2, k2, allowed)
                dprobs = dot(v2, dm2, 1, 1)
                inner = jnp.sum(probs * dprobs, axis=0, keepdims=True)
                ds = (probs * (dprobs - inner)).astype(bf16)
                cols[0].append((join_heads(dot(ds, k2, 0, 0)) * factor).astype(bf16))
                cols[1].append(dot(ds, q2, 1, 0).astype(bf16))
                cols[2].append(dot(probs.astype(bf16), dm2, 1, 0).astype(bf16))
            for c in range(3):
                every[c].append(jnp.concatenate(cols[c], 1) if len(cols[c]) > 1 else cols[c][0])
    dqkv = [jnp.concatenate(p, 0) for p in every]
    rows = step * depth
    pieces = [x[...].reshape(rows, part) for x in xs]
    rms = row_scale(pieces)
    inner = jnp.zeros((rows, 1), f32)
    for j in range(count):
        owner = me ^ j
        xhat = pieces[j].astype(f32) * rms
        scaled = xhat * gain_ref[owner]
        normed = scaled.astype(bf16)
        dn = jnp.zeros((rows, part), f32)
        for c in range(3):
            dn = dn + dot(dqkv[c], w_ref[c, owner], 1, 1)
            wsum_ref[c, owner] += dot(normed, dqkv[c], 0, 0)
        inner = inner + jnp.sum(scaled * dn, axis=-1, keepdims=True)
        gsum_ref[owner] += jnp.sum(dn * xhat, axis=0, keepdims=True)
        (send_ref if j & 1 else keep_ref)[j // 2, :rows] = dn.astype(bf16)
    size = GROUP * depth
    lines = [column_to_row(inner[g * size : (g + 1) * size]) for g in range(step // GROUP)]
    lines = [line[:, i : i + part] for line in lines for i in range(0, size, part)]
    lines.append(jnp.zeros((EXTRA - len(lines), part), f32))
    lines = jnp.concatenate(lines, 0).astype(bf16)
    for i in range(count // 2):
        send_ref[i, rows:] = lines
        keep_ref[i, rows:] = lines

    @pl.when(pl.program_id(0) == pl.num_programs(0) - 1)
    def _():
        size = part * count // ring
        for i in range(ring):
            block, line = i * size // part, i * size % part
            for c in range(3):
                wlow_ref[i, c * size : (c + 1) * size] = wsum_ref[
                    c, block, line : line + size
                ].astype(bf16)


def attention_back(idx, xs, dms, qkv, w, gain, live, ring):
    count = len(xs)
    frames, depth, part = xs[0].shape
    local = dms[0].shape[0]
    step = per_step(frames, STEP)
    n = frames // step
    rows = step * depth
    low_shape = (ring, 3 * part * count // ring, part)
    lives = pl.BlockSpec((step // GROUP, 1, GROUP * depth), lambda i, s: (i, 0, 0))
    return pl.pallas_call(
        functools.partial(attn_back_kernel, count, ring),
        grid_spec=pltpu.PrefetchScalarGridSpec(
            num_scalar_prefetch=1,
            grid=(n,),
            in_specs=[pl.BlockSpec((step, depth, part), lambda i, s: (i, 0, 0))] * count
            + [pl.BlockSpec((local, step, part), lambda i, s: (0, i, 0))] * count
            + [
                pl.BlockSpec((3, rows, part), lambda i, s: (0, i, 0)),
                pl.BlockSpec(w.shape, lambda i, s: (0, 0, 0, 0)),
                pl.BlockSpec(gain.shape, lambda i, s: (0, 0, 0)),
                lives,
            ],
            out_specs=[pl.BlockSpec((count // 2, rows + EXTRA, part), lambda i, s: (0, i, 0))] * 2
            + [
                pl.BlockSpec(low_shape, lambda i, s: (0, 0, 0)),
                pl.BlockSpec((count, 1, part), lambda i, s: (0, 0, 0)),
            ],
            scratch_shapes=[pltpu.VMEM(w.shape, f32)],
        ),
        out_shape=[jax.ShapeDtypeStruct((count // 2, n * (rows + EXTRA), part), bf16)] * 2
        + [
            jax.ShapeDtypeStruct(low_shape, bf16),
            jax.ShapeDtypeStruct((count, 1, part), f32),
        ],
        compiler_params=params(),
        cost_estimate=cost(26),
    )(idx, *xs, *dms, qkv, w, gain, live)


def fold_kernel(n, idx_ref, *refs):
    total = refs[0][...].astype(f32)
    for r in refs[1:n]:
        total = total + r[...].astype(f32)
    refs[n][...] = total.astype(bf16)


def fold(idx, terms, bit):
    n = len(terms)
    _, rows, part = terms[0].shape
    hop = bit // 2

    def spec(i):
        step = 1 if i < 2 else 1 << (i - 1)
        return pl.BlockSpec((1, rows, part), lambda g, s: (hop * (2 * g + 1) // step, 0, 0))

    return pl.pallas_call(
        functools.partial(fold_kernel, n),
        grid_spec=pltpu.PrefetchScalarGridSpec(
            num_scalar_prefetch=1,
            grid=(terms[0].shape[0] // bit,),
            in_specs=[spec(i) for i in range(n)],
            out_specs=pl.BlockSpec((1, rows, part), lambda g, s: (g, 0, 0)),
        ),
        out_shape=jax.ShapeDtypeStruct((terms[0].shape[0] // bit, rows, part), bf16),
        compiler_params=params(),
        cost_estimate=cost(2),
    )(idx, *terms)


def out_kernel(count, chunks, idx_ref, *refs):
    low_ref, outs = refs[count * chunks], refs[count * chunks + 1 :]
    local, size, _ = refs[0].shape
    width = low_ref.shape[2]
    lows = []
    for c in range(chunks):
        part_ = low_ref[:, c * size : (c + 1) * size]
        lows.append(part_.reshape(local * size, width))
    low = jnp.concatenate(lows, 0)
    for j in range(count):
        mine = [refs[c * count + j][...].reshape(local * size, -1) for c in range(chunks)]
        out = dot(jnp.concatenate(mine, 0), low, 0, 0).astype(bf16)
        if j & 1:
            outs[-1][j // 2] = out
        else:
            outs[j // 2][...] = out


def out_terms(idx, mixeds, low):
    chunks, count = len(mixeds), len(mixeds[0])
    part, width = mixeds[0][0].shape[2], low.shape[2]
    return pl.pallas_call(
        functools.partial(out_kernel, count, chunks),
        grid_spec=pltpu.PrefetchScalarGridSpec(
            num_scalar_prefetch=1,
            grid=(1,),
            in_specs=[pl.BlockSpec(m.shape, lambda i, s: (0, 0, 0)) for p in mixeds for m in p]
            + [pl.BlockSpec(low.shape, lambda i, s: (0, 0, 0))],
            out_specs=[pl.BlockSpec((part, width), lambda i, s: (0, 0))] * (count // 2)
            + [pl.BlockSpec((count // 2, part, width), lambda i, s: (0, 0, 0))],
        ),
        out_shape=[jax.ShapeDtypeStruct((part, width), bf16)] * (count // 2)
        + [jax.ShapeDtypeStruct((count // 2, part, width), bf16)],
        compiler_params=params(),
        cost_estimate=cost(6),
    )(idx, *[m for p in mixeds for m in p], low)


def input_kernel(count, terms_count, idx_ref, *refs):
    xs = refs[:count]
    dhs = refs[count : 2 * count]
    terms = refs[2 * count : 2 * count + terms_count]
    gain_ref, out_ref = refs[2 * count + terms_count :]
    me = idx_ref[0]
    step, depth, part = xs[0].shape
    rows = GROUP * depth
    back = from_owners(me, rows, depth, depth // count)
    sums = terms[0][0, step * depth :].astype(f32)
    for t in terms[1:]:
        sums = sums + t[0, step * depth :].astype(f32)
    lines = rows // part
    for g in range(step // GROUP):
        f = slice(g * GROUP, (g + 1) * GROUP)
        r = slice(g * rows, (g + 1) * rows)
        resid = place(back, dhs, f)
        pieces = [x[f].reshape(rows, part) for x in xs]
        rms = row_scale(pieces)
        xhat = pieces[0].astype(f32) * rms
        dn = terms[0][0, r].astype(f32)
        for t in terms[1:]:
            dn = dn + t[0, r].astype(f32)
        line = [sums[i : i + 1] for i in range(g * lines, (g + 1) * lines)]
        line = jnp.concatenate(line, 1) if lines > 1 else line[0]
        inner = row_to_column(line) / (part * count)
        out = resid + rms * (dn * gain_ref[me] - xhat * inner)
        out_ref[f] = out.astype(bf16).reshape(GROUP, depth, part)


def input_grad(idx, xs, dhs, terms, gain, chunk, chunks):
    count = len(xs)
    frames, depth, part = xs[0].shape
    local = dhs[0].shape[0]
    frames = frames // chunks
    step = per_step(frames, STEP)
    n = frames // step
    base = chunk * n
    rows = step * depth
    return pl.pallas_call(
        functools.partial(input_kernel, count, len(terms)),
        grid_spec=pltpu.PrefetchScalarGridSpec(
            num_scalar_prefetch=1,
            grid=(n,),
            in_specs=[pl.BlockSpec((step, depth, part), lambda i, s: (i + base, 0, 0))] * count
            + [pl.BlockSpec((local, step, part), lambda i, s: (0, i + base, 0))] * count
            + [pl.BlockSpec((1, rows + EXTRA, part), lambda i, s: (0, i, 0))] * len(terms)
            + [pl.BlockSpec(gain.shape, lambda i, s: (0, 0, 0))],
            out_specs=pl.BlockSpec((step, depth, part), lambda i, s: (i, 0, 0)),
        ),
        out_shape=jax.ShapeDtypeStruct((frames, depth, part), bf16),
        compiler_params=params(),
        cost_estimate=cost(4),
    )(idx, *xs, *dhs, *terms, gain)


def block_kernel(count, idx_ref, *refs):
    up, down, own, hidden_ref, live_ref = refs[:5]
    outs = refs[5:]
    me = idx_ref[0]
    part = outs[0].shape[2]
    branch = up[0].astype(f32) + down[0].astype(f32) + own[0].astype(f32)
    rows = ((hidden_ref[0] + branch) * row_to_column(live_ref[0])).astype(bf16)
    blocks = [rows[:, b * part : (b + 1) * part] for b in range(count)]
    for j in range(count):
        outs[j][0] = pick(blocks, me ^ j)


def block_rows(idx, recv, own, hidden, live, count):
    local, frames, width = hidden.shape
    part = width // count
    each = pl.BlockSpec((1, frames, width), lambda k, s: (k, 0, 0))
    return pl.pallas_call(
        functools.partial(block_kernel, count),
        grid_spec=pltpu.PrefetchScalarGridSpec(
            num_scalar_prefetch=1,
            grid=(local,),
            in_specs=[each] * 4 + [pl.BlockSpec((1, 1, frames), lambda k, s: (k, 0, 0))],
            out_specs=[pl.BlockSpec((1, frames, part), lambda k, s: (k, 0, 0))] * count,
        ),
        out_shape=[jax.ShapeDtypeStruct((local, frames, part), bf16)] * count,
        compiler_params=params(),
        cost_estimate=cost(4),
    )(idx, *recv, own, hidden, live)


def gather_kernel(count, idx_ref, *refs):
    pieces, out_ref = refs[:count], refs[count]
    step, depth, part = out_ref.shape
    back = from_owners(idx_ref[0], GROUP * depth, depth, depth // count)
    for g in range(step // GROUP):
        f = slice(g * GROUP, (g + 1) * GROUP)
        out = place(back, pieces, f)
        out_ref[f] = out.astype(bf16).reshape(GROUP, depth, part)


def gather_block(idx, pieces):
    count = len(pieces)
    local, frames, part = pieces[0].shape
    depth = local * count
    step = per_step(frames, 64)
    return pl.pallas_call(
        functools.partial(gather_kernel, count),
        grid_spec=pltpu.PrefetchScalarGridSpec(
            num_scalar_prefetch=1,
            grid=(frames // step,),
            in_specs=[pl.BlockSpec((local, step, part), lambda i, s: (0, i, 0))] * count,
            out_specs=pl.BlockSpec((step, depth, part), lambda i, s: (i, 0, 0)),
        ),
        out_shape=jax.ShapeDtypeStruct((frames, depth, part), bf16),
        compiler_params=params(),
        cost_estimate=cost(4),
    )(idx, *pieces)


class Order:
    def __init__(self):
        self.last = []

    def tie(self, *values, after=()):
        flat, tree = jax.tree.flatten(values)
        held = [*self.last, *jax.tree.leaves(after)]
        if held:
            flat = lax.optimization_barrier((*flat, *held))[: len(flat)]
        values = jax.tree.unflatten(tree, flat)
        return values[0] if len(values) == 1 else values

    def run(self, kernel, first, *args, after=()):
        out = kernel(self.tie(first, after=after), *args)
        self.last = [min(jax.tree.leaves(out), key=lambda v: v.size)]
        return out

    def fuse(self, step, *args, after=()):
        args = self.tie(*args, after=after)
        out = step(*args) if isinstance(args, tuple) else step(args)
        self.last = jax.tree.leaves(out)
        return out

    def send(self, value, axis, pairs):
        return lax.ppermute(self.tie(value), axis, pairs)

    def swap(self, value, bits, axis="pos"):
        count = lax.axis_size(axis)
        return self.send(value, axis, [(i, i ^ bits) for i in range(count)])

    def exchange(self, pieces):
        back = {j: self.swap(pieces[j], j) for j in range(len(pieces) - 1, 0, -1)}
        return [pieces[0]] + [back[j] for j in range(1, len(pieces))]


def ring_steps(count):
    order = list(range(0, count, 2)) + list(range(count - 1, 0, -2))
    forward = [(order[i], order[(i + 1) % count]) for i in range(count)]
    return forward, [(b, a) for a, b in forward]


class RingGather:
    def __init__(self, order, count, value):
        self.order, self.count = order, count
        self.forward, self.back = ring_steps(count)
        self.blocks = [value] + [None] * (count - 1)

    def step(self, s):
        count, blocks = self.count, self.blocks
        up, down = blocks[s - 1], blocks[(count - s + 1) % count]
        if s == count // 2:
            half = up.shape[0] // 2
            up, down = up[:half], down[half:]
        up = self.order.send(up, "frames", self.forward)
        down = self.order.send(down, "frames", self.back)
        if s < count // 2:
            blocks[s], blocks[count - s] = up, down
        else:
            blocks[s] = (up, down)

    def received(self, s):
        return [self.blocks[s], self.blocks[self.count - s]]


class RingSumWhole:
    def __init__(self, order, count, blocks, idx):
        self.order, self.count, self.blocks, self.idx = order, count, blocks, idx
        self.forward, self.back = ring_steps(count)

    def step(self, s, after=()):
        count, far = self.count, self.count // 2
        if s == 1:
            block = self.blocks[far]
            half = block.shape[0] // 2
            f, b = block[:half], block[half:]
        else:
            h = far - s + 1
            f, b = self.order.run(
                merge_whole, self.idx, self.blocks[count - h], self.blocks[h], *self.parts, after=after
            )
        self.parts = [
            self.order.send(f, "frames", self.forward),
            self.order.send(b, "frames", self.back),
        ]


class RingSum:
    def __init__(self, order, count, blocks, idx):
        self.order, self.count, self.blocks, self.idx = order, count, blocks, idx
        self.forward, self.back = ring_steps(count)
        self.parts = {}

    def step(self, chains, s, after=()):
        count, far = self.count, self.count // 2
        mine = []
        for chain in chains:
            h = far - s + 1 if chain == "x" else far - s
            first, second = (0, 1) if chain == "x" else (1, 0)
            mine += [self.blocks[(count - h) % count][first], self.blocks[h][second]]
        if s > 1:
            moved = [p for chain in chains for p in self.parts[chain]]
            mine = self.order.run(merge, self.idx, mine, moved, after=after)
        for i, chain in enumerate(chains):
            self.parts[chain] = [
                self.order.send(mine[2 * i], "frames", self.forward),
                self.order.send(mine[2 * i + 1], "frames", self.back),
            ]

    def received(self):
        return [self.parts["x"][0], self.parts["y"][0], self.parts["y"][1], self.parts["x"][1]]


CHUNKS = 1


def body(inputs, counts, gain_attn, weight_qkv, weight_out, gain_ffn, weight_ffn, cotangent):
    count = lax.axis_size("pos")
    ring = lax.axis_size("frames")
    far = ring // 2
    me = lax.axis_index("pos")
    idx = me.astype(jnp.int32).reshape(1)
    frames, depth, part = inputs.shape
    width = part * count
    local = depth // count
    half = local // 2
    order = Order()

    positions = jnp.arange(depth, dtype=jnp.int32)
    live = (positions[None, :] < counts[:, None]).astype(f32)
    live_rows = live.reshape(frames // GROUP, 1, GROUP * depth)
    live_own = lax.dynamic_slice_in_dim(live, me * local, local, 1).T.reshape(local, 1, frames)
    w_qkv = weight_qkv.transpose(1, 0, 2).reshape(3, count, part, part)
    w_out = weight_out.reshape(count, part, width)
    gain1 = gain_attn.reshape(count, 1, part)
    gain2 = gain_ffn.reshape(local, 1, width)
    distance = me ^ jnp.arange(count)

    def in_order(blocks):
        return jnp.take(blocks, distance, axis=0, mode="clip")

    cots = order.exchange(order.run(split_cot, idx, cotangent, live_rows, count))
    w_ffn = order.fuse(lambda w: w.transpose(1, 2, 0, 3), weight_ffn)

    def assemble(first, *rest):
        rows = in_order(jnp.stack([first, *rest])).transpose(1, 2, 0, 3)
        return rows.reshape(local, frames, width)

    branch = order.fuse(assemble, *cots)
    grads = RingGather(order, ring, branch)
    grads.step(1)

    xs = {0: inputs}
    bit = count // 2
    while bit:
        for j in list(xs):
            xs[j ^ bit] = order.swap(xs[j], bit)
        bit //= 2
    xs = [xs[j] for j in range(count)]
    grads.step(2)
    qkv, resid, *mixed = order.run(
        attention, idx, xs, w_qkv, gain1, live_rows, 0, 1, after=grads.received(1)
    )
    mixed = order.exchange(mixed)
    grads.step(3)
    hidden, norm = order.run(
        project, idx, [mixed], [resid], w_out, gain2, after=grads.received(2)
    )
    norms = RingGather(order, ring, norm)
    norms.step(1)

    groups = [[0]] + [[s, ring - s] for s in range(1, far)] + [[far]]
    dnorms, branches, acts = [None] * ring, [None] * ring, []

    def feed(s, after=()):
        group = groups[s]
        down, forth, act = order.run(
            ffn,
            idx,
            [norms.blocks[d] for d in group],
            [grads.blocks[d] for d in group],
            w_ffn,
            after=after,
        )
        for i, d in enumerate(group):
            dnorms[d], branches[d] = down[i], forth[i]
        acts.append(act)

    feed(0, after=grads.received(3))
    for s in range(4, far + 1):
        grads.step(s)
    for s in range(2, far + 1):
        norms.step(s)
        feed(s - 1)

    totals = {}

    def weights(row):
        for q in range(0, far + 1, 6):
            chosen = range(q, min(q + 6, far + 1))
            source = (grads if row == 2 else norms).blocks
            totals[q] = order.run(
                weight_grad,
                idx,
                [acts[i] for i in chosen],
                [source[d] for i in chosen for d in groups[i]],
                row,
                totals.get(q),
            )

    dnorm = RingSum(order, ring, dnorms, idx)
    forth = RingSumWhole(order, ring, branches, idx)
    dnorm.step("y", 1)
    feed(far)
    dnorm.step("x", 1)
    for s in range(2, far):
        dnorm.step("y", s)
        dnorm.step("x", s)
    dnorm.step("x", far)
    forth.step(1)

    low, gsum, *rest = order.run(
        resid_grad, idx, dnorm.received(), dnorms[0], hidden, branch, gain2, w_out
    )
    bits = [1 << i for i in range((count - 1).bit_length())]

    dms = order.exchange(rest[:count])
    *stay, going = order.run(out_terms, idx, [mixed], low)

    def out_sum(stay, moved):
        shape = (2, part // 2, width)
        mine = [v.reshape(shape) for v in stay]
        moved = [moved[i].reshape(shape) for i in range(len(stay))]
        return [v.reshape(part, width) for v in order.run(merge, idx, mine, moved)]

    rows = width // ring

    def pack(out, gsum):
        columns = gsum.reshape(local, ring, rows).transpose(1, 0, 2).reshape(ring, 1, local * rows)
        columns = jnp.pad(columns, ((0, 0), (0, 0), (0, -(local * rows) % width)))
        pieces = [out.reshape(ring, part // ring, width), columns.reshape(ring, -1, width)]
        return jnp.concatenate([p.astype(bf16) for p in pieces], 1)

    forth.step(2, after=dms)
    dhs = order.exchange(rest[count:])
    keep, send, qkv_low, gain_sum = order.run(
        attention_back, idx, xs, dms, qkv, w_qkv, gain1, live_rows, ring
    )
    forth.step(3, after=dhs)
    out_moved = order.swap(going, 1)
    sums = [keep, order.swap(send, 1)]
    outs = out_sum(stay, out_moved)
    for bit in bits[1:]:
        out_moved = order.swap(jnp.stack(outs[1::2]), bit)
        sums.append(order.swap(order.run(fold, idx, sums, bit), bit))
        outs = out_sum(outs[0::2], out_moved)
    packed = order.fuse(pack, outs[0], gsum)
    packed = lax.all_to_all(packed, "frames", 0, 0, tiled=True)
    weights(1)
    for s in range(4, far + 1):
        forth.step(s)
    weights(2)
    packed = order.fuse(lambda m: jnp.sum(m.astype(f32), axis=0), packed)
    out_low = packed[: part // ring].astype(bf16)
    gain_ffn_grad = packed[part // ring :].reshape(-1)[: local * rows]

    def both(a, b):
        return jnp.concatenate([a, b], 0)

    def unmix(blocks, axis, bits):
        have = [0]
        for bit in bits:
            have = have + [j ^ bit for j in have]
        inverse = jnp.array([have.index(j) for j in range(len(have))])
        places = jnp.take(inverse, lax.axis_index(axis) ^ jnp.arange(len(have)), mode="clip")
        return jnp.take(blocks, places, axis=0, mode="clip")

    def join(a, b, c, d):
        return both(a, c), b + d

    def both_ways(out, gain, axis, bit):
        nearby = order.swap(out, bit, axis), order.swap(gain, bit, axis)
        return order.fuse(join, out, gain, *nearby)

    ring_bits = [1 << i for i in range((ring - 1).bit_length())][::-1]
    out_low = out_low[None]
    for i, bit in enumerate(ring_bits):
        nearby = order.swap(out_low, bit, "frames"), order.swap(gain_sum, bit, "frames")
        if i == 1:
            block = order.run(
                block_rows, idx, forth.parts, branches[0], hidden, live_own, count
            )
        out_low, gain_sum = order.fuse(join, out_low, gain_sum, *nearby)
    moved = lax.all_to_all(order.tie(qkv_low), "frames", 0, 0, tiled=True)
    block = order.exchange(block)
    grad_in = order.run(input_grad, idx, xs, dhs, sums, gain1, 0, 1)
    block_out = order.run(gather_block, idx, block)
    out_low = unmix(out_low, "frames", ring_bits)[None]
    for i, bit in enumerate(bits[::-1]):
        nearby = order.swap(out_low, bit), order.swap(gain_sum, bit)
        if i == 0:
            weights(0)
        out_low, gain_sum = order.fuse(join, out_low, gain_sum, *nearby)
    qkv_grad = order.fuse(lambda m: jnp.sum(m.astype(f32), axis=0), moved).reshape(3, rows, part)
    out_grad = unmix(out_low, "pos", bits[::-1]).reshape(width, width).astype(f32)
    gain_attn_grad = gain_sum

    ffn_grad = None
    for term in totals.values():
        ffn_grad = term if ffn_grad is None else ffn_grad + term
    return (
        block_out,
        grad_in,
        gain_attn_grad.reshape(width),
        qkv_grad.transpose(1, 0, 2),
        out_grad,
        gain_ffn_grad.reshape(local, rows),
        ffn_grad.transpose(0, 2, 1, 3),
    )


def solution(mesh):
    placed = (
        P("frames", None, "pos"),
        P("frames"),
        P(),
        P(None, None, "pos"),
        P(),
        P("pos", None),
        P("frames", "pos", None, None),
        P("frames", None, "pos"),
    )
    return jax.shard_map(
        body,
        mesh=mesh,
        in_specs=placed,
        out_specs=(
            P("frames", None, "pos"),
            P("frames", None, "pos"),
            P(),
            P("frames", None, "pos"),
            P(),
            P("pos", "frames"),
            P("frames", "pos", None, None),
        ),
        check_vma=False,
    )
```

```python
import functools

import jax
import jax.numpy as jnp
from jax import lax
from jax.experimental import pallas as pl
from jax.experimental.pallas import tpu as pltpu
from jax.sharding import PartitionSpec as P

HEAD_DIM = 64
EPS = 1e-05
MASKED = -1e30
GROUP = 16
STEP = 64
EXTRA = 16
COST = 0.0001
VMEM_LIMIT = 56 * 1024 * 1024

f32 = jnp.float32
bf16 = jnp.bfloat16


def dot(a, b, ca, cb):
    return lax.dot_general(a, b, (((ca,), (cb,)), ((), ())), preferred_element_type=f32)


def cost(us):
    us = us * COST
    return pl.CostEstimate(flops=int(us * 1.15e9), bytes_accessed=int(us * 1e6), transcendentals=0)


def params():
    return pltpu.CompilerParams(vmem_limit_bytes=VMEM_LIMIT)


def to_owners(me, rows, depth, local):
    r = lax.broadcasted_iota(jnp.int32, (rows, rows), 0)
    c = lax.broadcasted_iota(jnp.int32, (rows, rows), 1)
    frames = rows // depth
    k = r // frames
    source = (r % frames) * depth + ((k // local) ^ me) * local + k % local
    return jnp.where(c == source, 1.0, 0.0).astype(bf16)


def from_owners(me, rows, depth, local):
    r = lax.broadcasted_iota(jnp.int32, (rows, rows), 0)
    c = lax.broadcasted_iota(jnp.int32, (rows, rows), 1)
    frames = rows // depth
    k = r % depth
    source = (((k // local) ^ me) * local + k % local) * frames + r // depth
    return jnp.where(c == source, 1.0, 0.0).astype(bf16)


def pick(blocks, index):
    out = blocks[0]
    for b in range(1, len(blocks)):
        out = jnp.where(index == b, blocks[b], out)
    return out


def row_to_column(row):
    n = row.shape[1]
    r = lax.broadcasted_iota(jnp.int32, (n, n), 0)
    c = lax.broadcasted_iota(jnp.int32, (n, n), 1)
    return jnp.sum(jnp.where(r == c, row, 0.0), axis=1, keepdims=True)


def column_to_row(column):
    n = column.shape[0]
    r = lax.broadcasted_iota(jnp.int32, (n, n), 0)
    c = lax.broadcasted_iota(jnp.int32, (n, n), 1)
    return jnp.sum(jnp.where(r == c, column, 0.0), axis=0, keepdims=True)


def pair_mask(live_row, half, depth):
    n = live_row.shape[1] // 2
    live = row_to_column(live_row[:, half * n : (half + 1) * n])
    r = lax.broadcasted_iota(jnp.int32, (n, n), 0)
    c = lax.broadcasted_iota(jnp.int32, (n, n), 1)
    allowed = ((r // depth) == (c // depth)) & (r <= c) & (live > 0.5)
    return jnp.concatenate([allowed, allowed], 1)


def split_heads(block):
    lane = lax.broadcasted_iota(jnp.int32, block.shape, 1)
    zero = jnp.zeros_like(block)
    return jnp.concatenate(
        [jnp.where(lane < HEAD_DIM, block, zero), jnp.where(lane >= HEAD_DIM, block, zero)], 0
    )


def join_heads(pair):
    n = pair.shape[0] // 2
    lane = lax.broadcasted_iota(jnp.int32, (n, pair.shape[1]), 1)
    return jnp.where(lane < HEAD_DIM, pair[:n], pair[n:])


def pair_probs(q2, k2, allowed):
    scores = jnp.where(allowed, dot(k2, q2, 1, 1), MASKED)
    e = jnp.exp(scores - jnp.max(scores, axis=0, keepdims=True))
    return e * (1.0 / jnp.sum(e, axis=0, keepdims=True))


def per_step(frames, step):
    return min(step, frames)


def place(back, pieces, f):
    local, _, part = pieces[0].shape
    blocks = [p[:, f].reshape(local * GROUP, part) for p in pieces]
    return dot(back, jnp.concatenate(blocks, 0), 1, 0)


def row_scale(pieces):
    total = None
    for x in pieces:
        xf = x.astype(f32)
        term = jnp.sum(xf * xf, axis=-1, keepdims=True)
        total = term if total is None else total + term
    return lax.rsqrt(total / (pieces[0].shape[1] * len(pieces)) + EPS)


def cot_kernel(count, idx_ref, cot_ref, live_ref, *outs):
    step, depth, part = cot_ref.shape
    rows = GROUP * depth
    local = depth // count
    move = to_owners(idx_ref[0], rows, depth, local)
    for g in range(step // GROUP):
        f = slice(g * GROUP, (g + 1) * GROUP)
        live = row_to_column(live_ref[g])
        masked = (cot_ref[f].reshape(rows, part).astype(f32) * live).astype(bf16)
        moved = dot(move, masked, 1, 0).astype(bf16).reshape(count, local, GROUP, part)
        for j in range(count):
            outs[j][:, f] = moved[j]


def split_cot(idx, cot, live, count):
    frames, depth, part = cot.shape
    local = depth // count
    step = per_step(frames, 64)
    return pl.pallas_call(
        functools.partial(cot_kernel, count),
        grid_spec=pltpu.PrefetchScalarGridSpec(
            num_scalar_prefetch=1,
            grid=(frames // step,),
            in_specs=[
                pl.BlockSpec((step, depth, part), lambda i, s: (i, 0, 0)),
                pl.BlockSpec((step // GROUP, 1, GROUP * depth), lambda i, s: (i, 0, 0)),
            ],
            out_specs=[pl.BlockSpec((local, step, part), lambda i, s: (0, i, 0))] * count,
        ),
        out_shape=[jax.ShapeDtypeStruct((local, frames, part), bf16)] * count,
        compiler_params=params(),
        cost_estimate=cost(4),
    )(idx, cot, live)


def attn_kernel(count, idx_ref, *refs):
    xs = refs[:count]
    w_ref, gain_ref, live_ref = refs[count : count + 3]
    qkv_ref, resid_ref = refs[count + 3 : count + 5]
    outs = refs[count + 5 :]
    me = idx_ref[0]
    step, depth, part = xs[0].shape
    rows = GROUP * depth
    local = depth // count
    half_rows = rows // 2
    move = to_owners(me, rows, depth, local)
    own = move[: local * GROUP]
    for g in range(step // GROUP):
        f = slice(g * GROUP, (g + 1) * GROUP)
        r = slice(g * rows, (g + 1) * rows)
        pieces = [x[f].reshape(rows, part) for x in xs]
        rms = row_scale(pieces)
        acc = [None] * 3
        for j in range(count):
            normed = (pieces[j].astype(f32) * rms * gain_ref[me ^ j]).astype(bf16)
            for c in range(3):
                term = dot(normed, w_ref[c, me ^ j], 1, 0)
                acc[c] = term if acc[c] is None else acc[c] + term
            moved = dot(own, pieces[j], 1, 0).astype(bf16)
            resid_ref[me ^ j, :, f] = moved.reshape(local, GROUP, part)
        q, k, v = [a.astype(bf16) for a in acc]
        qkv_ref[0, r], qkv_ref[1, r], qkv_ref[2, r] = q, k, v
        q = q * (HEAD_DIM**-0.5)
        mixed = []
        for half in range(2):
            allowed = pair_mask(live_ref[g], half, depth)
            sl = slice(half * half_rows, (half + 1) * half_rows)
            cols = []
            for pair in range(part // 128):
                ln = slice(pair * 128, (pair + 1) * 128)
                probs = pair_probs(split_heads(q[sl, ln]), k[sl, ln], allowed).astype(bf16)
                cols.append(join_heads(dot(probs, v[sl, ln], 0, 0)).astype(bf16))
            mixed.append(jnp.concatenate(cols, 1) if len(cols) > 1 else cols[0])
        mixed = jnp.concatenate(mixed, 0)
        moved = dot(move, mixed, 1, 0).astype(bf16).reshape(count, local, GROUP, part)
        for j in range(count):
            outs[j][:, f] = moved[j]


def attention(idx, xs, w, gain, live, chunk, chunks):
    count = len(xs)
    frames, depth, part = xs[0].shape
    local = depth // count
    frames = frames // chunks
    step = per_step(frames, STEP)
    n = frames // step
    base = chunk * n
    rows = step * depth
    return pl.pallas_call(
        functools.partial(attn_kernel, count),
        grid_spec=pltpu.PrefetchScalarGridSpec(
            num_scalar_prefetch=1,
            grid=(n,),
            in_specs=[pl.BlockSpec((step, depth, part), lambda i, s: (i + base, 0, 0))] * count
            + [
                pl.BlockSpec(w.shape, lambda i, s: (0, 0, 0, 0)),
                pl.BlockSpec(gain.shape, lambda i, s: (0, 0, 0)),
                pl.BlockSpec((step // GROUP, 1, GROUP * depth), lambda i, s: (i + base, 0, 0)),
            ],
            out_specs=[
                pl.BlockSpec((3, rows, part), lambda i, s: (0, i, 0)),
                pl.BlockSpec((count, local, step, part), lambda i, s: (0, 0, i, 0)),
            ]
            + [pl.BlockSpec((local, step, part), lambda i, s: (0, i, 0))] * count,
        ),
        out_shape=[
            jax.ShapeDtypeStruct((3, frames * depth, part), bf16),
            jax.ShapeDtypeStruct((count, local, frames, part), bf16),
        ]
        + [jax.ShapeDtypeStruct((local, frames, part), bf16)] * count,
        compiler_params=params(),
        cost_estimate=cost(8),
    )(idx, *xs, w, gain, live)


def half_specs(local, frames, width):
    half = local // 2
    return [
        pl.BlockSpec((1, frames, width), lambda k, *s: (jnp.minimum(k, half - 1), 0, 0)),
        pl.BlockSpec((1, frames, width), lambda k, *s: (jnp.maximum(k - half, 0), 0, 0)),
    ]


def store_half(is_first, first_ref, second_ref, at, value):
    @pl.when(is_first)
    def _():
        first_ref[at] = value

    @pl.when(jnp.logical_not(is_first))
    def _():
        second_ref[at] = value


def load_half(is_first, first_ref, second_ref):
    return jnp.where(is_first, first_ref[0], second_ref[0])


def project_kernel(count, chunks, idx_ref, *refs):
    mixed = refs[: count * chunks]
    resids = refs[count * chunks : (count + 1) * chunks]
    w_ref, gain_ref, hidden_ref, norm_ref = refs[(count + 1) * chunks :]
    me = idx_ref[0]
    size = mixed[0].shape[1]
    for c in range(chunks):
        f = slice(c * size, (c + 1) * size)
        hidden = jnp.concatenate([resids[c][b, 0] for b in range(count)], 1).astype(f32)
        for j in range(count):
            hidden = hidden + dot(mixed[c * count + j][0], w_ref[me ^ j], 1, 0)
        hidden_ref[0, f] = hidden
        rms = lax.rsqrt(jnp.mean(hidden * hidden, axis=-1, keepdims=True) + EPS)
        norm_ref[0, f] = (hidden * rms * gain_ref[0]).astype(bf16)


def project(idx, mixed, resids, w, gain):
    chunks, count = len(mixed), len(mixed[0])
    local, size, part = mixed[0][0].shape
    frames, width = size * chunks, part * count
    each = pl.BlockSpec((1, frames, width), lambda k, s: (k, 0, 0))
    return pl.pallas_call(
        functools.partial(project_kernel, count, chunks),
        grid_spec=pltpu.PrefetchScalarGridSpec(
            num_scalar_prefetch=1,
            grid=(local,),
            in_specs=[pl.BlockSpec((1, size, part), lambda k, s: (k, 0, 0))] * (count * chunks)
            + [pl.BlockSpec((count, 1, size, part), lambda k, s: (0, k, 0, 0))] * chunks
            + [
                pl.BlockSpec(w.shape, lambda k, s: (0, 0, 0)),
                pl.BlockSpec((1, 1, width), lambda k, s: (k, 0, 0)),
            ],
            out_specs=[each, each],
        ),
        out_shape=[
            jax.ShapeDtypeStruct((local, frames, width), f32),
            jax.ShapeDtypeStruct((local, frames, width), bf16),
        ],
        compiler_params=params(),
        cost_estimate=cost(6),
    )(idx, *[m for part_ in mixed for m in part_], *resids, w, gain)


def load_block(is_first, refs):
    return refs[0][0] if len(refs) == 1 else load_half(is_first, *refs)


def block_parts(block):
    return list(block) if isinstance(block, tuple) else [block]


def ffn_kernel(sizes, idx_ref, *refs):
    n = len(sizes) // 2
    ins = sum(sizes)
    w_ref = refs[ins]
    dnorms, branches = refs[ins + 1 : ins + 1 + 2 * n], refs[ins + 1 + 2 * n : ins + 1 + 3 * n]
    act_ref = refs[-1]
    is_first = pl.program_id(0) < pl.num_programs(0) // 2
    blocks, at = [], 0
    for size in sizes:
        blocks.append(load_block(is_first, refs[at : at + size]))
        at += size
    frames = blocks[0].shape[0]
    norm = jnp.concatenate(blocks[:n], 0)
    grad = jnp.concatenate(blocks[n:], 0)
    gate = dot(norm, w_ref[0, 0], 1, 1)
    up = dot(norm, w_ref[0, 1], 1, 1)
    dact = dot(grad, w_ref[0, 2], 1, 1)
    sig = jax.nn.sigmoid(gate)
    silu = gate * sig
    act = (silu * up).astype(bf16)
    dgate = (dact * up * sig * (1.0 + gate * (1.0 - sig))).astype(bf16)
    dup = (dact * silu).astype(bf16)
    act_ref[0, 0] = dgate
    act_ref[0, 1] = dup
    act_ref[0, 2] = act
    dnorm = (dot(dgate, w_ref[0, 0], 1, 0) + dot(dup, w_ref[0, 1], 1, 0)).astype(bf16)
    branch = dot(act, w_ref[0, 2], 1, 0).astype(bf16)
    for i in range(n):
        rows = slice(i * frames, (i + 1) * frames)
        store_half(is_first, *dnorms[2 * i : 2 * i + 2], 0, dnorm[rows])
        branches[i][0] = branch[rows]


def ffn(idx, norms, grads, w):
    n = len(norms)
    blocks = [block_parts(v) for v in (*norms, *grads)]
    local, _, hidden, width = w.shape
    frames = blocks[0][0].shape[1]
    halves = half_specs(local, frames, width)
    whole = [pl.BlockSpec((1, frames, width), lambda k, s: (k, 0, 0))]
    *out, act = pl.pallas_call(
        functools.partial(ffn_kernel, [len(v) for v in blocks]),
        grid_spec=pltpu.PrefetchScalarGridSpec(
            num_scalar_prefetch=1,
            grid=(local,),
            in_specs=[x for v in blocks for x in (whole if len(v) == 1 else halves)]
            + [pl.BlockSpec((1, 3, hidden, width), lambda k, s: (k, 0, 0, 0))],
            out_specs=halves * n
            + whole * n
            + [pl.BlockSpec((1, 3, n * frames, hidden), lambda k, s: (k, 0, 0, 0))],
        ),
        out_shape=[jax.ShapeDtypeStruct((local // 2, frames, width), bf16)] * (2 * n)
        + [jax.ShapeDtypeStruct((local, frames, width), bf16)] * n
        + [jax.ShapeDtypeStruct((local, 3, n * frames, hidden), bf16)],
        compiler_params=params(),
        cost_estimate=cost(3.5 + 5 * n),
    )(idx, *[x for v in blocks for x in v], w)
    pairs = [out[i : i + 2] for i in range(0, 2 * n, 2)]
    return pairs, out[2 * n :], act


def weight_kernel(n, row, sizes, idx_ref, *refs):
    acts, out_ref = refs[:n], refs[-1]
    local = acts[0].shape[0]
    others, at = [], n
    for size in sizes:
        others.append(refs[at : at + size])
        at += size
    frames = others[0][0].shape[1]

    def entry(block, k):
        return block[k // block[0].shape[0]][k % block[0].shape[0]]

    for k in range(local):
        total, first = None, 0
        for a in acts:
            size = a.shape[2] // frames
            both = [entry(others[first + i], k) for i in range(size)]
            first += size
            both = jnp.concatenate(both, 0) if size > 1 else both[0]
            term = dot(a[k, 0], both, 0, 0)
            total = term if total is None else total + term
        out_ref[:, 0, k] = total


def weight_grad(idx, acts, others, row, out):
    n = len(acts)
    local, _, _, hidden = acts[0].shape
    chunk = min(128, hidden)
    others = [block_parts(v) for v in others]
    width = others[0][0].shape[2]
    ins = list(acts) + [x for v in others for x in v]
    specs = [
        pl.BlockSpec((local, 1, a.shape[2], chunk), lambda c, s: (0, row, 0, c)) for a in acts
    ] + [
        pl.BlockSpec(x.shape, lambda c, s: (0, 0, 0), pipeline_mode=pl.Buffered(1))
        for v in others
        for x in v
    ]
    aliases = {}
    kernel = functools.partial(weight_kernel, n, row, [len(v) for v in others])
    if out is not None:
        aliases = {1 + len(ins): 0}
        ins.append(out)
        specs.append(pl.BlockSpec(memory_space=pl.ANY))
    return pl.pallas_call(
        kernel,
        grid_spec=pltpu.PrefetchScalarGridSpec(
            num_scalar_prefetch=1,
            grid=(hidden // chunk,),
            in_specs=specs,
            out_specs=pl.BlockSpec((chunk, 1, local, width), lambda c, s: (c, row, 0, 0)),
        ),
        out_shape=jax.ShapeDtypeStruct((hidden, 3, local, width), f32),
        input_output_aliases=aliases,
        compiler_params=params(),
        cost_estimate=cost(12),
    )(idx, *ins)


def add_low(x, y):
    return (x.astype(f32) + y.astype(f32)).astype(bf16)


def merge_kernel(n, idx_ref, *refs):
    for i in range(n):
        refs[2 * n + i][...] = add_low(refs[i][...], refs[n + i][...])


def merge(idx, mine, moved):
    n = len(mine)
    half, frames, width = mine[0].shape
    each = pl.BlockSpec((1, frames, width), lambda k, s: (k, 0, 0))
    return pl.pallas_call(
        functools.partial(merge_kernel, n),
        grid_spec=pltpu.PrefetchScalarGridSpec(
            num_scalar_prefetch=1,
            grid=(half,),
            in_specs=[each] * (2 * n),
            out_specs=[each] * n,
        ),
        out_shape=[jax.ShapeDtypeStruct(mine[0].shape, bf16)] * n,
        compiler_params=params(),
        cost_estimate=cost(1.2 * n),
    )(idx, *mine, *moved)


def whole_kernel(half, idx_ref, f_ref, b_ref, up_ref, down_ref, fo_ref, bo_ref):
    if half is None:
        fo_ref[...] = add_low(f_ref[...], up_ref[...])
        bo_ref[...] = add_low(b_ref[...], down_ref[...])
        return
    is_first = pl.program_id(0) < half
    fo_ref[...] = jnp.where(is_first, add_low(f_ref[...], up_ref[...]), f_ref[...])
    bo_ref[...] = jnp.where(is_first, b_ref[...], add_low(b_ref[...], down_ref[...]))


def merge_whole(idx, f, b, up, down):
    local, frames, width = f.shape
    half = None if up.shape == f.shape else local // 2
    each = pl.BlockSpec((1, frames, width), lambda k, s: (k, 0, 0))
    moved = half_specs(local, frames, width) if half else [each] * 2
    return pl.pallas_call(
        functools.partial(whole_kernel, half),
        grid_spec=pltpu.PrefetchScalarGridSpec(
            num_scalar_prefetch=1,
            grid=(local,),
            in_specs=[each, each, *moved],
            out_specs=[each, each],
        ),
        out_shape=[jax.ShapeDtypeStruct(f.shape, bf16)] * 2,
        compiler_params=params(),
        cost_estimate=cost(4),
    )(idx, f, b, up, down)


def sum_halves(refs):
    is_first = pl.program_id(0) < pl.num_programs(0) // 2
    total = None
    for i in range(0, len(refs), 2):
        term = load_half(is_first, *refs[i : i + 2]).astype(f32)
        total = term if total is None else total + term
    return total


def resid_kernel(count, idx_ref, *refs):
    hidden_ref, branch_ref, gain_ref, w_ref, low_ref, gsum_ref = refs[6:12]
    dms, dhs = refs[12 : 12 + count], refs[12 + count :]
    me = idx_ref[0]
    part = w_ref.shape[1]
    dnorm = sum_halves(refs[:6])
    hidden = hidden_ref[0]
    rms = lax.rsqrt(jnp.mean(hidden * hidden, axis=-1, keepdims=True) + EPS)
    xhat = hidden * rms
    gsum_ref[0] = jnp.sum(dnorm * xhat, axis=0, keepdims=True)
    u = dnorm * gain_ref[0]
    inner = jnp.mean(xhat * u, axis=-1, keepdims=True)
    low = (branch_ref[0].astype(f32) + rms * (u - xhat * inner)).astype(bf16)
    low_ref[0] = low
    blocks = [low[:, b * part : (b + 1) * part] for b in range(count)]
    for j in range(count):
        dhs[j][0] = pick(blocks, me ^ j)
        dms[j][0] = dot(low, w_ref[me ^ j], 1, 1).astype(bf16)


def resid_grad(idx, recv, own, hidden, branch, gain, w):
    count, part, width = w.shape
    local, frames, _ = hidden.shape
    each = pl.BlockSpec((1, frames, width), lambda k, s: (k, 0, 0))
    return pl.pallas_call(
        functools.partial(resid_kernel, count),
        grid_spec=pltpu.PrefetchScalarGridSpec(
            num_scalar_prefetch=1,
            grid=(local,),
            in_specs=half_specs(local, frames, width) * 3
            + [each] * 2
            + [
                pl.BlockSpec((1, 1, width), lambda k, s: (k, 0, 0)),
                pl.BlockSpec(w.shape, lambda k, s: (0, 0, 0)),
            ],
            out_specs=[each, pl.BlockSpec((1, 1, width), lambda k, s: (k, 0, 0))]
            + [pl.BlockSpec((1, frames, part), lambda k, s: (k, 0, 0))] * (2 * count),
        ),
        out_shape=[
            jax.ShapeDtypeStruct((local, frames, width), bf16),
            jax.ShapeDtypeStruct((local, 1, width), f32),
        ]
        + [jax.ShapeDtypeStruct((local, frames, part), bf16)] * (2 * count),
        compiler_params=params(),
        cost_estimate=cost(8),
    )(idx, *recv, *own, hidden, branch, gain, w)


def attn_back_kernel(count, ring, idx_ref, *refs):
    xs = refs[:count]
    dms = refs[count : 2 * count]
    qkv_ref, w_ref, gain_ref, live_ref = refs[2 * count : 2 * count + 4]
    keep_ref, send_ref, wlow_ref, gsum_ref, wsum_ref = refs[2 * count + 4 :]
    me = idx_ref[0]
    step, depth, part = xs[0].shape
    rows = GROUP * depth
    back = from_owners(me, rows, depth, depth // count)
    half_rows = rows // 2
    factor = HEAD_DIM**-0.5

    @pl.when(pl.program_id(0) == 0)
    def _():
        wsum_ref[...] = jnp.zeros_like(wsum_ref)
        gsum_ref[...] = jnp.zeros_like(gsum_ref)

    every, rmss = [[], [], []], []
    for g in range(step // GROUP):
        f = slice(g * GROUP, (g + 1) * GROUP)
        r = slice(g * rows, (g + 1) * rows)
        dmixed = place(back, dms, f).astype(bf16)
        q, k, v = qkv_ref[0, r] * factor, qkv_ref[1, r], qkv_ref[2, r]
        for half in range(2):
            allowed = pair_mask(live_ref[g], half, depth)
            sl = slice(half * half_rows, (half + 1) * half_rows)
            cols = [[], [], []]
            for pair in range(part // 128):
                ln = slice(pair * 128, (pair + 1) * 128)
                q2, k2, v2 = split_heads(q[sl, ln]), k[sl, ln], v[sl, ln]
                dm2 = split_heads(dmixed[sl, ln])
                probs = pair_probs(q2, k2, allowed)
                dprobs = dot(v2, dm2, 1, 1)
                inner = jnp.sum(probs * dprobs, axis=0, keepdims=True)
                ds = (probs * (dprobs - inner)).astype(bf16)
                cols[0].append((join_heads(dot(ds, k2, 0, 0)) * factor).astype(bf16))
                cols[1].append(dot(ds, q2, 1, 0).astype(bf16))
                cols[2].append(dot(probs.astype(bf16), dm2, 1, 0).astype(bf16))
            for c in range(3):
                every[c].append(jnp.concatenate(cols[c], 1) if len(cols[c]) > 1 else cols[c][0])
    dqkv = [jnp.concatenate(p, 0) for p in every]
    rows = step * depth
    pieces = [x[...].reshape(rows, part) for x in xs]
    rms = row_scale(pieces)
    inner = jnp.zeros((rows, 1), f32)
    for j in range(count):
        owner = me ^ j
        xhat = pieces[j].astype(f32) * rms
        scaled = xhat * gain_ref[owner]
        normed = scaled.astype(bf16)
        dn = jnp.zeros((rows, part), f32)
        for c in range(3):
            dn = dn + dot(dqkv[c], w_ref[c, owner], 1, 1)
            wsum_ref[c, owner] += dot(normed, dqkv[c], 0, 0)
        inner = inner + jnp.sum(scaled * dn, axis=-1, keepdims=True)
        gsum_ref[owner] += jnp.sum(dn * xhat, axis=0, keepdims=True)
        (send_ref if j & 1 else keep_ref)[j // 2, :rows] = dn.astype(bf16)
    size = GROUP * depth
    lines = [column_to_row(inner[g * size : (g + 1) * size]) for g in range(step // GROUP)]
    lines = [line[:, i : i + part] for line in lines for i in range(0, size, part)]
    lines.append(jnp.zeros((EXTRA - len(lines), part), f32))
    lines = jnp.concatenate(lines, 0).astype(bf16)
    for i in range(count // 2):
        send_ref[i, rows:] = lines
        keep_ref[i, rows:] = lines

    @pl.when(pl.program_id(0) == pl.num_programs(0) - 1)
    def _():
        size = part * count // ring
        for i in range(ring):
            block, line = i * size // part, i * size % part
            for c in range(3):
                wlow_ref[i, c * size : (c + 1) * size] = wsum_ref[
                    c, block, line : line + size
                ].astype(bf16)


def attention_back(idx, xs, dms, qkv, w, gain, live, ring):
    count = len(xs)
    frames, depth, part = xs[0].shape
    local = dms[0].shape[0]
    step = per_step(frames, STEP)
    n = frames // step
    rows = step * depth
    low_shape = (ring, 3 * part * count // ring, part)
    lives = pl.BlockSpec((step // GROUP, 1, GROUP * depth), lambda i, s: (i, 0, 0))
    return pl.pallas_call(
        functools.partial(attn_back_kernel, count, ring),
        grid_spec=pltpu.PrefetchScalarGridSpec(
            num_scalar_prefetch=1,
            grid=(n,),
            in_specs=[pl.BlockSpec((step, depth, part), lambda i, s: (i, 0, 0))] * count
            + [pl.BlockSpec((local, step, part), lambda i, s: (0, i, 0))] * count
            + [
                pl.BlockSpec((3, rows, part), lambda i, s: (0, i, 0)),
                pl.BlockSpec(w.shape, lambda i, s: (0, 0, 0, 0)),
                pl.BlockSpec(gain.shape, lambda i, s: (0, 0, 0)),
                lives,
            ],
            out_specs=[pl.BlockSpec((count // 2, rows + EXTRA, part), lambda i, s: (0, i, 0))] * 2
            + [
                pl.BlockSpec(low_shape, lambda i, s: (0, 0, 0)),
                pl.BlockSpec((count, 1, part), lambda i, s: (0, 0, 0)),
            ],
            scratch_shapes=[pltpu.VMEM(w.shape, f32)],
        ),
        out_shape=[jax.ShapeDtypeStruct((count // 2, n * (rows + EXTRA), part), bf16)] * 2
        + [
            jax.ShapeDtypeStruct(low_shape, bf16),
            jax.ShapeDtypeStruct((count, 1, part), f32),
        ],
        compiler_params=params(),
        cost_estimate=cost(26),
    )(idx, *xs, *dms, qkv, w, gain, live)


def fold_kernel(n, idx_ref, *refs):
    total = refs[0][...].astype(f32)
    for r in refs[1:n]:
        total = total + r[...].astype(f32)
    refs[n][...] = total.astype(bf16)


def fold(idx, terms, bit):
    n = len(terms)
    _, rows, part = terms[0].shape
    hop = bit // 2

    def spec(i):
        step = 1 if i < 2 else 1 << (i - 1)
        return pl.BlockSpec((1, rows, part), lambda g, s: (hop * (2 * g + 1) // step, 0, 0))

    return pl.pallas_call(
        functools.partial(fold_kernel, n),
        grid_spec=pltpu.PrefetchScalarGridSpec(
            num_scalar_prefetch=1,
            grid=(terms[0].shape[0] // bit,),
            in_specs=[spec(i) for i in range(n)],
            out_specs=pl.BlockSpec((1, rows, part), lambda g, s: (g, 0, 0)),
        ),
        out_shape=jax.ShapeDtypeStruct((terms[0].shape[0] // bit, rows, part), bf16),
        compiler_params=params(),
        cost_estimate=cost(2),
    )(idx, *terms)


def out_kernel(count, chunks, idx_ref, *refs):
    low_ref, outs = refs[count * chunks], refs[count * chunks + 1 :]
    local, size, _ = refs[0].shape
    width = low_ref.shape[2]
    lows = []
    for c in range(chunks):
        part_ = low_ref[:, c * size : (c + 1) * size]
        lows.append(part_.reshape(local * size, width))
    low = jnp.concatenate(lows, 0)
    for j in range(count):
        mine = [refs[c * count + j][...].reshape(local * size, -1) for c in range(chunks)]
        out = dot(jnp.concatenate(mine, 0), low, 0, 0).astype(bf16)
        if j & 1:
            outs[-1][j // 2] = out
        else:
            outs[j // 2][...] = out


def out_terms(idx, mixeds, low):
    chunks, count = len(mixeds), len(mixeds[0])
    part, width = mixeds[0][0].shape[2], low.shape[2]
    return pl.pallas_call(
        functools.partial(out_kernel, count, chunks),
        grid_spec=pltpu.PrefetchScalarGridSpec(
            num_scalar_prefetch=1,
            grid=(1,),
            in_specs=[pl.BlockSpec(m.shape, lambda i, s: (0, 0, 0)) for p in mixeds for m in p]
            + [pl.BlockSpec(low.shape, lambda i, s: (0, 0, 0))],
            out_specs=[pl.BlockSpec((part, width), lambda i, s: (0, 0))] * (count // 2)
            + [pl.BlockSpec((count // 2, part, width), lambda i, s: (0, 0, 0))],
        ),
        out_shape=[jax.ShapeDtypeStruct((part, width), bf16)] * (count // 2)
        + [jax.ShapeDtypeStruct((count // 2, part, width), bf16)],
        compiler_params=params(),
        cost_estimate=cost(6),
    )(idx, *[m for p in mixeds for m in p], low)


def input_kernel(count, terms_count, idx_ref, *refs):
    xs = refs[:count]
    dhs = refs[count : 2 * count]
    terms = refs[2 * count : 2 * count + terms_count]
    gain_ref, out_ref = refs[2 * count + terms_count :]
    me = idx_ref[0]
    step, depth, part = xs[0].shape
    rows = GROUP * depth
    back = from_owners(me, rows, depth, depth // count)
    sums = terms[0][0, step * depth :].astype(f32)
    for t in terms[1:]:
        sums = sums + t[0, step * depth :].astype(f32)
    lines = rows // part
    for g in range(step // GROUP):
        f = slice(g * GROUP, (g + 1) * GROUP)
        r = slice(g * rows, (g + 1) * rows)
        resid = place(back, dhs, f)
        pieces = [x[f].reshape(rows, part) for x in xs]
        rms = row_scale(pieces)
        xhat = pieces[0].astype(f32) * rms
        dn = terms[0][0, r].astype(f32)
        for t in terms[1:]:
            dn = dn + t[0, r].astype(f32)
        line = [sums[i : i + 1] for i in range(g * lines, (g + 1) * lines)]
        line = jnp.concatenate(line, 1) if lines > 1 else line[0]
        inner = row_to_column(line) / (part * count)
        out = resid + rms * (dn * gain_ref[me] - xhat * inner)
        out_ref[f] = out.astype(bf16).reshape(GROUP, depth, part)


def input_grad(idx, xs, dhs, terms, gain, chunk, chunks):
    count = len(xs)
    frames, depth, part = xs[0].shape
    local = dhs[0].shape[0]
    frames = frames // chunks
    step = per_step(frames, STEP)
    n = frames // step
    base = chunk * n
    rows = step * depth
    return pl.pallas_call(
        functools.partial(input_kernel, count, len(terms)),
        grid_spec=pltpu.PrefetchScalarGridSpec(
            num_scalar_prefetch=1,
            grid=(n,),
            in_specs=[pl.BlockSpec((step, depth, part), lambda i, s: (i + base, 0, 0))] * count
            + [pl.BlockSpec((local, step, part), lambda i, s: (0, i + base, 0))] * count
            + [pl.BlockSpec((1, rows + EXTRA, part), lambda i, s: (0, i, 0))] * len(terms)
            + [pl.BlockSpec(gain.shape, lambda i, s: (0, 0, 0))],
            out_specs=pl.BlockSpec((step, depth, part), lambda i, s: (i, 0, 0)),
        ),
        out_shape=jax.ShapeDtypeStruct((frames, depth, part), bf16),
        compiler_params=params(),
        cost_estimate=cost(4),
    )(idx, *xs, *dhs, *terms, gain)


def block_kernel(count, idx_ref, *refs):
    up, down, own, hidden_ref, live_ref = refs[:5]
    outs = refs[5:]
    me = idx_ref[0]
    part = outs[0].shape[2]
    branch = up[0].astype(f32) + down[0].astype(f32) + own[0].astype(f32)
    rows = ((hidden_ref[0] + branch) * row_to_column(live_ref[0])).astype(bf16)
    blocks = [rows[:, b * part : (b + 1) * part] for b in range(count)]
    for j in range(count):
        outs[j][0] = pick(blocks, me ^ j)


def block_rows(idx, recv, own, hidden, live, count):
    local, frames, width = hidden.shape
    part = width // count
    each = pl.BlockSpec((1, frames, width), lambda k, s: (k, 0, 0))
    return pl.pallas_call(
        functools.partial(block_kernel, count),
        grid_spec=pltpu.PrefetchScalarGridSpec(
            num_scalar_prefetch=1,
            grid=(local,),
            in_specs=[each] * 4 + [pl.BlockSpec((1, 1, frames), lambda k, s: (k, 0, 0))],
            out_specs=[pl.BlockSpec((1, frames, part), lambda k, s: (k, 0, 0))] * count,
        ),
        out_shape=[jax.ShapeDtypeStruct((local, frames, part), bf16)] * count,
        compiler_params=params(),
        cost_estimate=cost(4),
    )(idx, *recv, own, hidden, live)


def gather_kernel(count, idx_ref, *refs):
    pieces, out_ref = refs[:count], refs[count]
    step, depth, part = out_ref.shape
    back = from_owners(idx_ref[0], GROUP * depth, depth, depth // count)
    for g in range(step // GROUP):
        f = slice(g * GROUP, (g + 1) * GROUP)
        out = place(back, pieces, f)
        out_ref[f] = out.astype(bf16).reshape(GROUP, depth, part)


def gather_block(idx, pieces):
    count = len(pieces)
    local, frames, part = pieces[0].shape
    depth = local * count
    step = per_step(frames, 64)
    return pl.pallas_call(
        functools.partial(gather_kernel, count),
        grid_spec=pltpu.PrefetchScalarGridSpec(
            num_scalar_prefetch=1,
            grid=(frames // step,),
            in_specs=[pl.BlockSpec((local, step, part), lambda i, s: (0, i, 0))] * count,
            out_specs=pl.BlockSpec((step, depth, part), lambda i, s: (i, 0, 0)),
        ),
        out_shape=jax.ShapeDtypeStruct((frames, depth, part), bf16),
        compiler_params=params(),
        cost_estimate=cost(4),
    )(idx, *pieces)


class Order:
    def __init__(self):
        self.last = []

    def tie(self, *values, after=()):
        flat, tree = jax.tree.flatten(values)
        held = [*self.last, *jax.tree.leaves(after)]
        if held:
            flat = lax.optimization_barrier((*flat, *held))[: len(flat)]
        values = jax.tree.unflatten(tree, flat)
        return values[0] if len(values) == 1 else values

    def run(self, kernel, first, *args, after=()):
        out = kernel(self.tie(first, after=after), *args)
        self.last = [min(jax.tree.leaves(out), key=lambda v: v.size)]
        return out

    def fuse(self, step, *args, after=()):
        args = self.tie(*args, after=after)
        out = step(*args) if isinstance(args, tuple) else step(args)
        self.last = jax.tree.leaves(out)
        return out

    def send(self, value, axis, pairs):
        return lax.ppermute(self.tie(value), axis, pairs)

    def swap(self, value, bits, axis="pos"):
        count = lax.axis_size(axis)
        return self.send(value, axis, [(i, i ^ bits) for i in range(count)])

    def exchange(self, pieces):
        back = {j: self.swap(pieces[j], j) for j in range(len(pieces) - 1, 0, -1)}
        return [pieces[0]] + [back[j] for j in range(1, len(pieces))]


def ring_steps(count):
    order = list(range(0, count, 2)) + list(range(count - 1, 0, -2))
    forward = [(order[i], order[(i + 1) % count]) for i in range(count)]
    return forward, [(b, a) for a, b in forward]


class RingGather:
    def __init__(self, order, count, value):
        self.order, self.count = order, count
        self.forward, self.back = ring_steps(count)
        self.blocks = [value] + [None] * (count - 1)

    def step(self, s):
        count, blocks = self.count, self.blocks
        up, down = blocks[s - 1], blocks[(count - s + 1) % count]
        if s == count // 2:
            half = up.shape[0] // 2
            up, down = up[:half], down[half:]
        up = self.order.send(up, "frames", self.forward)
        down = self.order.send(down, "frames", self.back)
        if s < count // 2:
            blocks[s], blocks[count - s] = up, down
        else:
            blocks[s] = (up, down)

    def received(self, s):
        return [self.blocks[s], self.blocks[self.count - s]]


class RingSumWhole:
    def __init__(self, order, count, blocks, idx):
        self.order, self.count, self.blocks, self.idx = order, count, blocks, idx
        self.forward, self.back = ring_steps(count)

    def step(self, s, after=()):
        count, far = self.count, self.count // 2
        if s == 1:
            block = self.blocks[far]
            half = block.shape[0] // 2
            f, b = block[:half], block[half:]
        else:
            h = far - s + 1
            f, b = self.order.run(
                merge_whole, self.idx, self.blocks[count - h], self.blocks[h], *self.parts, after=after
            )
        self.parts = [
            self.order.send(f, "frames", self.forward),
            self.order.send(b, "frames", self.back),
        ]


class RingSum:
    def __init__(self, order, count, blocks, idx):
        self.order, self.count, self.blocks, self.idx = order, count, blocks, idx
        self.forward, self.back = ring_steps(count)
        self.parts = {}

    def step(self, chains, s, after=()):
        count, far = self.count, self.count // 2
        mine = []
        for chain in chains:
            h = far - s + 1 if chain == "x" else far - s
            first, second = (0, 1) if chain == "x" else (1, 0)
            mine += [self.blocks[(count - h) % count][first], self.blocks[h][second]]
        if s > 1:
            moved = [p for chain in chains for p in self.parts[chain]]
            mine = self.order.run(merge, self.idx, mine, moved, after=after)
        for i, chain in enumerate(chains):
            self.parts[chain] = [
                self.order.send(mine[2 * i], "frames", self.forward),
                self.order.send(mine[2 * i + 1], "frames", self.back),
            ]

    def received(self):
        return [self.parts["x"][0], self.parts["y"][0], self.parts["y"][1], self.parts["x"][1]]


CHUNKS = 1


def body(inputs, counts, gain_attn, weight_qkv, weight_out, gain_ffn, weight_ffn, cotangent):
    count = lax.axis_size("pos")
    ring = lax.axis_size("frames")
    far = ring // 2
    me = lax.axis_index("pos")
    idx = me.astype(jnp.int32).reshape(1)
    frames, depth, part = inputs.shape
    width = part * count
    local = depth // count
    half = local // 2
    order = Order()

    positions = jnp.arange(depth, dtype=jnp.int32)
    live = (positions[None, :] < counts[:, None]).astype(f32)
    live_rows = live.reshape(frames // GROUP, 1, GROUP * depth)
    live_own = lax.dynamic_slice_in_dim(live, me * local, local, 1).T.reshape(local, 1, frames)
    w_qkv = weight_qkv.transpose(1, 0, 2).reshape(3, count, part, part)
    w_out = weight_out.reshape(count, part, width)
    gain1 = gain_attn.reshape(count, 1, part)
    gain2 = gain_ffn.reshape(local, 1, width)
    distance = me ^ jnp.arange(count)

    def in_order(blocks):
        return jnp.take(blocks, distance, axis=0, mode="clip")

    cots = order.exchange(order.run(split_cot, idx, cotangent, live_rows, count))
    w_ffn = order.fuse(lambda w: w.transpose(1, 2, 0, 3), weight_ffn)

    def assemble(first, *rest):
        rows = in_order(jnp.stack([first, *rest])).transpose(1, 2, 0, 3)
        return rows.reshape(local, frames, width)

    branch = order.fuse(assemble, *cots)
    grads = RingGather(order, ring, branch)
    grads.step(1)

    xs = {0: inputs}
    bit = count // 2
    while bit:
        for j in list(xs):
            xs[j ^ bit] = order.swap(xs[j], bit)
        bit //= 2
    xs = [xs[j] for j in range(count)]
    grads.step(2)
    qkv, resid, *mixed = order.run(
        attention, idx, xs, w_qkv, gain1, live_rows, 0, 1, after=grads.received(1)
    )
    mixed = order.exchange(mixed)
    grads.step(3)
    hidden, norm = order.run(
        project, idx, [mixed], [resid], w_out, gain2, after=grads.received(2)
    )
    norms = RingGather(order, ring, norm)
    norms.step(1)

    groups = [[0]] + [[s, ring - s] for s in range(1, far)] + [[far]]
    dnorms, branches, acts = [None] * ring, [None] * ring, []

    def feed(s, after=()):
        group = groups[s]
        down, forth, act = order.run(
            ffn,
            idx,
            [norms.blocks[d] for d in group],
            [grads.blocks[d] for d in group],
            w_ffn,
            after=after,
        )
        for i, d in enumerate(group):
            dnorms[d], branches[d] = down[i], forth[i]
        acts.append(act)

    feed(0, after=grads.received(3))
    for s in range(4, far + 1):
        grads.step(s)
    for s in range(2, far + 1):
        norms.step(s)
        feed(s - 1)

    totals = {}

    def weights(row):
        for q in range(0, far + 1, 6):
            chosen = range(q, min(q + 6, far + 1))
            source = (grads if row == 2 else norms).blocks
            totals[q] = order.run(
                weight_grad,
                idx,
                [acts[i] for i in chosen],
                [source[d] for i in chosen for d in groups[i]],
                row,
                totals.get(q),
            )

    dnorm = RingSum(order, ring, dnorms, idx)
    forth = RingSumWhole(order, ring, branches, idx)
    dnorm.step("y", 1)
    feed(far)
    dnorm.step("x", 1)
    for s in range(2, far):
        dnorm.step("y", s)
        dnorm.step("x", s)
    dnorm.step("x", far)
    forth.step(1)

    low, gsum, *rest = order.run(
        resid_grad, idx, dnorm.received(), dnorms[0], hidden, branch, gain2, w_out
    )
    bits = [1 << i for i in range((count - 1).bit_length())]

    dms = order.exchange(rest[:count])
    *stay, going = order.run(out_terms, idx, [mixed], low)

    def out_sum(stay, moved):
        shape = (2, part // 2, width)
        mine = [v.reshape(shape) for v in stay]
        moved = [moved[i].reshape(shape) for i in range(len(stay))]
        return [v.reshape(part, width) for v in order.run(merge, idx, mine, moved)]

    rows = width // ring

    def pack(out, gsum):
        columns = gsum.reshape(local, ring, rows).transpose(1, 0, 2).reshape(ring, 1, local * rows)
        columns = jnp.pad(columns, ((0, 0), (0, 0), (0, -(local * rows) % width)))
        pieces = [out.reshape(ring, part // ring, width), columns.reshape(ring, -1, width)]
        return jnp.concatenate([p.astype(bf16) for p in pieces], 1)

    forth.step(2, after=dms)
    dhs = order.exchange(rest[count:])
    keep, send, qkv_low, gain_sum = order.run(
        attention_back, idx, xs, dms, qkv, w_qkv, gain1, live_rows, ring
    )
    forth.step(3, after=dhs)
    out_moved = order.swap(going, 1)
    sums = [keep, order.swap(send, 1)]
    outs = out_sum(stay, out_moved)
    for bit in bits[1:]:
        out_moved = order.swap(jnp.stack(outs[1::2]), bit)
        sums.append(order.swap(order.run(fold, idx, sums, bit), bit))
        outs = out_sum(outs[0::2], out_moved)
    packed = order.fuse(pack, outs[0], gsum)
    packed = lax.all_to_all(packed, "frames", 0, 0, tiled=True)
    weights(1)
    for s in range(4, far + 1):
        forth.step(s)
    weights(2)
    packed = order.fuse(lambda m: jnp.sum(m.astype(f32), axis=0), packed)
    out_low = packed[: part // ring].astype(bf16)
    gain_ffn_grad = packed[part // ring :].reshape(-1)[: local * rows]

    def both(a, b):
        return jnp.concatenate([a, b], 0)

    def unmix(blocks, axis, bits):
        have = [0]
        for bit in bits:
            have = have + [j ^ bit for j in have]
        inverse = jnp.array([have.index(j) for j in range(len(have))])
        places = jnp.take(inverse, lax.axis_index(axis) ^ jnp.arange(len(have)), mode="clip")
        return jnp.take(blocks, places, axis=0, mode="clip")

    def join(a, b, c, d):
        return both(a, c), b + d

    def both_ways(out, gain, axis, bit):
        nearby = order.swap(out, bit, axis), order.swap(gain, bit, axis)
        return order.fuse(join, out, gain, *nearby)

    ring_bits = [1 << i for i in range((ring - 1).bit_length())][::-1]
    out_low = out_low[None]
    for i, bit in enumerate(ring_bits):
        nearby = order.swap(out_low, bit, "frames"), order.swap(gain_sum, bit, "frames")
        if i == 1:
            block = order.run(
                block_rows, idx, forth.parts, branches[0], hidden, live_own, count
            )
        out_low, gain_sum = order.fuse(join, out_low, gain_sum, *nearby)
    moved = lax.all_to_all(order.tie(qkv_low), "frames", 0, 0, tiled=True)
    block = order.exchange(block)
    grad_in = order.run(input_grad, idx, xs, dhs, sums, gain1, 0, 1)
    block_out = order.run(gather_block, idx, block)
    out_low = unmix(out_low, "frames", ring_bits)[None]
    for i, bit in enumerate(bits[::-1]):
        nearby = order.swap(out_low, bit), order.swap(gain_sum, bit)
        if i == 0:
            weights(0)
        out_low, gain_sum = order.fuse(join, out_low, gain_sum, *nearby)
    qkv_grad = order.fuse(lambda m: jnp.sum(m.astype(f32), axis=0), moved).reshape(3, rows, part)
    out_grad = unmix(out_low, "pos", bits[::-1]).reshape(width, width).astype(f32)
    gain_attn_grad = gain_sum

    ffn_grad = None
    for term in totals.values():
        ffn_grad = term if ffn_grad is None else ffn_grad + term
    return (
        block_out,
        grad_in,
        gain_attn_grad.reshape(width),
        qkv_grad.transpose(1, 0, 2),
        out_grad,
        gain_ffn_grad.reshape(local, rows),
        ffn_grad.transpose(0, 2, 1, 3),
    )


def solution(mesh):
    placed = (
        P("frames", None, "pos"),
        P("frames"),
        P(),
        P(None, None, "pos"),
        P(),
        P("pos", None),
        P("frames", "pos", None, None),
        P("frames", None, "pos"),
    )
    return jax.shard_map(
        body,
        mesh=mesh,
        in_specs=placed,
        out_specs=(
            P("frames", None, "pos"),
            P("frames", None, "pos"),
            P(),
            P("frames", None, "pos"),
            P(),
            P("pos", "frames"),
            P("frames", "pos", None, None),
        ),
        check_vma=False,
    )
```
